32 devices in a mesh: rep: 4 (over y, x), shard: 8 (over z, core).
Axes of the slice: x: 2, y: 2, z: 4, core: 2. Of those that a mesh axis runs over, the one named last changes fastest.
Arguments:
- inputs: bfloat16 [4096, 1024], P(('rep', 'shard')), may hold values from -6 to 6
- cotangent: bfloat16 [4096, 1024], P(('rep', 'shard')), may hold values from -6 to 6
- mix_gain: bfloat16 [1024], P('shard'), may hold values from 0.5 to 1.5
- query_proj: bfloat16 [1024, 512], P('shard'), may hold values from -0.1875 to 0.1875
- key_proj: bfloat16 [1024, 512], P('shard'), may hold values from -0.1875 to 0.1875
- value_proj: bfloat16 [1024, 1024], P('shard'), may hold values from -0.1875 to 0.1875
- beta_proj: bfloat16 [1024, 4], P('shard'), may hold values from -0.1875 to 0.1875
- decay_proj: bfloat16 [1024, 4], P('shard'), may hold values from -0.1875 to 0.1875
- gate_proj: bfloat16 [1024, 1024], P('shard'), may hold values from -0.1875 to 0.1875
- query_conv: bfloat16 [4, 512], P(None, 'shard'), may hold values from -3 to 3
- key_conv: bfloat16 [4, 512], P(None, 'shard'), may hold values from -3 to 3
- value_conv: bfloat16 [4, 1024], P(None, 'shard'), may hold values from -3 to 3
- decay_log: float32 [4], replicated, may hold values from -1.5 to 0.5
- decay_bias: float32 [4], replicated, may hold values from -4 to -2
- head_gain: bfloat16 [256], P('shard'), may hold values from 0.5 to 1.5
- out_proj: bfloat16 [1024, 1024], P('shard'), may hold values from -0.1875 to 0.1875
- ffn_gain: bfloat16 [1024], P('shard'), may hold values from 0.5 to 1.5
- ffn_gate: bfloat16 [1024, 2816], P('shard'), may hold values from -0.1875 to 0.1875
- ffn_up: bfloat16 [1024, 2816], P('shard'), may hold values from -0.1875 to 0.1875
- ffn_down: bfloat16 [2816, 1024], P('shard'), may hold values from -0.109375 to 0.109375
Outputs:
- outputs: bfloat16 [4096, 1024], P(('rep', 'shard'))
- inputs_grad: float32 [4096, 1024], P(('rep', 'shard'))
- mix_gain_grad: float32 [1024], P('shard')
- query_proj_grad: float32 [1024, 512], P('shard')
- key_proj_grad: float32 [1024, 512], P('shard')
- value_proj_grad: float32 [1024, 1024], P('shard')
- beta_proj_grad: float32 [1024, 4], P('shard')
- decay_proj_grad: float32 [1024, 4], P('shard')
- gate_proj_grad: float32 [1024, 1024], P('shard')
- query_conv_grad: float32 [4, 512], P(None, 'shard')
- key_conv_grad: float32 [4, 512], P(None, 'shard')
- value_conv_grad: float32 [4, 1024], P(None, 'shard')
- decay_log_grad: float32 [4], replicated
- decay_bias_grad: float32 [4], replicated
- head_gain_grad: float32 [256], P('shard')
- out_proj_grad: float32 [1024, 1024], P('shard')
- ffn_gain_grad: float32 [1024], P('shard')
- ffn_gate_grad: float32 [1024, 2816], P('shard')
- ffn_up_grad: float32 [1024, 2816], P('shard')
- ffn_down_grad: float32 [2816, 1024], P('shard')
The draws below stay inside these ranges and needn't reach their ends.
All inputs are finite; a program needn't handle non-finite values.
Results may differ from the reference program's by a relative error of at most 0.018.
Values may be sent and summed in bfloat16 or wider, within the bound.
No kernel may reach another device: no remote copies, remote signals or barrier semaphores. Data moves between devices by JAX's collectives and lax.ppermute only.
A program may use at most 192 MiB of HBM per device.

```python
import math
import jax
import jax.numpy as jnp
from jax import lax

D = 1024
HEADS = 4
VHEAD = 256
FF = 2816
CONV = 4
SPAN = 64
TOK_DEV = 128
KEYS = 512
VALUES = 1024
TOKENS = 4096
N_REP = 4
N_SHARD = 8


def level_of(rng, dims, cuts, low, largest):
    def one(dim, shards_of):
        steps = jax.random.uniform(jax.random.fold_in(jax.random.fold_in(rng, 6), dim), (shards_of,), jnp.float32, low / len(cuts), largest / len(cuts))
        return jnp.repeat(jnp.exp(steps), dims[dim] // shards_of).reshape((-1,) + (1,) * (len(dims) - dim - 1))

    gain = one(*cuts[0])
    for cut in cuts[1:]:
        gain = gain * one(*cut)
    return gain


def noise(own_key, dims, deviation, bound, cuts=(), held_as=jnp.bfloat16):
    values = jax.random.normal(own_key, dims, jnp.float32) * deviation
    if len(cuts) > 0:
        values = level_of(own_key, dims, cuts, -0.22, 0.18) * values
    return jnp.clip(values, min=-bound, max=bound).astype(held_as)


def setup_inputs(seed: int = 0) -> dict:
    seeds = jax.random.split(jax.random.key(seed), 21)
    inputs = noise(seeds[0], (TOKENS, D), 1.0, 6.0, ((0, 32),))
    cotangent = noise(seeds[1], (TOKENS, D), 1.0, 6.0, ((0, 32),))
    mix_gain = jnp.clip(1.0 + 0.1 * jax.random.normal(seeds[2], (D,), jnp.float32), 0.5, 1.5).astype(jnp.bfloat16)
    query_proj = noise(seeds[3], (D, KEYS), D ** -0.5, 0.1875, ((0, 8),))
    key_proj = noise(seeds[4], (D, KEYS), D ** -0.5, 0.1875, ((0, 8),))
    value_proj = noise(seeds[5], (D, VALUES), D ** -0.5, 0.1875, ((0, 8),))
    beta_proj = noise(seeds[6], (D, HEADS), D ** -0.5, 0.1875, ((0, 8),))
    decay_proj = noise(seeds[7], (D, HEADS), D ** -0.5, 0.1875, ((0, 8),))
    gate_proj = noise(seeds[8], (D, VALUES), D ** -0.5, 0.1875, ((0, 8),))
    query_conv = noise(seeds[9], (CONV, KEYS), CONV ** -0.5, 3.0, ((1, 8),))
    key_conv = noise(seeds[10], (CONV, KEYS), CONV ** -0.5, 3.0, ((1, 8),))
    value_conv = noise(seeds[11], (CONV, VALUES), CONV ** -0.5, 3.0, ((1, 8),))
    decay_log = jnp.clip(jax.random.uniform(seeds[12], (HEADS,), jnp.float32, -1.5, 0.5), -1.5, 0.5)
    decay_bias = jnp.clip(jax.random.uniform(seeds[13], (HEADS,), jnp.float32, -4.0, -2.0), -4.0, -2.0)
    head_gain = jnp.clip(1.0 + 0.1 * jax.random.normal(seeds[14], (VHEAD,), jnp.float32), 0.5, 1.5).astype(jnp.bfloat16)
    out_proj = noise(seeds[15], (VALUES, D), VALUES ** -0.5, 0.1875, ((0, 8),))
    ffn_gain = jnp.clip(1.0 + 0.1 * jax.random.normal(seeds[16], (D,), jnp.float32), 0.5, 1.5).astype(jnp.bfloat16)
    ffn_gate = noise(seeds[17], (D, FF), D ** -0.5, 0.1875, ((0, 8),))
    ffn_up = noise(seeds[18], (D, FF), D ** -0.5, 0.1875, ((0, 8),))
    ffn_down = noise(seeds[19], (FF, D), FF ** -0.5, 0.109375, ((0, 8),))
    return dict(inputs=inputs, cotangent=cotangent, mix_gain=mix_gain, query_proj=query_proj, key_proj=key_proj, value_proj=value_proj, beta_proj=beta_proj, decay_proj=decay_proj, gate_proj=gate_proj, query_conv=query_conv, key_conv=key_conv, value_conv=value_conv, decay_log=decay_log, decay_bias=decay_bias, head_gain=head_gain, out_proj=out_proj, ffn_gain=ffn_gain, ffn_gate=ffn_gate, ffn_up=ffn_up, ffn_down=ffn_down)


EPS = 1e-06
HIGH = lax.Precision.HIGHEST

@jax.custom_vjp
def low(v):
    return lax.optimization_barrier(v.astype(jnp.bfloat16)).astype(jnp.float32)

@jax.custom_vjp
def low_back(v):
    return v

def low_keep(v):
    return (low(v), None)

def low_pass(kept, grad):
    return (grad,)

def back_keep(v):
    return (v, None)

def back_low(kept, grad):
    return (low(grad),)
low.defvjp(low_keep, low_pass)
low_back.defvjp(back_keep, back_low)

def wide_dot(left, right):
    return jnp.dot(left, right, precision=HIGH)

def rms_scale(values, scale_vec):
    return values * lax.rsqrt(lax.optimization_barrier(jnp.mean(values * values, -1, keepdims=True)) + EPS) * scale_vec

def shortconv(raw_input, kernel):
    taps_count = kernel.shape[0]
    length = raw_input.shape[1]
    padded = jnp.pad(raw_input, ((0, 0), (taps_count - 1, 0), (0, 0)))
    running = padded[:, 0:length, :] * kernel[0]
    for offset in range(1, taps_count):
        running = running + padded[:, offset:offset + length, :] * kernel[offset]
    return jax.nn.silu(running)

def split_blocks(values, block_size):
    batch_size, length, head_count = values.shape[:3]
    count_blocks = length // block_size
    shaped = values.reshape((batch_size, count_blocks, block_size, head_count) + values.shape[3:])
    if values.ndim == 4:
        return shaped.transpose(1, 0, 3, 2, 4)
    return shaped.transpose(1, 0, 3, 2)

def span_step(carry_state, pieces):
    query_part, key_part, value_part, beta_part, decay_part = pieces
    block_size = key_part.shape[-2]
    cumulative = jnp.cumsum(decay_part, -1)
    row_ids = lax.broadcasted_iota(jnp.int32, (block_size, block_size), 0)
    col_ids = lax.broadcasted_iota(jnp.int32, (block_size, block_size), 1)
    strict = row_ids > col_ids
    within = row_ids >= col_ids
    spread = cumulative[..., :, None] - cumulative[..., None, :]
    decay_below = jnp.where(strict, jnp.exp(jnp.where(strict, spread, 0.0)), 0.0)
    decay_upto = jnp.where(within, jnp.exp(jnp.where(within, spread, 0.0)), 0.0)
    keykey = jnp.einsum('bhik,bhjk->bhij', key_part, key_part, precision=HIGH)
    system = beta_part[..., :, None] * keykey * decay_below
    factor = jnp.exp(cumulative)[..., None]
    target = beta_part[..., None] * (value_part - factor * jnp.einsum('bhck,bhkv->bhcv', key_part, carry_state, precision=HIGH))
    update = lax.linalg.triangular_solve(system, target, left_side=True, lower=True, unit_diagonal=True)
    scores = jnp.einsum('bhik,bhjk->bhij', query_part, key_part, precision=HIGH) * decay_upto
    output = factor * jnp.einsum('bhck,bhkv->bhcv', query_part, carry_state, precision=HIGH) + jnp.einsum('bhij,bhjv->bhiv', scores, update, precision=HIGH)
    final_log = cumulative[..., -1:]
    carried = jnp.exp(final_log - cumulative)[..., None] * key_part
    carry_state = jnp.exp(final_log)[..., None] * carry_state + jnp.einsum('bhck,bhcv->bhkv', carried, update, precision=HIGH)
    return (carry_state, output)

def delta_rule(query_unit, key_unit, value_heads, beta_gate, log_decay):
    batch_size, length, head_count, key_size = key_unit.shape
    value_size = value_heads.shape[-1]
    pieces = (split_blocks(query_unit, SPAN), split_blocks(key_unit, SPAN), split_blocks(value_heads, SPAN), split_blocks(beta_gate, SPAN), split_blocks(log_decay, SPAN))
    initial = jnp.zeros((batch_size, head_count, key_size, value_size), jnp.float32)
    last_state, outputs = lax.scan(jax.checkpoint(span_step), initial, pieces)
    return outputs.transpose(1, 0, 3, 2, 4).reshape(batch_size, length, head_count, value_size)

def mixer(query_raw, key_raw, value_raw, beta_raw, decay_raw, gate_raw, query_kernel, key_kernel, value_kernel, decay_log, decay_bias, head_scale):
    batch_size, length, head_count = beta_raw.shape
    query_act = shortconv(query_raw, query_kernel).reshape(batch_size, length, head_count, -1)
    key_act = shortconv(key_raw, key_kernel).reshape(batch_size, length, head_count, -1)
    value_act = shortconv(value_raw, value_kernel).reshape(batch_size, length, head_count, -1)
    query_unit = query_act * lax.rsqrt(lax.optimization_barrier(jnp.sum(query_act * query_act, -1, keepdims=True)) + EPS) * (1.0 / math.sqrt(query_act.shape[-1]))
    key_unit = key_act * lax.rsqrt(lax.optimization_barrier(jnp.sum(key_act * key_act, -1, keepdims=True)) + EPS)
    beta_gate = jax.nn.sigmoid(beta_raw)
    log_decay = -jnp.exp(decay_log) * jax.nn.softplus(decay_raw + decay_bias)
    heads_out = delta_rule(query_unit, key_unit, value_act, beta_gate, log_decay)
    gate_heads = gate_raw.reshape(heads_out.shape)
    normed = heads_out * lax.rsqrt(lax.optimization_barrier(jnp.mean(heads_out * heads_out, -1, keepdims=True)) + EPS) * head_scale * jax.nn.silu(gate_heads)
    return normed.reshape(batch_size, length, -1)

def layer(seq_in, params):
    mix_gain, query_proj, key_proj, value_proj, beta_proj, decay_proj, gate_proj, query_conv, key_conv, value_conv, decay_log, decay_bias, head_gain, out_proj, ffn_gain, ffn_gate, ffn_up, ffn_down = params
    first = low(rms_scale(seq_in, mix_gain))
    query_raw = low_back(wide_dot(first, query_proj))
    key_raw = low_back(wide_dot(first, key_proj))
    value_raw = low_back(wide_dot(first, value_proj))
    gate_raw = low_back(wide_dot(first, gate_proj))
    beta_raw = wide_dot(first, beta_proj)
    decay_raw = wide_dot(first, decay_proj)
    mixed = low(mixer(query_raw, key_raw, value_raw, beta_raw, decay_raw, gate_raw, query_conv, key_conv, value_conv, decay_log, decay_bias, head_gain))
    hidden = seq_in + low_back(wide_dot(mixed, out_proj))
    second = low(rms_scale(hidden, ffn_gain))
    gate_val = low_back(wide_dot(second, ffn_gate))
    up_val = low_back(wide_dot(second, ffn_up))
    active = low(jax.nn.silu(gate_val) * up_val)
    return hidden + low_back(wide_dot(active, ffn_down))

def reference(inputs, cotangent, mix_gain, query_proj, key_proj, value_proj, beta_proj, decay_proj, gate_proj, query_conv, key_conv, value_conv, decay_log, decay_bias, head_gain, out_proj, ffn_gain, ffn_gate, ffn_up, ffn_down):
    params = tuple((item.astype(jnp.float32) for item in (mix_gain, query_proj, key_proj, value_proj, beta_proj, decay_proj, gate_proj, query_conv, key_conv, value_conv, decay_log, decay_bias, head_gain, out_proj, ffn_gain, ffn_gate, ffn_up, ffn_down)))
    seq_count = N_REP * N_SHARD
    per_group = math.gcd(seq_count, max(1, 4096 // TOK_DEV))
    blocks_in = inputs.astype(jnp.float32).reshape(seq_count // per_group, per_group, TOK_DEV, D)
    blocks_cot = cotangent.astype(jnp.float32).reshape(seq_count // per_group, per_group, TOK_DEV, D)

    def group_step(totals, pieces):
        block_in, block_cot = pieces
        result, pullback = jax.vjp(layer, block_in, params)
        block_grad, param_grads = pullback(block_cot)
        totals = jax.tree.map(jnp.add, totals, param_grads)
        return (totals, (result.astype(jnp.bfloat16), block_grad))
    initial = tuple((jnp.zeros_like(item) for item in params))
    totals, (results, grads_in) = lax.scan(group_step, initial, (blocks_in, blocks_cot))
    return (results.reshape(TOKENS, D), grads_in.reshape(TOKENS, D), totals[0], totals[1], totals[2], totals[3], totals[4], totals[5], totals[6], totals[7], totals[8], totals[9], totals[10], totals[11], totals[12], totals[13], totals[14], totals[15], totals[16], totals[17])
```

```python
import functools
import math

import jax
import jax.numpy as jnp
from jax import lax
from jax.experimental import pallas as pl
from jax.experimental.pallas import tpu as pltpu
from jax.sharding import PartitionSpec as P

EPS = 1e-06
HIGH = lax.Precision.HIGHEST
LOW = jnp.bfloat16
WIDE = jnp.float32
LANES = 128
ROWS16 = 16


def local_dot(left, right):
    return jnp.dot(left, right, preferred_element_type=WIDE)


def left_dot(left, right):
    return lax.dot_general(left, right, (((0,), (0,)), ((), ())), preferred_element_type=WIDE)


def right_dot(left, right):
    return lax.dot_general(left, right, (((1,), (1,)), ((), ())), preferred_element_type=WIDE)


def dot_nn(left, right):
    return jnp.dot(left, right, preferred_element_type=WIDE, precision=HIGH)


def dot_nt(left, right):
    return lax.dot_general(
        left, right, (((1,), (1,)), ((), ())), preferred_element_type=WIDE, precision=HIGH
    )


def dot_tn(left, right):
    return lax.dot_general(
        left, right, (((0,), (0,)), ((), ())), preferred_element_type=WIDE, precision=HIGH
    )


def sigmoid(v):
    return 1.0 / (1.0 + jnp.exp(-v))


def iotas(size):
    return (
        lax.broadcasted_iota(jnp.int32, (size, size), 0),
        lax.broadcasted_iota(jnp.int32, (size, size), 1),
    )


def later(v, steps):
    rows = lax.broadcasted_iota(jnp.int32, v.shape, 0)
    return jnp.where(rows >= steps, pltpu.roll(v, steps, 0), 0.0)


def earlier(v, steps):
    rows = lax.broadcasted_iota(jnp.int32, v.shape, 0)
    return jnp.where(rows < v.shape[0] - steps, pltpu.roll(v, v.shape[0] - steps, 0), 0.0)


def conv_silu(raw, taps):
    count = taps.shape[0]
    run = raw * taps[count - 1 : count]
    for steps in range(1, count):
        run = run + later(raw, steps) * taps[count - 1 - steps : count - steps]
    sig = sigmoid(run)
    return run, sig


def unit_features(act, keys):
    query_act, key_act, value = act[:, :keys], act[:, keys : 2 * keys], act[:, 2 * keys :]
    query_r = lax.rsqrt(jnp.sum(query_act * query_act, -1, keepdims=True) + EPS)
    key_r = lax.rsqrt(jnp.sum(key_act * key_act, -1, keepdims=True) + EPS)
    query = query_act * query_r * (1.0 / math.sqrt(keys))
    return query, key_act * key_r, value, query_act, query_r, key_act, key_r


def softplus(v):
    return jnp.maximum(v, 0.0) + jnp.log1p(jnp.exp(-jnp.abs(v)))


def decay_matrix(gates, decay, bias):
    size = gates.shape[0]
    rows, cols = iotas(size)
    beta = sigmoid(gates[:, 0:1])
    decay_in = gates[:, 1:2] + bias
    log_decay = -decay * softplus(decay_in)
    decay_row = jnp.sum(jnp.where(rows == cols, log_decay, 0.0), 0, keepdims=True)
    total_col = jnp.sum(jnp.where(cols <= rows, decay_row, 0.0), 1, keepdims=True)
    total_row = jnp.sum(jnp.where(rows <= cols, log_decay, 0.0), 0, keepdims=True)
    spread = jnp.where(rows >= cols, total_col - total_row, 0.0)
    upto = jnp.where(rows >= cols, jnp.exp(spread), 0.0)
    return beta, decay_in, log_decay, upto


def unit_lower_inverse(systems):
    size = systems[0].shape[0]
    rows, cols = iotas(size)
    block = 8
    near = [jnp.where(rows // block == cols // block, a, 0.0) for a in systems]
    eye = jnp.where(rows == cols, 1.0, 0.0)
    power = [dot_nn(a, a) for a in near]
    inverse = [eye - a for a in near]
    inverse = [x + dot_nn(x, p) for x, p in zip(inverse, power)]
    power = [dot_nn(p, p) for p in power]
    inverse = [x + dot_nn(x, p) for x, p in zip(inverse, power)]
    while block < size:
        cross = (rows // (2 * block) == cols // (2 * block)) & (rows // block != cols // block)
        middle = [dot_nn(jnp.where(cross, a, 0.0), x) for a, x in zip(systems, inverse)]
        inverse = [x - dot_nn(x, m) for x, m in zip(inverse, middle)]
        block *= 2
    return inverse


def mixer_forward_kernel(
    seqs,
    keys,
    scalars,
    tokens,
    gain,
    weights,
    gate_weights,
    taps,
    head_gain,
    first_out,
    raw_out,
    gates_out,
    inverse_out,
    update_out,
    heads_out,
    mixed_out,
):
    size = tokens.shape[0] // seqs
    conv_width = taps.shape[1]
    wide = tokens[...].astype(WIDE)
    first = (
        wide * lax.rsqrt(jnp.mean(wide * wide, -1, keepdims=True) + EPS) * gain[...]
    ).astype(LOW)
    first_out[...] = first
    raw_out[...] = local_dot(first, weights[...])
    gates_out[...] = local_dot(first, gate_weights[...])
    rows, cols = iotas(size)
    parts = []
    for seq in range(seqs):
        span = slice(seq * size, (seq + 1) * size)
        run, sig = conv_silu(raw_out[span, :conv_width], taps[...])
        query, key, value = unit_features(run * sig, keys)[:3]
        beta, _, _, upto = decay_matrix(gates_out[span], scalars[0], scalars[1])
        system = jnp.where(rows > cols, beta * dot_nt(key, key) * upto, 0.0)
        scores = dot_nt(query, key) * upto
        parts.append((system, scores, beta * value))
    inverses = unit_lower_inverse([p[0] for p in parts])
    for seq in range(seqs):
        span = slice(seq * size, (seq + 1) * size)
        inverse_out[span] = inverses[seq]
        update = dot_nn(inverses[seq], parts[seq][2])
        heads = dot_nn(parts[seq][1], update)
        update_out[span] = update
        heads_out[span] = heads
        gate = raw_out[span, conv_width:]
        normed = heads * lax.rsqrt(jnp.mean(heads * heads, -1, keepdims=True) + EPS)
        mixed_out[span] = (normed * head_gain[...] * (gate * sigmoid(gate))).astype(LOW)


def mixer_backward_kernel(
    seqs,
    keys,
    scalars,
    branch_grad,
    out_rows,
    raw,
    gates,
    inverse,
    update,
    heads,
    taps,
    head_gain,
    weights,
    gate_weights,
    tokens,
    raw_grad_out,
    gates_grad_out,
    first_grad_out,
    gain_grad_out,
    taps_grad_out,
    head_gain_grad_out,
    decay_grad_out,
):
    size = raw.shape[0] // seqs
    conv_width = taps.shape[1]
    count = taps.shape[0]
    rows, cols = iotas(size)
    taps_grad = [jnp.zeros((1, conv_width), WIDE) for _ in range(count)]
    head_gain_grad = jnp.zeros(head_gain.shape, WIDE)
    log_total = jnp.zeros((1, 1), WIDE)
    bias_total = jnp.zeros((1, 1), WIDE)
    mixed_grad_all = right_dot(branch_grad[...], out_rows[...])
    gain_row = head_gain[...]
    for seq in range(seqs):
        span = slice(seq * size, (seq + 1) * size)
        mixed_grad = mixed_grad_all[span]
        out = heads[span]
        gate = raw[span, conv_width:]
        scale = lax.rsqrt(jnp.mean(out * out, -1, keepdims=True) + EPS)
        normed = out * scale
        gate_sig = sigmoid(gate)
        gate_act = gate * gate_sig
        gate_grad = (
            mixed_grad * normed * gain_row * gate_sig * (1.0 + gate * (1.0 - gate_sig))
        )
        raw_grad_out[span, conv_width:] = gate_grad.astype(LOW)
        head_gain_grad = head_gain_grad + jnp.sum(
            mixed_grad * normed * gate_act, 0, keepdims=True
        )
        normed_grad = mixed_grad * gain_row * gate_act
        out_grad = scale * (
            normed_grad - normed * jnp.mean(normed_grad * normed, -1, keepdims=True)
        )
        raw_in = raw[span, :conv_width]
        run, sig = conv_silu(raw_in, taps[...])
        query, key, value, query_act, query_r, key_act, key_r = unit_features(run * sig, keys)
        beta, decay_in, log_decay, upto = decay_matrix(gates[span], scalars[0], scalars[1])
        key_key = dot_nt(key, key) * upto
        scores = dot_nt(query, key) * upto
        solved = update[span]
        scores_grad = jnp.where(rows >= cols, dot_nt(out_grad, solved), 0.0)
        solved_grad = dot_tn(scores, out_grad)
        target_grad = dot_tn(inverse[span], solved_grad)
        system_grad = jnp.where(rows > cols, -dot_nt(target_grad, solved), 0.0)
        value_grad = beta * target_grad
        system_part = system_grad * key_key
        beta_grad = jnp.sum(target_grad * value, 1, keepdims=True) + jnp.sum(
            system_part, 1, keepdims=True
        )
        key_key_grad = system_grad * (beta * upto)
        scores_part = scores_grad * upto
        spread_grad = system_part * beta + scores_grad * scores
        query_grad = dot_nn(scores_part, key)
        key_grad = (
            dot_tn(scores_part, query) + dot_nn(key_key_grad, key) + dot_tn(key_key_grad, key)
        )
        total_row = jnp.sum(
            jnp.where(rows == cols, jnp.sum(spread_grad, 1, keepdims=True), 0.0),
            0,
            keepdims=True,
        ) - jnp.sum(spread_grad, 0, keepdims=True)
        decay_grad = jnp.sum(jnp.where(cols >= rows, total_row, 0.0), 1, keepdims=True)
        decay_raw_grad = -scalars[0] * decay_grad * sigmoid(decay_in)
        beta_raw_grad = beta_grad * beta * (1.0 - beta)
        log_total = log_total + jnp.sum(decay_grad * log_decay, 0, keepdims=True)
        bias_total = bias_total + jnp.sum(decay_raw_grad, 0, keepdims=True)
        beta_high = beta_raw_grad.astype(LOW).astype(WIDE)
        decay_high = decay_raw_grad.astype(LOW).astype(WIDE)
        lane = lax.broadcasted_iota(jnp.int32, (size, LANES), 1)
        gates_grad_out[span] = jnp.where(
            lane == 0,
            beta_high,
            jnp.where(
                lane == 1,
                decay_high,
                jnp.where(
                    lane == 2,
                    beta_raw_grad - beta_high,
                    jnp.where(lane == 3, decay_raw_grad - decay_high, 0.0),
                ),
            ),
        ).astype(LOW)
        query_grad = query_grad * (1.0 / math.sqrt(keys))
        query_unit = query_act * query_r
        query_act_grad = query_r * (
            query_grad - query_unit * jnp.sum(query_unit * query_grad, -1, keepdims=True)
        )
        key_act_grad = key_r * (key_grad - key * jnp.sum(key * key_grad, -1, keepdims=True))
        act_grad = jnp.concatenate([query_act_grad, key_act_grad, value_grad], 1)
        run_grad = act_grad * sig * (1.0 + run * (1.0 - sig))
        raw_grad = run_grad * taps[count - 1 : count]
        taps_grad[count - 1] = taps_grad[count - 1] + jnp.sum(
            run_grad * raw_in, 0, keepdims=True
        )
        for steps in range(1, count):
            tap = count - 1 - steps
            moved = earlier(run_grad, steps)
            raw_grad = raw_grad + moved * taps[tap : tap + 1]
            taps_grad[tap] = taps_grad[tap] + jnp.sum(moved * raw_in, 0, keepdims=True)
        raw_grad_out[span, :conv_width] = raw_grad.astype(LOW)
    taps_grad_out[...] = jnp.concatenate(taps_grad, 0)
    head_gain_grad_out[...] = head_gain_grad
    lane = lax.broadcasted_iota(jnp.int32, (1, LANES), 1)
    decay_grad_out[...] = jnp.where(
        lane == 0, log_total, jnp.where(lane == 1, bias_total, 0.0)
    )
    first_grad = right_dot(raw_grad_out[...], weights[...]) + right_dot(
        gates_grad_out[...], gate_weights[...]
    )
    first_grad_out[...] = first_grad.astype(LOW)
    wide = tokens[...].astype(WIDE)
    scale = lax.rsqrt(jnp.mean(wide * wide, -1, keepdims=True) + EPS)
    gain_grad_out[...] = jnp.sum(first_grad * (wide * scale), 0, keepdims=True)


def vmem(shape, dtype):
    return jax.ShapeDtypeStruct(shape, dtype)


def mixer_forward(seqs, keys, scalars, tokens, gain, weights, gate_weights, taps, head_gain):
    count, width = tokens.shape
    values = head_gain.shape[1]
    features = weights.shape[1]
    size = count // seqs
    spec = pl.BlockSpec(memory_space=pltpu.VMEM)
    return pl.pallas_call(
        functools.partial(mixer_forward_kernel, seqs, keys),
        out_shape=(
            vmem((count, width), LOW),
            vmem((count, features), WIDE),
            vmem((count, LANES), WIDE),
            vmem((count, size), WIDE),
            vmem((count, values), WIDE),
            vmem((count, values), WIDE),
            vmem((count, values), LOW),
        ),
        in_specs=[pl.BlockSpec(memory_space=pltpu.SMEM)] + [spec] * 6,
        out_specs=[spec] * 7,
        compiler_params=pltpu.CompilerParams(vmem_limit_bytes=48 * 1024 * 1024),
        name="mixer_forward",
    )(scalars, tokens, gain, weights, gate_weights, taps, head_gain)


def mixer_backward(
    seqs,
    keys,
    scalars,
    branch_grad,
    out_rows,
    raw,
    gates,
    inverse,
    update,
    heads,
    taps,
    head_gain,
    weights,
    gate_weights,
    tokens,
):
    count, width = tokens.shape
    spec = pl.BlockSpec(memory_space=pltpu.VMEM)
    return pl.pallas_call(
        functools.partial(mixer_backward_kernel, seqs, keys),
        out_shape=(
            vmem(raw.shape, LOW),
            vmem((count, LANES), LOW),
            vmem((count, width), LOW),
            vmem((1, width), WIDE),
            vmem(taps.shape, WIDE),
            vmem(head_gain.shape, WIDE),
            vmem((1, LANES), WIDE),
        ),
        in_specs=[pl.BlockSpec(memory_space=pltpu.SMEM)] + [spec] * 12,
        out_specs=[spec] * 7,
        compiler_params=pltpu.CompilerParams(vmem_limit_bytes=48 * 1024 * 1024),
        name="mixer_backward",
    )(
        scalars,
        branch_grad,
        out_rows,
        raw,
        gates,
        inverse,
        update,
        heads,
        taps,
        head_gain,
        weights,
        gate_weights,
        tokens,
    )


def team_ring(devices, team, steps):
    return [(j, j // team * team + (j % team + steps) % team) for j in range(devices)]


def team_gather(block, devices, team):
    return [block] + [
        lax.ppermute(block, "rep", team_ring(devices, team, steps)) for steps in range(1, team)
    ]


def team_scatter(slots, devices, team):
    total = slots[0]
    for steps in range(1, team):
        moved = lax.ppermute(slots[steps].astype(LOW), "rep", team_ring(devices, team, -steps))
        total = total + moved.astype(WIDE)
    return total


def quarter(matrix, axis, shards, team, part):
    each = matrix.shape[axis] // (shards * team)
    return jnp.concatenate(
        [
            lax.dynamic_slice_in_dim(matrix, (s * team + part) * each, each, axis)
            for s in range(shards)
        ],
        axis,
    )


def norm_scale(v):
    return lax.rsqrt(jnp.mean(v * v, -1, keepdims=True) + EPS)


def split_three(v):
    high = lax.reduce_precision(v, 8, 7)
    middle = lax.reduce_precision(v - high, 8, 7)
    return high, middle, v - high - middle


def gather_sum(block, devices, team):
    blocks = lax.all_gather(block, "rep").astype(WIDE)
    return jnp.sum(blocks.reshape((devices // team, team) + block.shape), 0)


def body(
    inputs,
    cotangent,
    mix_gain,
    query_proj,
    key_proj,
    value_proj,
    beta_proj,
    decay_proj,
    gate_proj,
    query_conv,
    key_conv,
    value_conv,
    decay_log,
    decay_bias,
    head_gain,
    out_proj,
    ffn_gain,
    ffn_gate,
    ffn_up,
    ffn_down,
):
    devices = lax.axis_size("rep")
    shards = lax.axis_size("shard")
    team = beta_proj.shape[1]
    part = lax.axis_index("rep") % team
    shard = lax.axis_index("shard")
    tokens_each, width = inputs.shape
    chunk = mix_gain.shape[0]
    keys = query_proj.shape[1] // team
    values = value_proj.shape[1] // team
    outs = out_proj.shape[1] // team
    hidden_each = ffn_down.shape[0] // team
    hidden_part = hidden_each * shards
    taps_count = query_conv.shape[0]
    key_each, value_each = query_conv.shape[1], value_conv.shape[1]
    conv_each = 2 * key_each + value_each
    conv_size = taps_count * conv_each
    head_shards = shards // team
    head_each = head_gain.shape[0]

    def column_part(matrix, size):
        return lax.dynamic_slice_in_dim(matrix, part * size, size, 1)

    mixer_pack = jnp.concatenate(
        [
            column_part(query_proj, keys),
            column_part(key_proj, keys),
            column_part(value_proj, values),
            column_part(gate_proj, values),
            column_part(out_proj, outs),
        ],
        1,
    )
    mixer_weights = lax.all_gather(mixer_pack, "shard", axis=0, tiled=True)
    both = jnp.concatenate([inputs, cotangent], 0)
    both_slots = team_gather(both, devices, team)
    tokens = jnp.concatenate([b[:tokens_each] for b in both_slots], 0)
    cotangents = jnp.concatenate([b[tokens_each:] for b in both_slots], 0)
    small = jnp.concatenate(
        [
            mix_gain,
            ffn_gain,
            jnp.concatenate([query_conv, key_conv, value_conv], 1).reshape(-1),
            jnp.concatenate([beta_proj, decay_proj], 1).T.reshape(-1),
            head_gain,
        ]
    )
    small = jnp.pad(small, (0, -small.shape[0] % LANES))
    small = lax.all_gather(small, "shard", axis=0)
    up_pack = jnp.concatenate(
        [quarter(ffn_gate, 1, shards, team, part), quarter(ffn_up, 1, shards, team, part)], 1
    )
    up_weights = lax.all_gather(up_pack, "shard", axis=0, tiled=True)
    down_weights = lax.all_gather(
        lax.dynamic_slice_in_dim(ffn_down, part * hidden_each, hidden_each, 0),
        "shard",
        axis=0,
        tiled=True,
    )
    mix_row = small[:, :chunk].reshape(1, width).astype(WIDE)
    ffn_row = small[:, chunk : 2 * chunk].reshape(1, width).astype(WIDE)
    place = 2 * chunk
    conv_all = small[:, place : place + conv_size].reshape(shards, taps_count, conv_each)
    conv_head = lax.dynamic_slice_in_dim(conv_all, part * head_shards, head_shards, 0)
    conv_head = conv_head.transpose(1, 0, 2).astype(WIDE)
    taps = jnp.concatenate(
        [
            conv_head[:, :, :key_each].reshape(taps_count, keys),
            conv_head[:, :, key_each : 2 * key_each].reshape(taps_count, keys),
            conv_head[:, :, 2 * key_each :].reshape(taps_count, values),
        ],
        1,
    )
    place += conv_size
    gate_all = small[:, place : place + 2 * team * chunk].reshape(shards, 2, team, chunk)
    gate_part = lax.dynamic_index_in_dim(gate_all, part, 2, keepdims=False)
    gate_cols = gate_part.transpose(0, 2, 1).reshape(width, 2)
    gate_weights = jnp.pad(
        jnp.concatenate([gate_cols, gate_cols], 1), ((0, 0), (0, LANES - 4))
    )
    place += 2 * team * chunk
    head_row = small[:, place : place + head_each].reshape(1, values).astype(WIDE)
    scalars = jnp.stack(
        [
            jnp.exp(lax.dynamic_index_in_dim(decay_log, part, 0, keepdims=False)),
            lax.dynamic_index_in_dim(decay_bias, part, 0, keepdims=False),
        ]
    )

    head_weights = mixer_weights[:, : 2 * keys + 2 * values]
    first, raw, gates, inverse, update, heads, mixed_part = mixer_forward(
        team, keys, scalars, tokens, mix_row, head_weights, gate_weights, taps, head_row
    )
    out_slots = jnp.stack(
        team_gather(mixer_weights[:, 2 * keys + 2 * values :], devices, team)
    )
    out_full = jnp.concatenate(
        [
            lax.dynamic_index_in_dim(out_slots, (part - h) % team, 0, keepdims=False)
            for h in range(team)
        ],
        1,
    )
    mixed_slots = team_gather(mixed_part, devices, team)
    mixed_slots = jnp.stack(
        [
            jnp.roll(block.reshape(team, tokens_each, values), e, 0).reshape(-1, values)
            for e, block in enumerate(mixed_slots)
        ]
    )
    mixed = jnp.concatenate(
        [
            lax.dynamic_index_in_dim(mixed_slots, (part - h) % team, 0, keepdims=False)
            for h in range(team)
        ],
        1,
    )

    hidden = tokens.astype(WIDE) + local_dot(mixed, out_full)
    hidden_scale = norm_scale(hidden)
    second = (hidden * hidden_scale * ffn_row).astype(LOW)
    gate_up = local_dot(second, up_weights)
    gate_val, up_val = gate_up[:, :hidden_part], gate_up[:, hidden_part:]
    gate_sig = jax.nn.sigmoid(gate_val)
    active = (gate_val * gate_sig * up_val).astype(LOW)
    active_grad = right_dot(cotangents, down_weights)
    gate_back = active_grad * up_val * gate_sig * (1.0 + gate_val * (1.0 - gate_sig))
    up_back = active_grad * gate_val * gate_sig
    both_back = jnp.concatenate([gate_back.astype(LOW), up_back.astype(LOW)], 1)
    second_part = right_dot(both_back, up_weights)
    ffn_gain_part = jnp.sum(second_part * (hidden * hidden_scale), 0)

    def slots_of(v):
        return [v[e * tokens_each : (e + 1) * tokens_each] for e in range(team)]

    second_grad = team_scatter(slots_of(second_part), devices, team)
    hidden_own, scale_own = hidden[:tokens_each], hidden_scale[:tokens_each]
    weighted = second_grad * ffn_row
    hidden_grad = cotangent.astype(WIDE) + scale_own * (
        weighted
        - hidden_own
        * (scale_own * scale_own * jnp.mean(hidden_own * weighted, -1, keepdims=True))
    )
    branch_slots = team_gather(hidden_grad.astype(LOW), devices, team)
    branch_grad = jnp.concatenate(branch_slots, 0)
    result = hidden_own + team_scatter(
        slots_of(local_dot(active, down_weights)), devices, team
    )
    up_wgrad = left_dot(second, both_back).astype(LOW)
    down_wgrad = left_dot(active, cotangents).astype(LOW)
    up_shard = lax.psum_scatter(up_wgrad, "shard", scatter_dimension=0, tiled=True)
    down_shard = lax.psum_scatter(down_wgrad, "shard", scatter_dimension=0, tiled=True)

    out_rows = lax.dynamic_slice_in_dim(out_full, part * values, values, 0)
    (
        raw_grad,
        gates_grad,
        first_part,
        mix_gain_part,
        taps_grad,
        head_gain_part,
        decay_part,
    ) = mixer_backward(
        team,
        keys,
        scalars,
        branch_grad,
        out_rows,
        raw,
        gates,
        inverse,
        update,
        heads,
        taps,
        head_row,
        head_weights,
        gate_weights,
        tokens,
    )
    first_grad = team_scatter(slots_of(first_part), devices, team)
    seq_in = inputs.astype(WIDE)
    seq_scale = norm_scale(seq_in)
    weighted = first_grad * mix_row
    inputs_grad = hidden_grad + seq_scale * (
        weighted
        - seq_in * (seq_scale * seq_scale * jnp.mean(seq_in * weighted, -1, keepdims=True))
    )

    out_wgrad = left_dot(mixed, lax.dynamic_slice_in_dim(branch_grad, part * outs, outs, 1))
    head_wgrad = left_dot(first, raw_grad)
    gates_wgrad = left_dot(first, gates_grad)
    gates_wgrad = gates_wgrad[:, :2] + gates_wgrad[:, 2:4]
    conv_grad = jnp.concatenate(
        [
            taps_grad[:, :keys].reshape(taps_count, head_shards, key_each),
            taps_grad[:, keys : 2 * keys].reshape(taps_count, head_shards, key_each),
            taps_grad[:, 2 * keys :].reshape(taps_count, head_shards, value_each),
        ],
        2,
    ).transpose(1, 0, 2)
    conv_grad = lax.dynamic_update_slice_in_dim(
        jnp.zeros((shards, taps_count, conv_each), WIDE), conv_grad, part * head_shards, 0
    )
    decay_terms = jnp.stack(split_three(decay_part[0, :2]))[:, :, None]
    decay_terms = jnp.where(
        lax.broadcasted_iota(jnp.int32, (1, 1, shards), 2) == shard, decay_terms, 0.0
    ).reshape(1, -1)
    small_grad = jnp.concatenate(
        [
            gates_wgrad[:, 0].reshape(shards, chunk),
            gates_wgrad[:, 1].reshape(shards, chunk),
            mix_gain_part.reshape(shards, chunk),
            ffn_gain_part.reshape(shards, chunk),
            conv_grad.reshape(shards, conv_size),
            head_gain_part.reshape(shards, head_each),
            jnp.broadcast_to(decay_terms, (shards, decay_terms.shape[1])),
        ],
        1,
    )
    pack_width = 2 * keys + 2 * values + outs
    small_rows = -(-small_grad.shape[1] // (pack_width * ROWS16)) * ROWS16
    small_grad = jnp.pad(
        small_grad, ((0, 0), (0, small_rows * pack_width - small_grad.shape[1]))
    ).reshape(shards, small_rows, pack_width)
    grad_pack = jnp.concatenate(
        [
            jnp.concatenate([head_wgrad, out_wgrad], 1)
            .astype(LOW)
            .reshape(shards, chunk, pack_width),
            small_grad.astype(LOW),
        ],
        1,
    ).reshape(-1, pack_width)
    mixer_shard = lax.psum_scatter(grad_pack, "shard", scatter_dimension=0, tiled=True)

    up_total = gather_sum(up_shard, devices, team)
    down_total = gather_sum(down_shard, devices, team)
    mixer_total = gather_sum(mixer_shard, devices, team)

    def merge(block):
        return block.transpose(1, 0, 2).reshape(block.shape[1], -1)

    def merge_hidden(block):
        return (
            block.reshape(team, chunk, shards, hidden_each)
            .transpose(1, 2, 0, 3)
            .reshape(chunk, -1)
        )

    rows_total = mixer_total[:, :chunk]
    small_total = mixer_total[:, chunk:].reshape(team, -1)
    place = 2 * chunk
    mix_total = jnp.sum(small_total[:, place : place + chunk], 0)
    place += chunk
    ffn_total = jnp.sum(small_total[:, place : place + chunk], 0)
    place += chunk
    conv_total = jnp.sum(small_total[:, place : place + conv_size], 0)
    conv_total = conv_total.reshape(taps_count, conv_each)
    place += conv_size
    head_total = jnp.sum(small_total[:, place : place + head_each], 0)
    place += head_each
    decay_total = small_total[:, place : place + 6 * shards].reshape(team, 3, 2, shards)
    decay_total = jnp.sum(decay_total, (1, 3))
    return (
        result.astype(LOW),
        inputs_grad,
        mix_total,
        merge(rows_total[:, :, :keys]),
        merge(rows_total[:, :, keys : 2 * keys]),
        merge(rows_total[:, :, 2 * keys : 2 * keys + values]),
        small_total[:, :chunk].T,
        small_total[:, chunk : 2 * chunk].T,
        merge(rows_total[:, :, 2 * keys + values : 2 * keys + 2 * values]),
        conv_total[:, :key_each],
        conv_total[:, key_each : 2 * key_each],
        conv_total[:, 2 * key_each :],
        decay_total[:, 0],
        decay_total[:, 1],
        head_total,
        merge(rows_total[:, :, 2 * keys + 2 * values :]),
        ffn_total,
        merge_hidden(up_total[:, :, :hidden_part]),
        merge_hidden(up_total[:, :, hidden_part:]),
        down_total.reshape(-1, width),
    )


def solution(mesh):
    rows = P("shard", None)
    return jax.shard_map(
        body,
        mesh=mesh,
        in_specs=(
            P(("rep", "shard"), None),
            P(("rep", "shard"), None),
            P("shard"),
            rows,
            rows,
            rows,
            rows,
            rows,
            rows,
            P(None, "shard"),
            P(None, "shard"),
            P(None, "shard"),
            P(),
            P(),
            P("shard"),
            rows,
            P("shard"),
            rows,
            rows,
            rows,
        ),
        out_specs=(
            P(("rep", "shard"), None),
            P(("rep", "shard"), None),
            P("shard"),
            rows,
            rows,
            rows,
            rows,
            rows,
            rows,
            P(None, "shard"),
            P(None, "shard"),
            P(None, "shard"),
            P(),
            P(),
            P("shard"),
            rows,
            P("shard"),
            rows,
            rows,
            rows,
        ),
        check_vma=False,
    )
```

```python
import functools
import math

import jax
import jax.numpy as jnp
from jax import lax
from jax.experimental import pallas as pl
from jax.experimental.pallas import tpu as pltpu
from jax.sharding import PartitionSpec as P

EPS = 1e-06
HIGH = lax.Precision.HIGHEST
LOW = jnp.bfloat16
WIDE = jnp.float32
LANES = 128
ROWS16 = 16


def local_dot(left, right):
    return jnp.dot(left, right, preferred_element_type=WIDE)


def left_dot(left, right):
    return lax.dot_general(left, right, (((0,), (0,)), ((), ())), preferred_element_type=WIDE)


def right_dot(left, right):
    return lax.dot_general(left, right, (((1,), (1,)), ((), ())), preferred_element_type=WIDE)


def dot_nn(left, right):
    return jnp.dot(left, right, preferred_element_type=WIDE, precision=HIGH)


def dot_nt(left, right):
    return lax.dot_general(
        left, right, (((1,), (1,)), ((), ())), preferred_element_type=WIDE, precision=HIGH
    )


def dot_tn(left, right):
    return lax.dot_general(
        left, right, (((0,), (0,)), ((), ())), preferred_element_type=WIDE, precision=HIGH
    )


def sigmoid(v):
    return 1.0 / (1.0 + jnp.exp(-v))


def iotas(size):
    return (
        lax.broadcasted_iota(jnp.int32, (size, size), 0),
        lax.broadcasted_iota(jnp.int32, (size, size), 1),
    )


def later(v, steps):
    rows = lax.broadcasted_iota(jnp.int32, v.shape, 0)
    return jnp.where(rows >= steps, pltpu.roll(v, steps, 0), 0.0)


def earlier(v, steps):
    rows = lax.broadcasted_iota(jnp.int32, v.shape, 0)
    return jnp.where(rows < v.shape[0] - steps, pltpu.roll(v, v.shape[0] - steps, 0), 0.0)


def conv_silu(raw, taps):
    count = taps.shape[0]
    run = raw * taps[count - 1 : count]
    for steps in range(1, count):
        run = run + later(raw, steps) * taps[count - 1 - steps : count - steps]
    sig = sigmoid(run)
    return run, sig


def unit_features(act, keys):
    query_act, key_act, value = act[:, :keys], act[:, keys : 2 * keys], act[:, 2 * keys :]
    query_r = lax.rsqrt(jnp.sum(query_act * query_act, -1, keepdims=True) + EPS)
    key_r = lax.rsqrt(jnp.sum(key_act * key_act, -1, keepdims=True) + EPS)
    query = query_act * query_r * (1.0 / math.sqrt(keys))
    return query, key_act * key_r, value, query_act, query_r, key_act, key_r


def softplus(v):
    return jnp.maximum(v, 0.0) + jnp.log1p(jnp.exp(-jnp.abs(v)))


def decay_matrix(gates, decay, bias):
    size = gates.shape[0]
    rows, cols = iotas(size)
    beta = sigmoid(gates[:, 0:1])
    decay_in = gates[:, 1:2] + bias
    log_decay = -decay * softplus(decay_in)
    decay_row = jnp.sum(jnp.where(rows == cols, log_decay, 0.0), 0, keepdims=True)
    total_col = jnp.sum(jnp.where(cols <= rows, decay_row, 0.0), 1, keepdims=True)
    total_row = jnp.sum(jnp.where(rows <= cols, log_decay, 0.0), 0, keepdims=True)
    spread = jnp.where(rows >= cols, total_col - total_row, 0.0)
    upto = jnp.where(rows >= cols, jnp.exp(spread), 0.0)
    return beta, decay_in, log_decay, upto


def unit_lower_inverse(systems):
    size = systems[0].shape[0]
    rows, cols = iotas(size)
    block = 8
    near = [jnp.where(rows // block == cols // block, a, 0.0) for a in systems]
    eye = jnp.where(rows == cols, 1.0, 0.0)
    power = [dot_nn(a, a) for a in near]
    inverse = [eye - a for a in near]
    inverse = [x + dot_nn(x, p) for x, p in zip(inverse, power)]
    power = [dot_nn(p, p) for p in power]
    inverse = [x + dot_nn(x, p) for x, p in zip(inverse, power)]
    while block < size:
        cross = (rows // (2 * block) == cols // (2 * block)) & (rows // block != cols // block)
        middle = [dot_nn(jnp.where(cross, a, 0.0), x) for a, x in zip(systems, inverse)]
        inverse = [x - dot_nn(x, m) for x, m in zip(inverse, middle)]
        block *= 2
    return inverse


def pack_kernel(
    team,
    places,
    query,
    key,
    value,
    gate,
    proj,
    beta,
    decay,
    mix_gain,
    ffn_gain,
    query_conv,
    key_conv,
    value_conv,
    head_gain,
    pack_out,
    proj_out,
):
    part, shard = places[0], places[1]
    chunk = query.shape[0]
    keys, values = query.shape[1] // team, value.shape[1] // team
    outs = proj.shape[1] // team
    width = pack_out.shape[1]
    count = query_conv.shape[0]
    head_each = head_gain.shape[1]

    def columns(matrix, size):
        return matrix[:, pl.ds(pl.multiple_of(part * size, size), size)]

    pack_out[:chunk, :keys] = columns(query, keys)
    pack_out[:chunk, keys : 2 * keys] = columns(key, keys)
    pack_out[:chunk, 2 * keys : 2 * keys + values] = columns(value, values)
    pack_out[:chunk, 2 * keys + values :] = columns(gate, values)
    proj_out[...] = columns(proj, outs)
    rows, cols = iotas(chunk)

    def column_row(matrix):
        lane = lax.broadcasted_iota(jnp.int32, matrix.shape, 1)
        column = jnp.sum(jnp.where(lane == part, matrix[...].astype(WIDE), 0.0), 1, keepdims=True)
        return jnp.sum(jnp.where(rows == cols, column, 0.0), 0, keepdims=True)

    gains = [mix_gain[...].astype(WIDE), ffn_gain[...].astype(WIDE)]
    gains += [column_row(beta), column_row(decay)]
    gains.append(jnp.zeros((1, width - 4 * chunk), WIDE))
    pieces = []
    for taps, size in ((query_conv, keys), (key_conv, keys), (value_conv, values)):
        wide = taps[...].astype(WIDE)
        pieces.append(jnp.concatenate([wide] * (size // wide.shape[1]), 1))
    pieces = jnp.concatenate(pieces, 1)
    lane = lax.broadcasted_iota(jnp.int32, pieces.shape, 1)
    inside = jnp.where(lane < 2 * keys, lane % keys // query_conv.shape[1], 0)
    inside = jnp.where(lane < 2 * keys, inside, (lane - 2 * keys) // value_conv.shape[1])
    owners = keys // query_conv.shape[1]
    pieces = jnp.where(inside + part * owners == shard, pieces, 0.0)
    taps_rows = jnp.concatenate(
        [pieces, jnp.zeros((count, width - pieces.shape[1]), WIDE)], 1
    )
    head = jnp.concatenate([head_gain[...].astype(WIDE)] * (values // head_each), 1)
    lane = lax.broadcasted_iota(jnp.int32, head.shape, 1)
    head = jnp.where(lane // head_each == shard, head, 0.0)
    head = jnp.concatenate([head, jnp.zeros((1, width - values), WIDE)], 1)
    small = jnp.concatenate(
        [
            jnp.concatenate(gains, 1),
            taps_rows,
            head,
            jnp.zeros((ROWS16 - count - 2, width), WIDE),
        ],
        0,
    )
    pack_out[chunk:] = small.astype(LOW)


def slot_shard(places, slot, chips, same_core):
    chip, core = lax.div(places[1], 2), lax.rem(places[1], 2)
    return 2 * lax.rem(chip + chips - slot, chips) + (core if same_core else 1 - core)


def mixer_forward_kernel(
    seqs,
    keys,
    count,
    scalars,
    places,
    tokens,
    mine,
    theirs,
    first_out,
    raw_out,
    gate_out,
    gates_out,
    inverse_out,
    update_out,
    heads_out,
    mixed_out,
    weights,
    mix_row,
    ffn_row,
    gate_rows,
    taps,
    head_gain,
    gate_wide,
):
    size = tokens.shape[0] // seqs
    chips, block = mine.shape[0], mine.shape[1]
    chunk = block - ROWS16
    values = heads_out.shape[1]
    conv_width = 2 * keys + values
    gate_wide[...] = jnp.zeros(gate_wide.shape, WIDE)
    total = None
    for same_core, slots in ((True, mine), (False, theirs)):
        for slot in range(chips):
            shard = slot_shard(places, slot, chips, same_core)
            line = pl.ds(pl.multiple_of(shard * chunk, chunk), chunk)
            weights[line, :] = slots[slot, :chunk]
            small = slots[slot, chunk:].astype(WIDE)
            mix_row[:, line] = small[0:1, :chunk]
            ffn_row[:, line] = small[0:1, chunk : 2 * chunk]
            pair = small[0:1, 2 * chunk : 3 * chunk], small[0:1, 3 * chunk : 4 * chunk]
            for row in range(4):
                gate_wide[row : row + 1, line] = pair[row % 2]
            total = small if total is None else total + small
    gate_rows[...] = gate_wide[...].astype(LOW)
    taps[...] = total[1 : count + 1, :conv_width]
    head_gain[...] = total[count + 1 : count + 2, :values]
    wide = tokens[...].astype(WIDE)
    first = (
        wide * lax.rsqrt(jnp.mean(wide * wide, -1, keepdims=True) + EPS) * mix_row[...]
    ).astype(LOW)
    first_out[...] = first
    raw_out[...] = local_dot(first, weights[:, :conv_width])
    gate_out[...] = local_dot(first, weights[:, conv_width:])
    gates_out[...] = right_dot(first, gate_rows[...])
    rows, cols = iotas(size)
    parts = []
    for seq in range(seqs):
        span = slice(seq * size, (seq + 1) * size)
        run, sig = conv_silu(raw_out[span], taps[...])
        query, key, value = unit_features(run * sig, keys)[:3]
        beta, _, _, upto = decay_matrix(gates_out[span], scalars[0], scalars[1])
        system = jnp.where(rows > cols, beta * dot_nt(key, key) * upto, 0.0)
        scores = dot_nt(query, key) * upto
        parts.append((system, scores, beta * value))
    inverses = unit_lower_inverse([p[0] for p in parts])
    for seq in range(seqs):
        span = slice(seq * size, (seq + 1) * size)
        inverse_out[span] = inverses[seq]
        update = dot_nn(inverses[seq], parts[seq][2])
        heads = dot_nn(parts[seq][1], update)
        update_out[span] = update
        heads_out[span] = heads
        gate = gate_out[span]
        normed = heads * lax.rsqrt(jnp.mean(heads * heads, -1, keepdims=True) + EPS)
        mixed_out[span] = (normed * head_gain[...] * (gate * sigmoid(gate))).astype(LOW)


def member(part, steps):
    return jnp.bitwise_xor(part, steps)


def feed_forward_kernel(
    team,
    scalars,
    tokens,
    cotangents,
    *refs,
):
    mixed_slots, out_slots = refs[:team], refs[team : 2 * team]
    (
        gain,
        up_weights,
        down_weights,
        mixed_out,
        hidden_out,
        second_out,
        active_out,
        back_out,
        second_grad_out,
        gain_grad_out,
        result_out,
        out_full,
        hidden,
    ) = refs[2 * team :]
    part = scalars[0]
    size = tokens.shape[0] // team
    values = mixed_slots[0].shape[1]
    outs = out_slots[0].shape[2]
    for steps in range(team):
        place = pl.multiple_of(member(part, steps) * values, values)
        for slot in range(team):
            there = slot ^ steps
            mixed_out[slot * size : (slot + 1) * size, pl.ds(place, values)] = mixed_slots[
                steps
            ][there * size : (there + 1) * size]
    blocks = out_slots[0].shape[0]
    chunk = out_slots[0].shape[1]
    for steps in range(team):
        place = pl.multiple_of(member(part, steps) * outs, outs)
        for slot in range(blocks):
            chips = blocks // 2
            shard = slot_shard(scalars, slot % chips, chips, slot < chips)
            line = pl.ds(pl.multiple_of(shard * chunk, chunk), chunk)
            out_full[line, pl.ds(place, outs)] = out_slots[steps][slot]
    wide = tokens[...].astype(WIDE) + local_dot(mixed_out[...], out_full[...])
    hidden_out[...] = wide[:size]
    normed = wide * lax.rsqrt(jnp.mean(wide * wide, -1, keepdims=True) + EPS)
    second = (normed * gain[...]).astype(LOW)
    second_out[...] = second
    hidden[...] = normed
    part_width = active_out.shape[1]
    both = local_dot(second, up_weights[...])
    gate, up = both[:, :part_width], both[:, part_width:]
    gate_sig = sigmoid(gate)
    gate_act = gate * gate_sig
    active = (gate_act * up).astype(LOW)
    active_out[...] = active
    result_out[...] = local_dot(active, down_weights[...]).astype(LOW)
    active_grad = right_dot(cotangents[...], down_weights[...])
    gate_back = (active_grad * up * gate_sig * (1.0 + gate * (1.0 - gate_sig))).astype(LOW)
    up_back = (active_grad * gate_act).astype(LOW)
    back = jnp.concatenate([gate_back, up_back], 1)
    back_out[...] = back
    second_grad = right_dot(back, up_weights[...])
    second_grad_out[...] = second_grad.astype(LOW)
    gain_grad_out[...] = jnp.sum(second_grad * hidden[...], 0, keepdims=True)


def feed_forward_pack_kernel(team, shards, places, gate, up, down, pack):
    chunk = gate.shape[0]
    each = down.shape[0] // team
    padded = -(-each // ROWS16) * ROWS16
    ups = 2 * shards * each // LANES
    pad = jnp.zeros((padded - each, LANES), WIDE)

    for choice in range(team):

        @pl.when(places[0] == choice)
        def _():
            starts = [(s * team + choice) * each for s in range(shards)]
            wide = jnp.concatenate(
                [matrix[:, i : i + each].astype(WIDE) for matrix in (gate, up) for i in starts],
                1,
            )
            for index in range(ups):
                pack[index * chunk : (index + 1) * chunk] = wide[
                    :, index * LANES : (index + 1) * LANES
                ].astype(LOW)
            rows = down[...].astype(WIDE)[choice * each : (choice + 1) * each]
            for index in range(rows.shape[1] // LANES):
                start = ups * chunk + index * padded
                block = rows[:, index * LANES : (index + 1) * LANES]
                pack[start : start + padded] = jnp.concatenate([block, pad], 0).astype(LOW)


def feed_forward_unpack_kernel(shards, packs, up_out, down_out):
    chunk = up_out.shape[0] // shards
    each = down_out.shape[0] // shards
    padded = -(-each // ROWS16) * ROWS16
    ups = up_out.shape[1] // LANES
    for shard in range(shards):
        for index in range(ups):
            up_out[shard * chunk : (shard + 1) * chunk, index * LANES : (index + 1) * LANES] = (
                packs[shard, index * chunk : (index + 1) * chunk]
            )
    for pair in range(shards // 2):
        for index in range(down_out.shape[1] // LANES):
            start = ups * chunk + index * padded
            block = jnp.concatenate(
                [
                    packs[shard, start : start + padded].astype(WIDE)[:each]
                    for shard in (2 * pair, 2 * pair + 1)
                ],
                0,
            )
            down_out[
                2 * pair * each : 2 * (pair + 1) * each, index * LANES : (index + 1) * LANES
            ] = block.astype(LOW)


def feed_forward_weights_kernel(shards, second, back, active, cotangents, pack):
    up_grad = left_dot(second[...], back[...])
    down_grad = left_dot(active[...], cotangents[...])
    chunk = up_grad.shape[0] // shards
    each = down_grad.shape[0] // shards
    padded = -(-each // ROWS16) * ROWS16
    pad = jnp.zeros((padded - each, LANES), WIDE)
    ups = up_grad.shape[1] // LANES
    for shard in range(shards):
        for index in range(ups):
            pack[shard, index * chunk : (index + 1) * chunk] = up_grad[
                shard * chunk : (shard + 1) * chunk, index * LANES : (index + 1) * LANES
            ].astype(LOW)
        for index in range(down_grad.shape[1] // LANES):
            start = ups * chunk + index * padded
            block = down_grad[
                shard * each : (shard + 1) * each, index * LANES : (index + 1) * LANES
            ]
            pack[shard, start : start + padded] = jnp.concatenate([block, pad], 0).astype(LOW)


def feed_forward_finish_kernel(team, shards, places, *refs):
    slots = refs[:team]
    gate_out, up_out, down_out, ordered = refs[team:]
    chunk = gate_out.shape[0]
    each = down_out.shape[0] // team
    padded = -(-each // ROWS16) * ROWS16
    half = shards * each
    ups = 2 * half // LANES
    for steps in range(team):
        ordered[member(places[0], steps)] = slots[steps][...].astype(LOW)
    wide = [
        jnp.concatenate(
            [ordered[h, i * chunk : (i + 1) * chunk].astype(WIDE) for i in range(ups)], 1
        )
        for h in range(team)
    ]
    for base, out in ((0, gate_out), (half, up_out)):
        out[...] = jnp.concatenate(
            [
                wide[h][:, base + s * each : base + (s + 1) * each]
                for s in range(shards)
                for h in range(team)
            ],
            1,
        )
    for h in range(team):
        for index in range(down_out.shape[1] // LANES):
            start = ups * chunk + index * padded
            down_out[h * each : (h + 1) * each, index * LANES : (index + 1) * LANES] = ordered[
                h, start : start + padded
            ].astype(WIDE)[:each]


def mixer_backward_kernel(
    seqs,
    keys,
    shards,
    scalars,
    places,
    *refs,
):
    branch_slots = refs[:seqs]
    (
        out_full,
        gate_raw,
        heads,
        head_gain,
        first,
        mixed,
        raw,
        gates,
        inverse,
        update,
        taps,
        weights,
        gate_rows,
        tokens,
        ffn_gain_grad,
        mine,
        theirs,
        first_grad_out,
        raw_grad_out,
        gates_grad_out,
        branch_grad,
        heads_grad,
    ) = refs[seqs:]
    values = heads.shape[1]
    outs = out_full.shape[1] // seqs
    for slot in range(seqs):
        rows_each = branch_slots[slot].shape[0]
        branch_grad[slot * rows_each : (slot + 1) * rows_each] = branch_slots[slot][...]
    row = pl.multiple_of(places[0] * values, values)
    mixed_grad = right_dot(branch_grad[...], out_full[pl.ds(row, values)])
    out = heads[...]
    gate = gate_raw[...]
    gain = head_gain[...]
    scale = lax.rsqrt(jnp.mean(out * out, -1, keepdims=True) + EPS)
    normed = out * scale
    gate_sig = sigmoid(gate)
    gate_act = gate * gate_sig
    gate_grad = (
        mixed_grad * normed * gain * gate_sig * (1.0 + gate * (1.0 - gate_sig))
    ).astype(LOW)
    head_gain_grad = jnp.sum(mixed_grad * normed * gate_act, 0, keepdims=True)
    normed_grad = mixed_grad * gain * gate_act
    heads_grad[...] = scale * (
        normed_grad - normed * jnp.mean(normed_grad * normed, -1, keepdims=True)
    )
    place = pl.multiple_of(places[0] * outs, outs)
    gate_wgrad = left_dot(first[...], gate_grad)
    out_wgrad = left_dot(mixed[...], branch_grad[:, pl.ds(place, outs)])
    size = raw.shape[0] // seqs
    conv_width = taps.shape[1]
    count = taps.shape[0]
    part, shard = places[0], places[1]
    rows, cols = iotas(size)
    taps_grad = [jnp.zeros((1, conv_width), WIDE) for _ in range(count)]
    log_total = jnp.zeros((1, 1), WIDE)
    bias_total = jnp.zeros((1, 1), WIDE)
    for seq in range(seqs):
        span = slice(seq * size, (seq + 1) * size)
        out_grad = heads_grad[span]
        raw_in = raw[span]
        run, sig = conv_silu(raw_in, taps[...])
        query, key, value, query_act, query_r, key_act, key_r = unit_features(run * sig, keys)
        beta, decay_in, log_decay, upto = decay_matrix(gates[span], scalars[0], scalars[1])
        key_key = dot_nt(key, key) * upto
        scores = dot_nt(query, key) * upto
        solved = update[span]
        scores_grad = jnp.where(rows >= cols, dot_nt(out_grad, solved), 0.0)
        solved_grad = dot_tn(scores, out_grad)
        target_grad = dot_tn(inverse[span], solved_grad)
        system_grad = jnp.where(rows > cols, -dot_nt(target_grad, solved), 0.0)
        value_grad = beta * target_grad
        system_part = system_grad * key_key
        beta_grad = jnp.sum(target_grad * value, 1, keepdims=True) + jnp.sum(
            system_part, 1, keepdims=True
        )
        key_key_grad = system_grad * (beta * upto)
        scores_part = scores_grad * upto
        spread_grad = system_part * beta + scores_grad * scores
        query_grad = dot_nn(scores_part, key)
        key_grad = (
            dot_tn(scores_part, query) + dot_nn(key_key_grad, key) + dot_tn(key_key_grad, key)
        )
        total_row = jnp.sum(
            jnp.where(rows == cols, jnp.sum(spread_grad, 1, keepdims=True), 0.0),
            0,
            keepdims=True,
        ) - jnp.sum(spread_grad, 0, keepdims=True)
        decay_grad = jnp.sum(jnp.where(cols >= rows, total_row, 0.0), 1, keepdims=True)
        decay_raw_grad = -scalars[0] * decay_grad * sigmoid(decay_in)
        beta_raw_grad = beta_grad * beta * (1.0 - beta)
        log_total = log_total + jnp.sum(decay_grad * log_decay, 0, keepdims=True)
        bias_total = bias_total + jnp.sum(decay_raw_grad, 0, keepdims=True)
        beta_high = beta_raw_grad.astype(LOW).astype(WIDE)
        decay_high = decay_raw_grad.astype(LOW).astype(WIDE)
        lane = lax.broadcasted_iota(jnp.int32, (size, ROWS16), 1)
        gates_grad_out[span] = jnp.where(
            lane == 0,
            beta_high,
            jnp.where(
                lane == 1,
                decay_high,
                jnp.where(
                    lane == 2,
                    beta_raw_grad - beta_high,
                    jnp.where(lane == 3, decay_raw_grad - decay_high, 0.0),
                ),
            ),
        ).astype(LOW)
        query_grad = query_grad * (1.0 / math.sqrt(keys))
        query_unit = query_act * query_r
        query_act_grad = query_r * (
            query_grad - query_unit * jnp.sum(query_unit * query_grad, -1, keepdims=True)
        )
        key_act_grad = key_r * (key_grad - key * jnp.sum(key * key_grad, -1, keepdims=True))
        act_grad = jnp.concatenate([query_act_grad, key_act_grad, value_grad], 1)
        run_grad = act_grad * sig * (1.0 + run * (1.0 - sig))
        raw_grad = run_grad * taps[count - 1 : count]
        taps_grad[count - 1] = taps_grad[count - 1] + jnp.sum(
            run_grad * raw_in, 0, keepdims=True
        )
        for steps in range(1, count):
            tap = count - 1 - steps
            moved = earlier(run_grad, steps)
            raw_grad = raw_grad + moved * taps[tap : tap + 1]
            taps_grad[tap] = taps_grad[tap] + jnp.sum(moved * raw_in, 0, keepdims=True)
        raw_grad_out[span] = raw_grad.astype(LOW)
    width = tokens.shape[1]
    chunk = width // shards
    core = lax.rem(shard, 2)
    raw_low = raw_grad_out[...]
    head_wgrad = left_dot(first[...], raw_low)
    gates_rows = left_dot(gates_grad_out[...], first[...])
    first_grad = (
        right_dot(raw_low, weights[:, :conv_width])
        + right_dot(gate_grad, weights[:, conv_width:])
        + local_dot(gates_grad_out[...], gate_rows[...])
    )
    first_grad_out[...] = first_grad.astype(LOW)
    wide = tokens[...].astype(WIDE)
    normed = wide * lax.rsqrt(jnp.mean(wide * wide, -1, keepdims=True) + EPS)
    gain_grad = jnp.sum(first_grad * normed, 0, keepdims=True)
    beta_row = gates_rows[0:1] + gates_rows[2:3]
    decay_row = gates_rows[1:2] + gates_rows[3:4]
    head_shards = shards // seqs
    key_each = keys // head_shards
    value_each = (conv_width - 2 * keys) // head_shards
    head_each = head_gain_grad.shape[1] // shards
    all_taps = jnp.concatenate(taps_grad, 0)
    lane = lax.broadcasted_iota(jnp.int32, (1, conv_width), 1)
    decay_terms = jnp.zeros((1, conv_width), WIDE)
    for which, total in enumerate((log_total, bias_total)):
        for piece in range(3):
            high = total.astype(LOW).astype(WIDE)
            place = head_each + (which * 3 + piece) * shards + shard
            decay_terms = jnp.where(lane == place, high, decay_terms)
            total = total - high
    blocks = []
    for s in range(shards):
        line = slice(s * chunk, (s + 1) * chunk)
        i = s % head_shards
        gains = jnp.concatenate(
            [beta_row[:, line], decay_row[:, line], gain_grad[:, line], ffn_gain_grad[:, line]], 1
        )
        tap_rows = jnp.concatenate(
            [
                all_taps[:, i * key_each : (i + 1) * key_each],
                all_taps[:, keys + i * key_each : keys + (i + 1) * key_each],
                all_taps[:, 2 * keys + i * value_each : 2 * keys + (i + 1) * value_each],
            ],
            1,
        )
        tap_rows = jnp.where(part == s // head_shards, tap_rows, 0.0)
        tap_rows = jnp.concatenate(
            [tap_rows, jnp.zeros((count, conv_width - tap_rows.shape[1]), WIDE)], 1
        )
        head_row = jnp.concatenate(
            [
                head_gain_grad[:, s * head_each : (s + 1) * head_each],
                jnp.zeros((1, conv_width - head_each), WIDE),
            ],
            1,
        )
        small = jnp.concatenate(
            [
                gains,
                tap_rows,
                head_row + decay_terms,
                jnp.zeros((ROWS16 - count - 2, conv_width), WIDE),
            ],
            0,
        )
        empty = jnp.zeros((ROWS16, values + outs), WIDE)
        blocks.append(
            (
                head_wgrad[line],
                gate_wgrad[line],
                out_wgrad[line],
                jnp.concatenate([small, empty], 1),
            )
        )
    top, all_lanes = slice(0, chunk), slice(0, conv_width + values + outs)
    spots = (
        (top, slice(0, conv_width)),
        (top, slice(conv_width, conv_width + values)),
        (top, slice(conv_width + values, conv_width + values + outs)),
        (slice(chunk, chunk + ROWS16), all_lanes),
    )
    for pair in range(shards // 2):
        for even, odd, (line, lanes) in zip(blocks[2 * pair], blocks[2 * pair + 1], spots):
            mine[pair, line, lanes] = jnp.where(core == 0, even, odd).astype(LOW)
            theirs[pair, line, lanes] = jnp.where(core == 0, odd, even).astype(LOW)


def finish_kernel(
    team,
    keys,
    shards,
    count,
    scalars,
    *refs,
):
    slots = refs[:team]
    (
        query_out,
        key_out,
        value_out,
        gate_out,
        proj_out,
        beta_out,
        decay_out,
        mix_out,
        ffn_out,
        query_conv_out,
        key_conv_out,
        value_conv_out,
        head_out,
        log_out,
        bias_out,
        pair,
    ) = refs[team:]
    part = scalars[0]
    chunk = query_out.shape[0]
    values = value_out.shape[1] // team
    conv_width = 2 * keys + values
    key_each = query_conv_out.shape[1]
    conv_each = 2 * key_each + value_conv_out.shape[1]
    head_each = head_out.shape[1]
    total = None
    lane = lax.broadcasted_iota(jnp.int32, (1, LANES), 1)
    log_row = jnp.zeros((1, LANES), WIDE)
    bias_row = jnp.zeros((1, LANES), WIDE)
    pair[...] = jnp.zeros(pair.shape, WIDE)
    for steps in range(team):
        head = member(part, steps)
        key_place = pl.ds(pl.multiple_of(head * keys, keys), keys)
        value_place = pl.ds(pl.multiple_of(head * values, values), values)
        block = slots[steps]
        query_out[:, key_place] = block[:chunk, :keys].astype(WIDE)
        key_out[:, key_place] = block[:chunk, keys : 2 * keys].astype(WIDE)
        value_out[:, value_place] = block[:chunk, 2 * keys : conv_width].astype(WIDE)
        gate_out[:, value_place] = block[:chunk, conv_width : conv_width + values].astype(WIDE)
        proj_out[:, value_place] = block[:chunk, conv_width + values :].astype(WIDE)
        small = block[chunk:, :conv_width].astype(WIDE)
        total = small if total is None else total + small
        pair[pl.ds(head, 1), :] = small[0:1, :chunk]
        pair[pl.ds(head + team, 1), :] = small[0:1, chunk : 2 * chunk]
        terms = small[count + 1 : count + 2]
        wide_lane = lax.broadcasted_iota(jnp.int32, (1, conv_width), 1)
        ends = [head_each + 3 * shards * k for k in range(3)]
        log_sum = jnp.sum(
            jnp.where((wide_lane >= ends[0]) & (wide_lane < ends[1]), terms, 0.0),
            1,
            keepdims=True,
        )
        bias_sum = jnp.sum(
            jnp.where((wide_lane >= ends[1]) & (wide_lane < ends[2]), terms, 0.0),
            1,
            keepdims=True,
        )
        log_row = jnp.where(lane == head, log_sum, log_row)
        bias_row = jnp.where(lane == head, bias_sum, bias_row)
    flipped = pair[...].T
    beta_out[...] = flipped[:, :team]
    decay_out[...] = flipped[:, team : 2 * team]
    mix_out[...] = total[0:1, 2 * chunk : 3 * chunk]
    ffn_out[...] = total[0:1, 3 * chunk : 4 * chunk]
    query_conv_out[...] = total[1 : count + 1, :key_each]
    key_conv_out[...] = total[1 : count + 1, key_each : 2 * key_each]
    value_conv_out[...] = total[1 : count + 1, 2 * key_each : conv_each]
    head_out[...] = total[count + 1 : count + 2, :head_each]
    log_out[...] = log_row[:, :team]
    bias_out[...] = bias_row[:, :team]


def array(shape, dtype):
    return jax.ShapeDtypeStruct(shape, dtype)


def run_kernel(kernel, name, scalars, operands, outs, flops, scratch=()):
    spec = pl.BlockSpec(memory_space=pltpu.VMEM)
    moved = sum(math.prod(v.shape) * v.dtype.itemsize for v in (*operands, *outs))
    return pl.pallas_call(
        kernel,
        out_shape=tuple(outs),
        in_specs=[pl.BlockSpec(memory_space=pltpu.SMEM)] * len(scalars) + [spec] * len(operands),
        out_specs=[spec] * len(outs),
        scratch_shapes=list(scratch),
        compiler_params=pltpu.CompilerParams(vmem_limit_bytes=48 * 1024 * 1024),
        cost_estimate=pl.CostEstimate(flops=flops, bytes_accessed=moved, transcendentals=0),
        name=name,
    )(*scalars, *operands)


def team_pairs(devices, steps):
    return [(j, j ^ steps) for j in range(devices)]


def team_gather(block, devices, team):
    return [block] + [
        lax.ppermute(block, "rep", team_pairs(devices, steps)) for steps in range(1, team)
    ]


def team_double(block, devices, team, axis, order):
    size = block.shape[axis]
    held = {0: block}
    for bit in order:
        both = jnp.concatenate([held[e] for e in held], axis) if len(held) > 1 else block
        moved = lax.ppermute(both, "rep", team_pairs(devices, bit))
        fresh = {
            e ^ bit: lax.slice_in_dim(moved, i * size, (i + 1) * size, axis=axis)
            for i, e in enumerate(held)
        }
        held = held | fresh
    return [held[e] for e in range(team)]


def team_send(slots, devices, team):
    return [slots[0]] + [
        lax.ppermute(slots[steps], "rep", team_pairs(devices, steps)) for steps in range(1, team)
    ]


def wide_sum(blocks):
    total = blocks[0].astype(WIDE)
    for block in blocks[1:]:
        total = total + block.astype(WIDE)
    return total


def line_ring(shards, steps):
    return [(j, (j + 2 * steps) % shards) for j in range(shards)]


def pair_ring(shards):
    return [(j, j ^ 1) for j in range(shards)]


def line_gather(block, shards):
    return [block] + [
        lax.ppermute(block, "shard", line_ring(shards, steps))
        for steps in range(1, shards // 2)
    ]


def core_swap(block, shards):
    return lax.ppermute(block, "shard", pair_ring(shards))


def pair_sum(mine, theirs, shards):
    moved = lax.ppermute(theirs, "shard", pair_ring(shards))
    return (mine.astype(WIDE) + moved.astype(WIDE)).astype(LOW)


def line_send(summed, shard, shards):
    chips = shards // 2
    chip = shard // 2
    terms = [lax.dynamic_index_in_dim(summed, chip, 0, keepdims=False)]
    for steps in range(1, chips):
        block = lax.dynamic_index_in_dim(summed, (chip + steps) % chips, 0, keepdims=False)
        terms.append(lax.ppermute(block, "shard", line_ring(shards, steps)))
    return terms


def norm_scale(v):
    return lax.rsqrt(jnp.mean(v * v, -1, keepdims=True) + EPS)


def replica_slots(block, part, devices, team):
    if devices == team:
        return team_gather(block, devices, team)
    blocks = lax.all_gather(block, "rep").astype(WIDE)
    blocks = jnp.sum(blocks.reshape((devices // team, team) + block.shape), 0)
    return [
        lax.dynamic_index_in_dim(blocks, part ^ e, 0, keepdims=False)
        for e in range(team)
    ]


def after(values, first):
    return lax.optimization_barrier((values, first))[0]


def body(
    inputs,
    cotangent,
    mix_gain,
    query_proj,
    key_proj,
    value_proj,
    beta_proj,
    decay_proj,
    gate_proj,
    query_conv,
    key_conv,
    value_conv,
    decay_log,
    decay_bias,
    head_gain,
    out_proj,
    ffn_gain,
    ffn_gate,
    ffn_up,
    ffn_down,
):
    devices = lax.axis_size("rep")
    shards = lax.axis_size("shard")
    team = beta_proj.shape[1]
    part = lax.axis_index("rep") % team
    shard = lax.axis_index("shard")
    places = jnp.stack([part, shard]).astype(jnp.int32)
    tokens_each, width = inputs.shape
    count = team * tokens_each
    chunk = mix_gain.shape[0]
    keys = query_proj.shape[1] // team
    values = value_proj.shape[1] // team
    outs = out_proj.shape[1] // team
    conv_width = 2 * keys + values
    hidden_each = ffn_down.shape[0] // team
    hidden_part = hidden_each * shards
    taps_count = query_conv.shape[0]
    key_each, value_each = query_conv.shape[1], value_conv.shape[1]
    head_each = head_gain.shape[0]

    padded = -(-hidden_each // ROWS16) * ROWS16
    ffn_rows = 2 * hidden_part * chunk // LANES + padded * (width // LANES)

    mixer_pack, proj_part = run_kernel(
        functools.partial(pack_kernel, team),
        "pack",
        (places,),
        (
            query_proj,
            key_proj,
            value_proj,
            gate_proj,
            out_proj,
            beta_proj,
            decay_proj,
            mix_gain[None],
            ffn_gain[None],
            query_conv,
            key_conv,
            value_conv,
            head_gain[None],
        ),
        (
            array((chunk + ROWS16, conv_width + values), LOW),
            array((chunk, outs), LOW),
        ),
        10**8,
    )
    proj_slots = line_gather(proj_part, shards)
    mixer_slots = line_gather(mixer_pack, shards)
    ffn_pack = run_kernel(
        functools.partial(feed_forward_pack_kernel, team, shards),
        "feed_forward_pack",
        (places,),
        (ffn_gate, ffn_up, ffn_down),
        (array((ffn_rows, LANES), LOW),),
        10**8,
    )[0]
    ffn_packs = lax.all_gather(ffn_pack, "shard", axis=0)
    proj_mine = jnp.stack(proj_slots)
    proj_all = jnp.concatenate([proj_mine, core_swap(proj_mine, shards)], 0)
    token_slots = team_double(after(inputs, proj_mine), devices, team, 0, (1, 2))
    proj_slots = team_double(proj_all, devices, team, 0, (2, 1))
    pack_mine = jnp.stack(mixer_slots)
    pack_theirs = core_swap(pack_mine, shards)
    cotangent_slots = team_double(after(cotangent, pack_mine), devices, team, 0, (1, 2))
    tokens = jnp.concatenate(token_slots, 0)
    cotangents = jnp.concatenate(cotangent_slots, 0)
    scalars = jnp.stack(
        [
            jnp.exp(lax.dynamic_index_in_dim(decay_log, part, 0, keepdims=False)),
            lax.dynamic_index_in_dim(decay_bias, part, 0, keepdims=False),
        ]
    )

    (
        first,
        raw,
        gate_raw,
        gates,
        inverse,
        update,
        heads,
        mixed_part,
        head_weights,
        mix_row,
        ffn_row,
        gate_rows,
        taps,
        head_row,
    ) = run_kernel(
        functools.partial(mixer_forward_kernel, team, keys, taps_count),
        "mixer_forward",
        (scalars, places),
        (tokens, pack_mine, pack_theirs),
        (
            array((count, width), LOW),
            array((count, conv_width), WIDE),
            array((count, values), WIDE),
            array((count, ROWS16), WIDE),
            array((count, tokens_each), WIDE),
            array((count, values), WIDE),
            array((count, values), WIDE),
            array((count, values), LOW),
            array((width, conv_width + values), LOW),
            array((1, width), WIDE),
            array((1, width), WIDE),
            array((ROWS16, width), LOW),
            array((taps_count, conv_width), WIDE),
            array((1, values), WIDE),
        ),
        8 * 10**9,
        (pltpu.VMEM((ROWS16, width), WIDE),),
    )
    mixed_slots = team_gather(mixed_part, devices, team)
    up_weights, down_weights = run_kernel(
        functools.partial(feed_forward_unpack_kernel, shards),
        "feed_forward_unpack",
        (),
        (ffn_packs,),
        (
            array((width, 2 * hidden_part), LOW),
            array((hidden_part, width), LOW),
        ),
        10**8,
    )

    (
        mixed,
        hidden_own,
        second,
        active,
        both_back,
        second_part,
        ffn_gain_part,
        result_part,
        out_full,
    ) = run_kernel(
        functools.partial(feed_forward_kernel, team),
        "feed_forward",
        (places,),
        (tokens, cotangents, *mixed_slots, *proj_slots, ffn_row, up_weights, down_weights),
        (
            array((count, width), LOW),
            array((tokens_each, width), WIDE),
            array((count, width), LOW),
            array((count, hidden_part), LOW),
            array((count, 2 * hidden_part), LOW),
            array((count, width), LOW),
            array((1, width), WIDE),
            array((count, width), LOW),
            array((width, width), LOW),
        ),
        10 * 10**9,
        (pltpu.VMEM((count, width), WIDE),),
    )

    def slots_of(v):
        return [v[e * tokens_each : (e + 1) * tokens_each] for e in range(team)]

    second_slots = team_send(slots_of(second_part), devices, team)
    ffn_grads = run_kernel(
        functools.partial(feed_forward_weights_kernel, shards),
        "feed_forward_weights",
        (),
        (second, both_back, active, cotangents),
        (array((shards, ffn_rows, LANES), LOW),),
        6 * 10**9,
    )[0]
    second_slots = after(second_slots, ffn_grads)
    ffn_shard = lax.psum_scatter(ffn_grads, "shard", scatter_dimension=0)
    second_grad = wide_sum(second_slots)
    scale_own = norm_scale(hidden_own)
    weighted = second_grad * ffn_row
    hidden_grad = cotangent.astype(WIDE) + scale_own * (
        weighted
        - hidden_own
        * (scale_own * scale_own * jnp.mean(hidden_own * weighted, -1, keepdims=True))
    )
    branch_slots = team_gather(hidden_grad.astype(LOW), devices, team)
    result_part = after(result_part, branch_slots)
    result_slots = team_send(slots_of(result_part), devices, team)

    head_mine, head_theirs, first_part = run_kernel(
        functools.partial(mixer_backward_kernel, team, keys, shards),
        "mixer_backward",
        (scalars, places),
        (
            *branch_slots,
            out_full,
            gate_raw,
            heads,
            head_row,
            first,
            mixed,
            raw,
            gates,
            inverse,
            update,
            taps,
            head_weights,
            gate_rows,
            tokens,
            ffn_gain_part,
        ),
        (
            array((shards // 2, chunk + ROWS16, conv_width + values + outs), LOW),
            array((shards // 2, chunk + ROWS16, conv_width + values + outs), LOW),
            array((count, width), LOW),
        ),
        10 * 10**9,
        (
            pltpu.VMEM((count, conv_width), LOW),
            pltpu.VMEM((count, ROWS16), LOW),
            pltpu.VMEM((count, width), LOW),
            pltpu.VMEM((count, values), WIDE),
        ),
    )
    head_summed = pair_sum(head_mine, head_theirs, shards)
    head_terms = line_send(head_summed, shard, shards)
    first_grad = wide_sum(team_send(slots_of(first_part), devices, team))
    seq_in = inputs.astype(WIDE)
    seq_scale = norm_scale(seq_in)
    weighted = first_grad * mix_row
    inputs_grad = hidden_grad + seq_scale * (
        weighted
        - seq_in * (seq_scale * seq_scale * jnp.mean(seq_in * weighted, -1, keepdims=True))
    )
    result = hidden_own + wide_sum(result_slots)

    head_totals = replica_slots(wide_sum(head_terms).astype(LOW), part, devices, team)
    ffn_totals = replica_slots(ffn_shard, part, devices, team)
    gate_grads, up_grads, down_grads = run_kernel(
        functools.partial(feed_forward_finish_kernel, team, shards),
        "feed_forward_finish",
        (places,),
        ffn_totals,
        (
            array(ffn_gate.shape, WIDE),
            array(ffn_up.shape, WIDE),
            array(ffn_down.shape, WIDE),
        ),
        10**8,
        (pltpu.VMEM((team, ffn_rows, LANES), LOW),),
    )
    (
        query_total,
        key_total,
        value_total,
        gate_total,
        out_total,
        beta_total,
        decay_total,
        mix_total,
        ffn_total,
        query_conv_total,
        key_conv_total,
        value_conv_total,
        head_total,
        log_total,
        bias_total,
    ) = run_kernel(
        functools.partial(finish_kernel, team, keys, shards, taps_count),
        "finish",
        (places,),
        head_totals,
        (
            array((chunk, team * keys), WIDE),
            array((chunk, team * keys), WIDE),
            array((chunk, team * values), WIDE),
            array((chunk, team * values), WIDE),
            array((chunk, team * outs), WIDE),
            array((chunk, team), WIDE),
            array((chunk, team), WIDE),
            array((1, chunk), WIDE),
            array((1, chunk), WIDE),
            array((taps_count, key_each), WIDE),
            array((taps_count, key_each), WIDE),
            array((taps_count, value_each), WIDE),
            array((1, head_each), WIDE),
            array((1, team), WIDE),
            array((1, team), WIDE),
        ),
        10**8,
        (pltpu.VMEM((max(8, 2 * team), chunk), WIDE),),
    )
    return (
        result.astype(LOW),
        inputs_grad,
        mix_total[0],
        query_total,
        key_total,
        value_total,
        beta_total,
        decay_total,
        gate_total,
        query_conv_total,
        key_conv_total,
        value_conv_total,
        log_total[0],
        bias_total[0],
        head_total[0],
        out_total,
        ffn_total[0],
        gate_grads,
        up_grads,
        down_grads,
    )


def solution(mesh):
    rows = P("shard", None)
    return jax.shard_map(
        body,
        mesh=mesh,
        in_specs=(
            P(("rep", "shard"), None),
            P(("rep", "shard"), None),
            P("shard"),
            rows,
            rows,
            rows,
            rows,
            rows,
            rows,
            P(None, "shard"),
            P(None, "shard"),
            P(None, "shard"),
            P(),
            P(),
            P("shard"),
            rows,
            P("shard"),
            rows,
            rows,
            rows,
        ),
        out_specs=(
            P(("rep", "shard"), None),
            P(("rep", "shard"), None),
            P("shard"),
            rows,
            rows,
            rows,
            rows,
            rows,
            rows,
            P(None, "shard"),
            P(None, "shard"),
            P(None, "shard"),
            P(),
            P(),
            P("shard"),
            rows,
            P("shard"),
            rows,
            rows,
            rows,
        ),
        check_vma=False,
    )
```

```python
import functools
import math

import jax
import jax.numpy as jnp
from jax import lax
from jax.experimental import pallas as pl
from jax.experimental.pallas import tpu as pltpu
from jax.sharding import PartitionSpec as P

EPS = 1e-06
HIGH = lax.Precision.HIGHEST
LOW = jnp.bfloat16
WIDE = jnp.float32
LANES = 128
ROWS16 = 16


def local_dot(left, right):
    return jnp.dot(left, right, preferred_element_type=WIDE)


def left_dot(left, right):
    return lax.dot_general(left, right, (((0,), (0,)), ((), ())), preferred_element_type=WIDE)


def right_dot(left, right):
    return lax.dot_general(left, right, (((1,), (1,)), ((), ())), preferred_element_type=WIDE)


def dot_nn(left, right):
    return jnp.dot(left, right, preferred_element_type=WIDE, precision=HIGH)


def dot_nt(left, right):
    return lax.dot_general(
        left, right, (((1,), (1,)), ((), ())), preferred_element_type=WIDE, precision=HIGH
    )


def dot_tn(left, right):
    return lax.dot_general(
        left, right, (((0,), (0,)), ((), ())), preferred_element_type=WIDE, precision=HIGH
    )


def sigmoid(v):
    return 1.0 / (1.0 + jnp.exp(-v))


def iotas(size):
    return (
        lax.broadcasted_iota(jnp.int32, (size, size), 0),
        lax.broadcasted_iota(jnp.int32, (size, size), 1),
    )


def later(v, steps):
    rows = lax.broadcasted_iota(jnp.int32, v.shape, 0)
    return jnp.where(rows >= steps, pltpu.roll(v, steps, 0), 0.0)


def earlier(v, steps):
    rows = lax.broadcasted_iota(jnp.int32, v.shape, 0)
    return jnp.where(rows < v.shape[0] - steps, pltpu.roll(v, v.shape[0] - steps, 0), 0.0)


def conv_silu(raw, taps):
    count = taps.shape[0]
    run = raw * taps[count - 1 : count]
    for steps in range(1, count):
        run = run + later(raw, steps) * taps[count - 1 - steps : count - steps]
    sig = sigmoid(run)
    return run, sig


def unit_features(act, keys):
    query_act, key_act, value = act[:, :keys], act[:, keys : 2 * keys], act[:, 2 * keys :]
    query_r = lax.rsqrt(jnp.sum(query_act * query_act, -1, keepdims=True) + EPS)
    key_r = lax.rsqrt(jnp.sum(key_act * key_act, -1, keepdims=True) + EPS)
    query = query_act * query_r * (1.0 / math.sqrt(keys))
    return query, key_act * key_r, value, query_act, query_r, key_act, key_r


def softplus(v):
    return jnp.maximum(v, 0.0) + jnp.log1p(jnp.exp(-jnp.abs(v)))


def decay_matrix(gates, decay, bias):
    size = gates.shape[0]
    rows, cols = iotas(size)
    beta = sigmoid(gates[:, 0:1])
    decay_in = gates[:, 1:2] + bias
    log_decay = -decay * softplus(decay_in)
    decay_row = jnp.sum(jnp.where(rows == cols, log_decay, 0.0), 0, keepdims=True)
    total_col = jnp.sum(jnp.where(cols <= rows, decay_row, 0.0), 1, keepdims=True)
    total_row = jnp.sum(jnp.where(rows <= cols, log_decay, 0.0), 0, keepdims=True)
    spread = jnp.where(rows >= cols, total_col - total_row, 0.0)
    upto = jnp.where(rows >= cols, jnp.exp(spread), 0.0)
    return beta, decay_in, log_decay, upto


def unit_lower_inverse(systems):
    size = systems[0].shape[0]
    rows, cols = iotas(size)
    block = 8
    near = [jnp.where(rows // block == cols // block, a, 0.0) for a in systems]
    eye = jnp.where(rows == cols, 1.0, 0.0)
    power = [dot_nn(a, a) for a in near]
    inverse = [eye - a for a in near]
    inverse = [x + dot_nn(x, p) for x, p in zip(inverse, power)]
    power = [dot_nn(p, p) for p in power]
    inverse = [x + dot_nn(x, p) for x, p in zip(inverse, power)]
    while block < size:
        cross = (rows // (2 * block) == cols // (2 * block)) & (rows // block != cols // block)
        middle = [dot_nn(jnp.where(cross, a, 0.0), x) for a, x in zip(systems, inverse)]
        inverse = [x - dot_nn(x, m) for x, m in zip(inverse, middle)]
        block *= 2
    return inverse


def pack_kernel(
    team,
    places,
    query,
    key,
    value,
    gate,
    proj,
    beta,
    decay,
    mix_gain,
    ffn_gain,
    query_conv,
    key_conv,
    value_conv,
    head_gain,
    pack_out,
    sems,
):
    part, shard = places[0], places[1]
    chunk = query.shape[0]
    keys, values = query.shape[1] // team, value.shape[1] // team
    outs = proj.shape[1] // team
    width = pack_out.shape[1]
    count = query_conv.shape[0]
    head_each = head_gain.shape[1]
    copies = []
    start = 0
    for index, (matrix, size) in enumerate(
        ((query, keys), (key, keys), (value, values), (gate, values), (proj, outs))
    ):
        source = matrix.at[:, pl.ds(pl.multiple_of(part * size, size), size)]
        target = pack_out.at[:chunk, start : start + size]
        start += size
        copies.append(pltpu.make_async_copy(source, target, sems.at[index]))
    for copy in copies:
        copy.start()

    def head_row(matrix):
        line = lax.broadcasted_iota(jnp.int32, matrix.shape, 0)
        return jnp.sum(jnp.where(line == part, matrix[...].astype(WIDE), 0.0), 0, keepdims=True)

    gains = [mix_gain[...].astype(WIDE), ffn_gain[...].astype(WIDE)]
    gains += [head_row(beta), head_row(decay)]
    gains.append(jnp.zeros((1, width - 4 * chunk), WIDE))
    pieces = []
    for taps, size in ((query_conv, keys), (key_conv, keys), (value_conv, values)):
        wide = taps[...].astype(WIDE)
        pieces.append(jnp.concatenate([wide] * (size // wide.shape[1]), 1))
    pieces = jnp.concatenate(pieces, 1)
    lane = lax.broadcasted_iota(jnp.int32, pieces.shape, 1)
    inside = jnp.where(lane < 2 * keys, lane % keys // query_conv.shape[1], 0)
    inside = jnp.where(lane < 2 * keys, inside, (lane - 2 * keys) // value_conv.shape[1])
    owners = keys // query_conv.shape[1]
    pieces = jnp.where(inside + part * owners == shard, pieces, 0.0)
    taps_rows = jnp.concatenate(
        [pieces, jnp.zeros((count, width - pieces.shape[1]), WIDE)], 1
    )
    head = jnp.concatenate([head_gain[...].astype(WIDE)] * (values // head_each), 1)
    lane = lax.broadcasted_iota(jnp.int32, head.shape, 1)
    head = jnp.where(lane // head_each == shard, head, 0.0)
    head = jnp.concatenate([head, jnp.zeros((1, width - values), WIDE)], 1)
    small = jnp.concatenate(
        [
            jnp.concatenate(gains, 1),
            taps_rows,
            head,
            jnp.zeros((ROWS16 - count - 2, width), WIDE),
        ],
        0,
    )
    pack_out[chunk:] = small.astype(LOW)
    for copy in copies:
        copy.wait()


def slot_shard(places, slot, same_core):
    return jnp.bitwise_xor(places[1], 2 * slot + (0 if same_core else 1))


def mixer_forward_kernel(
    seqs,
    keys,
    count,
    scalars,
    places,
    tokens,
    mine,
    theirs,
    first_out,
    raw_out,
    gate_out,
    gates_out,
    inverse_out,
    update_out,
    heads_out,
    mixed_out,
    weights,
    mix_row,
    ffn_row,
    gate_rows,
    taps,
    head_gain,
    gate_wide,
):
    size = tokens.shape[0] // seqs
    chips, block = mine.shape[0], mine.shape[1]
    chunk = block - ROWS16
    values = heads_out.shape[1]
    conv_width = 2 * keys + values
    gate_wide[...] = jnp.zeros(gate_wide.shape, WIDE)
    total = None
    for same_core, slots in ((True, mine), (False, theirs)):
        for slot in range(chips):
            shard = slot_shard(places, slot, same_core)
            line = pl.ds(pl.multiple_of(shard * chunk, chunk), chunk)
            weights[line, :] = slots[slot, :chunk, : conv_width + values]
            small = slots[slot, chunk:].astype(WIDE)
            mix_row[:, line] = small[0:1, :chunk]
            ffn_row[:, line] = small[0:1, chunk : 2 * chunk]
            pair = small[0:1, 2 * chunk : 3 * chunk], small[0:1, 3 * chunk : 4 * chunk]
            for row in range(4):
                gate_wide[row : row + 1, line] = pair[row % 2]
            total = small if total is None else total + small
    gate_rows[...] = gate_wide[...].astype(LOW)
    taps[...] = total[1 : count + 1, :conv_width]
    head_gain[...] = total[count + 1 : count + 2, :values]
    wide = tokens[...].astype(WIDE)
    first = (
        wide * lax.rsqrt(jnp.mean(wide * wide, -1, keepdims=True) + EPS) * mix_row[...]
    ).astype(LOW)
    first_out[...] = first
    raw_out[...] = local_dot(first, weights[:, :conv_width])
    gate_out[...] = local_dot(first, weights[:, conv_width:])
    gates_out[...] = right_dot(first, gate_rows[...])
    rows, cols = iotas(size)
    parts = []
    for seq in range(seqs):
        span = slice(seq * size, (seq + 1) * size)
        run, sig = conv_silu(raw_out[span], taps[...])
        query, key, value = unit_features(run * sig, keys)[:3]
        beta, _, _, upto = decay_matrix(gates_out[span], scalars[0], scalars[1])
        system = jnp.where(rows > cols, beta * dot_nt(key, key) * upto, 0.0)
        scores = dot_nt(query, key) * upto
        parts.append((system, scores, beta * value))
    inverses = unit_lower_inverse([p[0] for p in parts])
    for seq in range(seqs):
        span = slice(seq * size, (seq + 1) * size)
        inverse_out[span] = inverses[seq]
        update = dot_nn(inverses[seq], parts[seq][2])
        heads = dot_nn(parts[seq][1], update)
        update_out[span] = update
        heads_out[span] = heads
        gate = gate_out[span]
        normed = heads * lax.rsqrt(jnp.mean(heads * heads, -1, keepdims=True) + EPS)
        mixed_out[span] = (normed * head_gain[...] * (gate * sigmoid(gate))).astype(LOW)


def member(part, steps):
    return jnp.bitwise_xor(part, steps)


def feed_forward_kernel(
    team,
    scalars,
    *refs,
):
    far_out, far = refs[:team], refs[team : team + 3]
    mixed_slots, gain = refs[team + 3 : 2 * team + 3], refs[2 * team + 3]
    (
        mixed_out,
        hidden_out,
        second_grad_out,
        gain_grad_out,
        result_out,
        out_full,
        grads_out,
        hidden,
        up_weights,
        down_weights,
        *near,
        sems,
    ) = refs[2 * team + 4 :]
    fetch = [
        pltpu.make_async_copy(source, target, sems.at[index])
        for index, (source, target) in enumerate(zip((*far_out, *far), near))
    ]
    for copy in fetch:
        copy.start()
    out_slots = near[:team]
    tokens, packs, cotangents = near[team:]
    part = scalars[0]
    size = tokens.shape[0] // team
    values = mixed_slots[0].shape[1]
    outs = out_slots[0].shape[2]
    for steps in range(team):
        place = pl.multiple_of(member(part, steps) * values, values)
        for slot in range(team):
            there = slot ^ steps
            mixed_out[slot * size : (slot + 1) * size, pl.ds(place, values)] = mixed_slots[
                steps
            ][there * size : (there + 1) * size]
    blocks = out_slots[0].shape[0]
    chunk = out_slots[0].shape[1]
    for copy in fetch[: team + 1]:
        copy.wait()
    for steps in range(team):
        place = pl.multiple_of(member(part, steps) * outs, outs)
        for slot in range(blocks):
            chips = blocks // 2
            shard = slot_shard(scalars, slot % chips, slot < chips)
            line = pl.ds(pl.multiple_of(shard * chunk, chunk), chunk)
            out_full[line, pl.ds(place, outs)] = out_slots[steps][slot]
    wide = tokens[...].astype(WIDE) + local_dot(mixed_out[...], out_full[...])
    hidden_out[...] = wide[:size]
    normed = wide * lax.rsqrt(jnp.mean(wide * wide, -1, keepdims=True) + EPS)
    second = (normed * gain[...]).astype(LOW)
    hidden[...] = normed
    fetch[team + 1].wait()
    feed_forward_unpack(packs.shape[0], packs, up_weights, down_weights)
    fetch[team + 2].wait()
    part_width = down_weights.shape[0]
    both = local_dot(second, up_weights[...])
    gate, up = both[:, :part_width], both[:, part_width:]
    gate_sig = sigmoid(gate)
    gate_act = gate * gate_sig
    active = (gate_act * up).astype(LOW)
    result_out[...] = local_dot(active, down_weights[...]).astype(LOW)
    active_grad = right_dot(cotangents[...], down_weights[...])
    gate_back = (active_grad * up * gate_sig * (1.0 + gate * (1.0 - gate_sig))).astype(LOW)
    up_back = (active_grad * gate_act).astype(LOW)
    back = jnp.concatenate([gate_back, up_back], 1)
    second_grad = right_dot(back, up_weights[...])
    second_grad_out[...] = second_grad.astype(LOW)
    gain_grad_out[...] = jnp.sum(second_grad * hidden[...], 0, keepdims=True)
    feed_forward_pack_grads(grads_out.shape[0], second, back, active, cotangents[...], grads_out)


def feed_forward_pack_kernel(team, shards, places, gate_far, up_far, down_far, pack, gate, up, down, sems):
    fetch = [
        pltpu.make_async_copy(far, near, sems.at[index])
        for index, (far, near) in enumerate(((gate_far, gate), (up_far, up), (down_far, down)))
    ]
    for copy in fetch:
        copy.start()
    chunk = gate.shape[0]
    each = down.shape[0] // team
    padded = -(-each // ROWS16) * ROWS16
    ups = 2 * shards * each // LANES
    pad = jnp.zeros((padded - each, LANES), WIDE)
    for copy in fetch:
        copy.wait()

    for choice in range(team):

        @pl.when(places[0] == choice)
        def _():
            starts = [(s * team + choice) * each for s in range(shards)]
            wide = jnp.concatenate(
                [matrix[:, i : i + each].astype(WIDE) for matrix in (gate, up) for i in starts],
                1,
            )
            for index in range(ups):
                pack[index * chunk : (index + 1) * chunk] = wide[
                    :, index * LANES : (index + 1) * LANES
                ].astype(LOW)
            rows = down[...].astype(WIDE)[choice * each : (choice + 1) * each]
            for index in range(rows.shape[1] // LANES):
                start = ups * chunk + index * padded
                block = rows[:, index * LANES : (index + 1) * LANES]
                pack[start : start + padded] = jnp.concatenate([block, pad], 0).astype(LOW)


def feed_forward_unpack(shards, packs, up_out, down_out):
    chunk = up_out.shape[0] // shards
    each = down_out.shape[0] // shards
    padded = -(-each // ROWS16) * ROWS16
    ups = up_out.shape[1] // LANES
    for shard in range(shards):
        for index in range(ups):
            up_out[shard * chunk : (shard + 1) * chunk, index * LANES : (index + 1) * LANES] = (
                packs[shard, index * chunk : (index + 1) * chunk]
            )
    for pair in range(shards // 2):
        for index in range(down_out.shape[1] // LANES):
            start = ups * chunk + index * padded
            block = jnp.concatenate(
                [
                    packs[shard, start : start + padded].astype(WIDE)[:each]
                    for shard in (2 * pair, 2 * pair + 1)
                ],
                0,
            )
            down_out[
                2 * pair * each : 2 * (pair + 1) * each, index * LANES : (index + 1) * LANES
            ] = block.astype(LOW)


def feed_forward_pack_grads(shards, second, back, active, cotangents, pack):
    up_grad = left_dot(second, back)
    down_grad = left_dot(active, cotangents)
    chunk = up_grad.shape[0] // shards
    each = down_grad.shape[0] // shards
    padded = -(-each // ROWS16) * ROWS16
    pad = jnp.zeros((padded - each, LANES), WIDE)
    ups = up_grad.shape[1] // LANES
    for shard in range(shards):
        for index in range(ups):
            pack[shard, index * chunk : (index + 1) * chunk] = up_grad[
                shard * chunk : (shard + 1) * chunk, index * LANES : (index + 1) * LANES
            ].astype(LOW)
        for index in range(down_grad.shape[1] // LANES):
            start = ups * chunk + index * padded
            block = down_grad[
                shard * each : (shard + 1) * each, index * LANES : (index + 1) * LANES
            ]
            pack[shard, start : start + padded] = jnp.concatenate([block, pad], 0).astype(LOW)


def feed_forward_finish_kernel(team, shards, places, *refs):
    *slots, gate_out, up_out, down_out, ordered = refs
    chunk = gate_out.shape[0]
    each = down_out.shape[0] // team
    padded = -(-each // ROWS16) * ROWS16
    half = shards * each
    ups = 2 * half // LANES
    size = slots[0].shape[0]
    for index, slot in enumerate(slots):
        start = index // team * size
        ordered[member(places[0], index % team), start : start + size] = slot[...].astype(LOW)
    wide = [
        jnp.concatenate(
            [ordered[h, i * chunk : (i + 1) * chunk].astype(WIDE) for i in range(ups)], 1
        )
        for h in range(team)
    ]
    for base, out in ((0, gate_out), (half, up_out)):
        out[...] = jnp.concatenate(
            [
                wide[h][:, base + s * each : base + (s + 1) * each]
                for s in range(shards)
                for h in range(team)
            ],
            1,
        )
    for h in range(team):
        for index in range(down_out.shape[1] // LANES):
            start = ups * chunk + index * padded
            down_out[h * each : (h + 1) * each, index * LANES : (index + 1) * LANES] = ordered[
                h, start : start + padded
            ].astype(WIDE)[:each]


def mixer_backward_kernel(
    seqs,
    keys,
    shards,
    scalars,
    places,
    *refs,
):
    branch_slots = refs[:seqs]
    (
        out_full,
        gate_raw,
        heads,
        head_gain,
        first,
        mixed,
        raw,
        gates,
        inverse,
        update,
        taps,
        weights,
        gate_rows,
        tokens,
        ffn_gain_grad,
        pack,
        first_grad_out,
        raw_grad_out,
        gates_grad_out,
        branch_grad,
        heads_grad,
    ) = refs[seqs:]
    values = heads.shape[1]
    outs = out_full.shape[1] // seqs
    for slot in range(seqs):
        rows_each = branch_slots[slot].shape[0]
        branch_grad[slot * rows_each : (slot + 1) * rows_each] = branch_slots[slot][...]
    row = pl.multiple_of(places[0] * values, values)
    mixed_grad = right_dot(branch_grad[...], out_full[pl.ds(row, values)])
    out = heads[...]
    gate = gate_raw[...]
    gain = head_gain[...]
    scale = lax.rsqrt(jnp.mean(out * out, -1, keepdims=True) + EPS)
    normed = out * scale
    gate_sig = sigmoid(gate)
    gate_act = gate * gate_sig
    gate_grad = (
        mixed_grad * normed * gain * gate_sig * (1.0 + gate * (1.0 - gate_sig))
    ).astype(LOW)
    head_gain_grad = jnp.sum(mixed_grad * normed * gate_act, 0, keepdims=True)
    normed_grad = mixed_grad * gain * gate_act
    heads_grad[...] = scale * (
        normed_grad - normed * jnp.mean(normed_grad * normed, -1, keepdims=True)
    )
    place = pl.multiple_of(places[0] * outs, outs)
    gate_wgrad = left_dot(first[...], gate_grad)
    out_wgrad = left_dot(mixed[...], branch_grad[:, pl.ds(place, outs)])
    size = raw.shape[0] // seqs
    conv_width = taps.shape[1]
    count = taps.shape[0]
    part, shard = places[0], places[1]
    rows, cols = iotas(size)
    taps_grad = [jnp.zeros((1, conv_width), WIDE) for _ in range(count)]
    log_total = jnp.zeros((1, 1), WIDE)
    bias_total = jnp.zeros((1, 1), WIDE)
    for seq in range(seqs):
        span = slice(seq * size, (seq + 1) * size)
        out_grad = heads_grad[span]
        raw_in = raw[span]
        run, sig = conv_silu(raw_in, taps[...])
        query, key, value, query_act, query_r, key_act, key_r = unit_features(run * sig, keys)
        beta, decay_in, log_decay, upto = decay_matrix(gates[span], scalars[0], scalars[1])
        key_key = dot_nt(key, key) * upto
        scores = dot_nt(query, key) * upto
        solved = update[span]
        scores_grad = jnp.where(rows >= cols, dot_nt(out_grad, solved), 0.0)
        solved_grad = dot_tn(scores, out_grad)
        target_grad = dot_tn(inverse[span], solved_grad)
        system_grad = jnp.where(rows > cols, -dot_nt(target_grad, solved), 0.0)
        value_grad = beta * target_grad
        system_part = system_grad * key_key
        beta_grad = jnp.sum(target_grad * value, 1, keepdims=True) + jnp.sum(
            system_part, 1, keepdims=True
        )
        key_key_grad = system_grad * (beta * upto)
        scores_part = scores_grad * upto
        spread_grad = system_part * beta + scores_grad * scores
        query_grad = dot_nn(scores_part, key)
        key_grad = (
            dot_tn(scores_part, query) + dot_nn(key_key_grad, key) + dot_tn(key_key_grad, key)
        )
        total_row = jnp.sum(
            jnp.where(rows == cols, jnp.sum(spread_grad, 1, keepdims=True), 0.0),
            0,
            keepdims=True,
        ) - jnp.sum(spread_grad, 0, keepdims=True)
        decay_grad = jnp.sum(jnp.where(cols >= rows, total_row, 0.0), 1, keepdims=True)
        decay_raw_grad = -scalars[0] * decay_grad * sigmoid(decay_in)
        beta_raw_grad = beta_grad * beta * (1.0 - beta)
        log_total = log_total + jnp.sum(decay_grad * log_decay, 0, keepdims=True)
        bias_total = bias_total + jnp.sum(decay_raw_grad, 0, keepdims=True)
        beta_high = beta_raw_grad.astype(LOW).astype(WIDE)
        decay_high = decay_raw_grad.astype(LOW).astype(WIDE)
        lane = lax.broadcasted_iota(jnp.int32, (size, ROWS16), 1)
        gates_grad_out[span] = jnp.where(
            lane == 0,
            beta_high,
            jnp.where(
                lane == 1,
                decay_high,
                jnp.where(
                    lane == 2,
                    beta_raw_grad - beta_high,
                    jnp.where(lane == 3, decay_raw_grad - decay_high, 0.0),
                ),
            ),
        ).astype(LOW)
        query_grad = query_grad * (1.0 / math.sqrt(keys))
        query_unit = query_act * query_r
        query_act_grad = query_r * (
            query_grad - query_unit * jnp.sum(query_unit * query_grad, -1, keepdims=True)
        )
        key_act_grad = key_r * (key_grad - key * jnp.sum(key * key_grad, -1, keepdims=True))
        act_grad = jnp.concatenate([query_act_grad, key_act_grad, value_grad], 1)
        run_grad = act_grad * sig * (1.0 + run * (1.0 - sig))
        raw_grad = run_grad * taps[count - 1 : count]
        taps_grad[count - 1] = taps_grad[count - 1] + jnp.sum(
            run_grad * raw_in, 0, keepdims=True
        )
        for steps in range(1, count):
            tap = count - 1 - steps
            moved = earlier(run_grad, steps)
            raw_grad = raw_grad + moved * taps[tap : tap + 1]
            taps_grad[tap] = taps_grad[tap] + jnp.sum(moved * raw_in, 0, keepdims=True)
        raw_grad_out[span] = raw_grad.astype(LOW)
    width = tokens.shape[1]
    chunk = width // shards
    raw_low = raw_grad_out[...]
    head_wgrad = left_dot(first[...], raw_low)
    gates_rows = left_dot(gates_grad_out[...], first[...])
    first_grad = (
        right_dot(raw_low, weights[:, :conv_width])
        + right_dot(gate_grad, weights[:, conv_width:])
        + local_dot(gates_grad_out[...], gate_rows[...])
    )
    first_grad_out[...] = first_grad.astype(LOW)
    wide = tokens[...].astype(WIDE)
    normed = wide * lax.rsqrt(jnp.mean(wide * wide, -1, keepdims=True) + EPS)
    gain_grad = jnp.sum(first_grad * normed, 0, keepdims=True)
    beta_row = gates_rows[0:1] + gates_rows[2:3]
    decay_row = gates_rows[1:2] + gates_rows[3:4]
    head_shards = shards // seqs
    key_each = keys // head_shards
    value_each = (conv_width - 2 * keys) // head_shards
    head_each = head_gain_grad.shape[1] // shards
    all_taps = jnp.concatenate(taps_grad, 0)
    lane = lax.broadcasted_iota(jnp.int32, (1, conv_width), 1)
    decay_terms = jnp.zeros((1, conv_width), WIDE)
    for which, total in enumerate((log_total, bias_total)):
        for piece in range(3):
            high = total.astype(LOW).astype(WIDE)
            place = head_each + (which * 3 + piece) * shards + shard
            decay_terms = jnp.where(lane == place, high, decay_terms)
            total = total - high
    blocks = []
    for s in range(shards):
        line = slice(s * chunk, (s + 1) * chunk)
        i = s % head_shards
        gains = jnp.concatenate(
            [beta_row[:, line], decay_row[:, line], gain_grad[:, line], ffn_gain_grad[:, line]], 1
        )
        tap_rows = jnp.concatenate(
            [
                all_taps[:, i * key_each : (i + 1) * key_each],
                all_taps[:, keys + i * key_each : keys + (i + 1) * key_each],
                all_taps[:, 2 * keys + i * value_each : 2 * keys + (i + 1) * value_each],
            ],
            1,
        )
        tap_rows = jnp.where(part == s // head_shards, tap_rows, 0.0)
        tap_rows = jnp.concatenate(
            [tap_rows, jnp.zeros((count, conv_width - tap_rows.shape[1]), WIDE)], 1
        )
        head_row = jnp.concatenate(
            [
                head_gain_grad[:, s * head_each : (s + 1) * head_each],
                jnp.zeros((1, conv_width - head_each), WIDE),
            ],
            1,
        )
        small = jnp.concatenate(
            [
                gains,
                tap_rows,
                head_row + decay_terms,
                jnp.zeros((ROWS16 - count - 2, conv_width), WIDE),
            ],
            0,
        )
        empty = jnp.zeros((ROWS16, values + outs), WIDE)
        blocks.append(
            (
                head_wgrad[line],
                gate_wgrad[line],
                out_wgrad[line],
                jnp.concatenate([small, empty], 1),
            )
        )
    top, all_lanes = slice(0, chunk), slice(0, conv_width + values + outs)
    spots = (
        (top, slice(0, conv_width)),
        (top, slice(conv_width, conv_width + values)),
        (top, slice(conv_width + values, conv_width + values + outs)),
        (slice(chunk, chunk + ROWS16), all_lanes),
    )
    for s in range(shards):
        for block, (line, lanes) in zip(blocks[s], spots):
            pack[s, line, lanes] = block.astype(LOW)


def finish_kernel(
    team,
    keys,
    shards,
    count,
    scalars,
    *refs,
):
    slots = refs[:team]
    (
        query_out,
        key_out,
        value_out,
        gate_out,
        proj_out,
        beta_out,
        decay_out,
        mix_out,
        ffn_out,
        query_conv_out,
        key_conv_out,
        value_conv_out,
        head_out,
        log_out,
        bias_out,
        pair,
    ) = refs[team:]
    part = scalars[0]
    chunk = query_out.shape[0]
    values = value_out.shape[1] // team
    conv_width = 2 * keys + values
    key_each = query_conv_out.shape[1]
    conv_each = 2 * key_each + value_conv_out.shape[1]
    head_each = head_out.shape[1]
    total = None
    lane = lax.broadcasted_iota(jnp.int32, (1, LANES), 1)
    log_row = jnp.zeros((1, LANES), WIDE)
    bias_row = jnp.zeros((1, LANES), WIDE)
    pair[...] = jnp.zeros(pair.shape, WIDE)
    for steps in range(team):
        head = member(part, steps)
        key_place = pl.ds(pl.multiple_of(head * keys, keys), keys)
        value_place = pl.ds(pl.multiple_of(head * values, values), values)
        block = slots[steps]
        query_out[:, key_place] = block[:chunk, :keys].astype(WIDE)
        key_out[:, key_place] = block[:chunk, keys : 2 * keys].astype(WIDE)
        value_out[:, value_place] = block[:chunk, 2 * keys : conv_width].astype(WIDE)
        gate_out[:, value_place] = block[:chunk, conv_width : conv_width + values].astype(WIDE)
        proj_out[:, value_place] = block[:chunk, conv_width + values :].astype(WIDE)
        small = block[chunk:, :conv_width].astype(WIDE)
        total = small if total is None else total + small
        pair[pl.ds(head, 1), :] = small[0:1, :chunk]
        pair[pl.ds(head + team, 1), :] = small[0:1, chunk : 2 * chunk]
        terms = small[count + 1 : count + 2]
        wide_lane = lax.broadcasted_iota(jnp.int32, (1, conv_width), 1)
        ends = [head_each + 3 * shards * k for k in range(3)]
        log_sum = jnp.sum(
            jnp.where((wide_lane >= ends[0]) & (wide_lane < ends[1]), terms, 0.0),
            1,
            keepdims=True,
        )
        bias_sum = jnp.sum(
            jnp.where((wide_lane >= ends[1]) & (wide_lane < ends[2]), terms, 0.0),
            1,
            keepdims=True,
        )
        log_row = jnp.where(lane == head, log_sum, log_row)
        bias_row = jnp.where(lane == head, bias_sum, bias_row)
    beta_out[...] = pair[:team]
    decay_out[...] = pair[team : 2 * team]
    mix_out[...] = total[0:1, 2 * chunk : 3 * chunk]
    ffn_out[...] = total[0:1, 3 * chunk : 4 * chunk]
    query_conv_out[...] = total[1 : count + 1, :key_each]
    key_conv_out[...] = total[1 : count + 1, key_each : 2 * key_each]
    value_conv_out[...] = total[1 : count + 1, 2 * key_each : conv_each]
    head_out[...] = total[count + 1 : count + 2, :head_each]
    log_out[...] = log_row[:, :team]
    bias_out[...] = bias_row[:, :team]


def array(shape, dtype):
    return jax.ShapeDtypeStruct(shape, dtype)


def run_kernel(kernel, name, scalars, operands, outs, flops, scratch=(), far=0):
    spec = pl.BlockSpec(memory_space=pltpu.VMEM)
    moved = sum(math.prod(v.shape) * v.dtype.itemsize for v in (*operands, *outs))
    return pl.pallas_call(
        kernel,
        out_shape=tuple(outs),
        in_specs=[pl.BlockSpec(memory_space=pltpu.SMEM)] * len(scalars)
        + [pl.BlockSpec(memory_space=pl.ANY)] * far
        + [spec] * (len(operands) - far),
        out_specs=[spec] * len(outs),
        scratch_shapes=list(scratch),
        compiler_params=pltpu.CompilerParams(vmem_limit_bytes=(60 if far else 48) * 1024 * 1024),
        cost_estimate=pl.CostEstimate(flops=flops, bytes_accessed=moved, transcendentals=0),
        name=name,
    )(*scalars, *operands)


def team_pairs(devices, steps):
    return [(j, j ^ steps) for j in range(devices)]


def team_gather(block, devices, team):
    return [block] + [
        lax.ppermute(block, "rep", team_pairs(devices, steps)) for steps in range(1, team)
    ]


def swap(block, name, size, mask):
    return lax.ppermute(block, name, [(j, j ^ mask) for j in range(size)])


def line_gather(block, shards):
    return [block] + [
        swap(block, "shard", shards, 2 * steps) for steps in range(1, shards // 2)
    ]


def team_halves(block, devices):
    half = block.shape[0] // 2
    found = []
    for part, (near, far) in ((block[:half], (1, 2)), (block[half:], (2, 1))):
        pair = swap(part, "rep", devices, near)
        quad = swap(both_ends(part, pair), "rep", devices, far)
        held = {0: part, near: pair, far: quad[:half], near | far: quad[half:]}
        found.append([held[e] for e in range(4)])
    return found[0] + found[1]


def both_ends(block, moved):
    return jnp.concatenate([block, moved], 0)


def team_send(slots, devices, team):
    return [slots[0]] + [
        lax.ppermute(slots[steps], "rep", team_pairs(devices, steps)) for steps in range(1, team)
    ]


def wide_sum(blocks):
    total = blocks[0].astype(WIDE)
    for block in blocks[1:]:
        total = total + block.astype(WIDE)
    return total


def norm_scale(v):
    return lax.rsqrt(jnp.mean(v * v, -1, keepdims=True) + EPS)


def replica_slots(block, part, devices, team):
    if devices == team:
        return team_gather(block, devices, team)
    blocks = lax.all_gather(block, "rep").astype(WIDE)
    blocks = jnp.sum(blocks.reshape((devices // team, team) + block.shape), 0)
    return [
        lax.dynamic_index_in_dim(blocks, part ^ e, 0, keepdims=False)
        for e in range(team)
    ]


def after(values, first):
    return lax.optimization_barrier((values, first))[0]


def body(
    inputs,
    cotangent,
    mix_gain,
    query_proj,
    key_proj,
    value_proj,
    beta_proj,
    decay_proj,
    gate_proj,
    query_conv,
    key_conv,
    value_conv,
    decay_log,
    decay_bias,
    head_gain,
    out_proj,
    ffn_gain,
    ffn_gate,
    ffn_up,
    ffn_down,
):
    devices = lax.axis_size("rep")
    shards = lax.axis_size("shard")
    team = beta_proj.shape[1]
    part = lax.axis_index("rep") % team
    shard = lax.axis_index("shard")
    places = jnp.stack([part, shard]).astype(jnp.int32)
    tokens_each, width = inputs.shape
    count = team * tokens_each
    chunk = mix_gain.shape[0]
    keys = query_proj.shape[1] // team
    values = value_proj.shape[1] // team
    outs = out_proj.shape[1] // team
    conv_width = 2 * keys + values
    hidden_each = ffn_down.shape[0] // team
    hidden_part = hidden_each * shards
    taps_count = query_conv.shape[0]
    key_each, value_each = query_conv.shape[1], value_conv.shape[1]
    head_each = head_gain.shape[0]

    padded = -(-hidden_each // ROWS16) * ROWS16
    ffn_rows = 2 * hidden_part * chunk // LANES + padded * (width // LANES)

    mixer_pack = run_kernel(
        functools.partial(pack_kernel, team),
        "pack",
        (places,),
        (
            query_proj,
            key_proj,
            value_proj,
            gate_proj,
            out_proj,
            beta_proj.T,
            decay_proj.T,
            mix_gain[None],
            ffn_gain[None],
            query_conv,
            key_conv,
            value_conv,
            head_gain[None],
        ),
        (
            array((chunk + ROWS16, conv_width + values + outs), LOW),
        ),
        10**8,
        (pltpu.SemaphoreType.DMA((5,)),),
        5,
    )[0]
    pack_slots = line_gather(mixer_pack, shards)
    token_pair = swap(inputs, "rep", devices, 1)
    cotangent_pair = swap(cotangent, "rep", devices, 2)
    token_pair = both_ends(inputs, token_pair)
    cotangent_pair = both_ends(cotangent, cotangent_pair)
    token_quad = swap(token_pair, "rep", devices, 2)
    cotangent_quad = swap(cotangent_pair, "rep", devices, 1)
    pack_slots = after(pack_slots, (token_quad, cotangent_quad))
    ffn_pack = run_kernel(
        functools.partial(feed_forward_pack_kernel, team, shards),
        "feed_forward_pack",
        (places,),
        (after(ffn_gate, pack_slots), ffn_up, ffn_down),
        (array((ffn_rows, LANES), LOW),),
        10**8,
        (
            pltpu.VMEM(ffn_gate.shape, LOW),
            pltpu.VMEM(ffn_up.shape, LOW),
            pltpu.VMEM(ffn_down.shape, LOW),
            pltpu.SemaphoreType.DMA((3,)),
        ),
        3,
    )[0]
    ffn_packs = lax.all_gather(ffn_pack, "shard", axis=0)
    pack_mine = jnp.stack(pack_slots)
    pack_theirs = swap(pack_mine, "shard", shards, 1)
    tokens = both_ends(token_pair, token_quad)
    cotangents = jnp.concatenate(
        [
            cotangent,
            cotangent_quad[:tokens_each],
            cotangent_pair[tokens_each:],
            cotangent_quad[tokens_each:],
        ],
        0,
    )
    scalars = jnp.stack(
        [
            jnp.exp(lax.dynamic_index_in_dim(decay_log, part, 0, keepdims=False)),
            lax.dynamic_index_in_dim(decay_bias, part, 0, keepdims=False),
        ]
    )

    (
        first,
        raw,
        gate_raw,
        gates,
        inverse,
        update,
        heads,
        mixed_part,
        head_weights,
        mix_row,
        ffn_row,
        gate_rows,
        taps,
        head_row,
    ) = run_kernel(
        functools.partial(mixer_forward_kernel, team, keys, taps_count),
        "mixer_forward",
        (scalars, places),
        (tokens, pack_mine, pack_theirs),
        (
            array((count, width), LOW),
            array((count, conv_width), WIDE),
            array((count, values), WIDE),
            array((count, ROWS16), WIDE),
            array((count, tokens_each), WIDE),
            array((count, values), WIDE),
            array((count, values), WIDE),
            array((count, values), LOW),
            array((width, conv_width + values), LOW),
            array((1, width), WIDE),
            array((1, width), WIDE),
            array((ROWS16, width), LOW),
            array((taps_count, conv_width), WIDE),
            array((1, values), WIDE),
        ),
        8 * 10**9,
        (pltpu.VMEM((ROWS16, width), WIDE),),
    )
    mixed_slots = team_gather(mixed_part, devices, team)
    proj_all = both_ends(
        pack_mine[:, :chunk, conv_width + values :],
        pack_theirs[:, :chunk, conv_width + values :],
    )
    proj_all = after(proj_all, mixed_part)
    proj_slots = team_gather(proj_all, devices, team)

    (
        mixed,
        hidden_own,
        second_part,
        ffn_gain_part,
        result_part,
        out_full,
        ffn_grads,
    ) = run_kernel(
        functools.partial(feed_forward_kernel, team),
        "feed_forward",
        (places,),
        (*proj_slots, tokens, ffn_packs, cotangents, *mixed_slots, ffn_row),
        (
            array((count, width), LOW),
            array((tokens_each, width), WIDE),
            array((count, width), LOW),
            array((1, width), WIDE),
            array((count, width), LOW),
            array((width, width), LOW),
            array((shards, ffn_rows, LANES), LOW),
        ),
        16 * 10**9,
        (
            pltpu.VMEM((count, width), WIDE),
            pltpu.VMEM((width, 2 * hidden_part), LOW),
            pltpu.VMEM((hidden_part, width), LOW),
            *(pltpu.VMEM(slot.shape, LOW) for slot in proj_slots),
            pltpu.VMEM(tokens.shape, LOW),
            pltpu.VMEM(ffn_packs.shape, LOW),
            pltpu.VMEM(cotangents.shape, LOW),
            pltpu.SemaphoreType.DMA((team + 3,)),
        ),
        team + 3,
    )

    def slots_of(v):
        return [v[e * tokens_each : (e + 1) * tokens_each] for e in range(team)]

    second_slots = team_send(slots_of(second_part), devices, team)
    ffn_shard = lax.psum_scatter(ffn_grads, "shard", scatter_dimension=0)
    second_grad = wide_sum(second_slots)
    scale_own = norm_scale(hidden_own)
    weighted = second_grad * ffn_row
    hidden_grad = cotangent.astype(WIDE) + scale_own * (
        weighted
        - hidden_own
        * (scale_own * scale_own * jnp.mean(hidden_own * weighted, -1, keepdims=True))
    )
    branch_slots = team_gather(hidden_grad.astype(LOW), devices, team)


    head_grads, first_part = run_kernel(
        functools.partial(mixer_backward_kernel, team, keys, shards),
        "mixer_backward",
        (scalars, places),
        (
            *branch_slots,
            out_full,
            gate_raw,
            heads,
            head_row,
            first,
            mixed,
            raw,
            gates,
            inverse,
            update,
            taps,
            head_weights,
            gate_rows,
            tokens,
            ffn_gain_part,
        ),
        (
            array((shards, chunk + ROWS16, conv_width + values + outs), LOW),
            array((count, width), LOW),
        ),
        10 * 10**9,
        (
            pltpu.VMEM((count, conv_width), LOW),
            pltpu.VMEM((count, ROWS16), LOW),
            pltpu.VMEM((count, width), LOW),
            pltpu.VMEM((count, values), WIDE),
        ),
    )
    head_shard = lax.psum_scatter(head_grads, "shard", scatter_dimension=0)
    last_slots = [
        jnp.concatenate(pair, 0) for pair in zip(slots_of(first_part), slots_of(result_part))
    ]
    last_slots = team_send(last_slots, devices, team)
    if devices == team == 4:
        ffn_totals = team_halves(ffn_shard, devices)
    else:
        ffn_totals = replica_slots(ffn_shard, part, devices, team)
    last = wide_sum(after(last_slots, ffn_totals))
    first_grad = last[:tokens_each]
    seq_in = inputs.astype(WIDE)
    seq_scale = norm_scale(seq_in)
    weighted = first_grad * mix_row
    inputs_grad = hidden_grad + seq_scale * (
        weighted
        - seq_in * (seq_scale * seq_scale * jnp.mean(seq_in * weighted, -1, keepdims=True))
    )
    result = hidden_own + last[tokens_each:]

    head_totals = replica_slots(after(head_shard, ffn_totals), part, devices, team)
    gate_grads, up_grads, down_grads = run_kernel(
        functools.partial(feed_forward_finish_kernel, team, shards),
        "feed_forward_finish",
        (places,),
        ffn_totals,
        (
            array(ffn_gate.shape, WIDE),
            array(ffn_up.shape, WIDE),
            array(ffn_down.shape, WIDE),
        ),
        10**8,
        (pltpu.VMEM((team, ffn_rows, LANES), LOW),),
    )
    (
        query_total,
        key_total,
        value_total,
        gate_total,
        out_total,
        beta_total,
        decay_total,
        mix_total,
        ffn_total,
        query_conv_total,
        key_conv_total,
        value_conv_total,
        head_total,
        log_total,
        bias_total,
    ) = run_kernel(
        functools.partial(finish_kernel, team, keys, shards, taps_count),
        "finish",
        (places,),
        head_totals,
        (
            array((chunk, team * keys), WIDE),
            array((chunk, team * keys), WIDE),
            array((chunk, team * values), WIDE),
            array((chunk, team * values), WIDE),
            array((chunk, team * outs), WIDE),
            array((team, chunk), WIDE),
            array((team, chunk), WIDE),
            array((1, chunk), WIDE),
            array((1, chunk), WIDE),
            array((taps_count, key_each), WIDE),
            array((taps_count, key_each), WIDE),
            array((taps_count, value_each), WIDE),
            array((1, head_each), WIDE),
            array((1, team), WIDE),
            array((1, team), WIDE),
        ),
        10**8,
        (pltpu.VMEM((max(8, 2 * team), chunk), WIDE),),
    )
    return (
        result.astype(LOW),
        inputs_grad,
        mix_total[0],
        query_total,
        key_total,
        value_total,
        beta_total.T,
        decay_total.T,
        gate_total,
        query_conv_total,
        key_conv_total,
        value_conv_total,
        log_total[0],
        bias_total[0],
        head_total[0],
        out_total,
        ffn_total[0],
        gate_grads,
        up_grads,
        down_grads,
    )


def solution(mesh):
    rows = P("shard", None)
    return jax.shard_map(
        body,
        mesh=mesh,
        in_specs=(
            P(("rep", "shard"), None),
            P(("rep", "shard"), None),
            P("shard"),
            rows,
            rows,
            rows,
            rows,
            rows,
            rows,
            P(None, "shard"),
            P(None, "shard"),
            P(None, "shard"),
            P(),
            P(),
            P("shard"),
            rows,
            P("shard"),
            rows,
            rows,
            rows,
        ),
        out_specs=(
            P(("rep", "shard"), None),
            P(("rep", "shard"), None),
            P("shard"),
            rows,
            rows,
            rows,
            rows,
            rows,
            rows,
            P(None, "shard"),
            P(None, "shard"),
            P(None, "shard"),
            P(),
            P(),
            P("shard"),
            rows,
            P("shard"),
            rows,
            rows,
            rows,
        ),
        check_vma=False,
    )
```

```python
import functools
import math

import jax
import jax.numpy as jnp
from jax import lax
from jax.experimental import pallas as pl
from jax.experimental.pallas import tpu as pltpu
from jax.sharding import PartitionSpec as P

EPS = 1e-06
HIGH = lax.Precision.HIGHEST
LOW = jnp.bfloat16
WIDE = jnp.float32
LANES = 128
ROWS16 = 16


def local_dot(left, right):
    return jnp.dot(left, right, preferred_element_type=WIDE)


def left_dot(left, right):
    return lax.dot_general(left, right, (((0,), (0,)), ((), ())), preferred_element_type=WIDE)


def right_dot(left, right):
    return lax.dot_general(left, right, (((1,), (1,)), ((), ())), preferred_element_type=WIDE)


def dot_nn(left, right):
    return jnp.dot(left, right, preferred_element_type=WIDE, precision=HIGH)


def dot_nt(left, right):
    return lax.dot_general(
        left, right, (((1,), (1,)), ((), ())), preferred_element_type=WIDE, precision=HIGH
    )


def dot_tn(left, right):
    return lax.dot_general(
        left, right, (((0,), (0,)), ((), ())), preferred_element_type=WIDE, precision=HIGH
    )


def sigmoid(v):
    return 1.0 / (1.0 + jnp.exp(-v))


def iotas(size):
    return (
        lax.broadcasted_iota(jnp.int32, (size, size), 0),
        lax.broadcasted_iota(jnp.int32, (size, size), 1),
    )


def later(v, steps):
    rows = lax.broadcasted_iota(jnp.int32, v.shape, 0)
    return jnp.where(rows >= steps, pltpu.roll(v, steps, 0), 0.0)


def earlier(v, steps):
    rows = lax.broadcasted_iota(jnp.int32, v.shape, 0)
    return jnp.where(rows < v.shape[0] - steps, pltpu.roll(v, v.shape[0] - steps, 0), 0.0)


def conv_silu(raw, taps):
    count = taps.shape[0]
    run = raw * taps[count - 1 : count]
    for steps in range(1, count):
        run = run + later(raw, steps) * taps[count - 1 - steps : count - steps]
    sig = sigmoid(run)
    return run, sig


def unit_features(act, keys):
    query_act, key_act, value = act[:, :keys], act[:, keys : 2 * keys], act[:, 2 * keys :]
    query_r = lax.rsqrt(jnp.sum(query_act * query_act, -1, keepdims=True) + EPS)
    key_r = lax.rsqrt(jnp.sum(key_act * key_act, -1, keepdims=True) + EPS)
    query = query_act * query_r * (1.0 / math.sqrt(keys))
    return query, key_act * key_r, value, query_act, query_r, key_act, key_r


def softplus(v):
    return jnp.maximum(v, 0.0) + jnp.log1p(jnp.exp(-jnp.abs(v)))


def decay_matrix(gates, decay, bias):
    size = gates.shape[0]
    rows, cols = iotas(size)
    beta = sigmoid(gates[:, 0:1])
    decay_in = gates[:, 1:2] + bias
    log_decay = -decay * softplus(decay_in)
    decay_row = jnp.sum(jnp.where(rows == cols, log_decay, 0.0), 0, keepdims=True)
    total_col = jnp.sum(jnp.where(cols <= rows, decay_row, 0.0), 1, keepdims=True)
    total_row = jnp.sum(jnp.where(rows <= cols, log_decay, 0.0), 0, keepdims=True)
    spread = jnp.where(rows >= cols, total_col - total_row, 0.0)
    upto = jnp.where(rows >= cols, jnp.exp(spread), 0.0)
    return beta, decay_in, log_decay, upto


def unit_lower_inverse(systems):
    size = systems[0].shape[0]
    rows, cols = iotas(size)
    block = 8
    near = [jnp.where(rows // block == cols // block, a, 0.0) for a in systems]
    eye = jnp.where(rows == cols, 1.0, 0.0)
    power = [dot_nn(a, a) for a in near]
    inverse = [eye - a for a in near]
    inverse = [x + dot_nn(x, p) for x, p in zip(inverse, power)]
    power = [dot_nn(p, p) for p in power]
    inverse = [x + dot_nn(x, p) for x, p in zip(inverse, power)]
    while block < size:
        cross = (rows // (2 * block) == cols // (2 * block)) & (rows // block != cols // block)
        middle = [dot_nn(jnp.where(cross, a, 0.0), x) for a, x in zip(systems, inverse)]
        inverse = [x - dot_nn(x, m) for x, m in zip(inverse, middle)]
        block *= 2
    return inverse


def pack_kernel(
    team,
    places,
    query,
    key,
    value,
    gate,
    proj,
    beta,
    decay,
    mix_gain,
    ffn_gain,
    query_conv,
    key_conv,
    value_conv,
    head_gain,
    pack_out,
    sems,
):
    part, shard = places[0], places[1]
    chunk = query.shape[0]
    keys, values = query.shape[1] // team, value.shape[1] // team
    outs = proj.shape[1] // team
    width = pack_out.shape[1]
    count = query_conv.shape[0]
    head_each = head_gain.shape[1]
    copies = []
    start = 0
    for index, (matrix, size) in enumerate(
        ((query, keys), (key, keys), (value, values), (gate, values), (proj, outs))
    ):
        source = matrix.at[:, pl.ds(pl.multiple_of(part * size, size), size)]
        target = pack_out.at[:chunk, start : start + size]
        start += size
        copies.append(pltpu.make_async_copy(source, target, sems.at[index]))
    for copy in copies:
        copy.start()

    def head_row(matrix):
        line = lax.broadcasted_iota(jnp.int32, matrix.shape, 0)
        return jnp.sum(jnp.where(line == part, matrix[...].astype(WIDE), 0.0), 0, keepdims=True)

    gains = [mix_gain[...].astype(WIDE), ffn_gain[...].astype(WIDE)]
    gains += [head_row(beta), head_row(decay)]
    gains.append(jnp.zeros((1, width - 4 * chunk), WIDE))
    pieces = []
    for taps, size in ((query_conv, keys), (key_conv, keys), (value_conv, values)):
        wide = taps[...].astype(WIDE)
        pieces.append(jnp.concatenate([wide] * (size // wide.shape[1]), 1))
    pieces = jnp.concatenate(pieces, 1)
    lane = lax.broadcasted_iota(jnp.int32, pieces.shape, 1)
    inside = jnp.where(lane < 2 * keys, lane % keys // query_conv.shape[1], 0)
    inside = jnp.where(lane < 2 * keys, inside, (lane - 2 * keys) // value_conv.shape[1])
    owners = keys // query_conv.shape[1]
    pieces = jnp.where(inside + part * owners == shard, pieces, 0.0)
    taps_rows = jnp.concatenate(
        [pieces, jnp.zeros((count, width - pieces.shape[1]), WIDE)], 1
    )
    head = jnp.concatenate([head_gain[...].astype(WIDE)] * (values // head_each), 1)
    lane = lax.broadcasted_iota(jnp.int32, head.shape, 1)
    head = jnp.where(lane // head_each == shard, head, 0.0)
    head = jnp.concatenate([head, jnp.zeros((1, width - values), WIDE)], 1)
    small = jnp.concatenate(
        [
            jnp.concatenate(gains, 1),
            taps_rows,
            head,
            jnp.zeros((ROWS16 - count - 2, width), WIDE),
        ],
        0,
    )
    pack_out[chunk:] = small.astype(LOW)
    for copy in copies:
        copy.wait()


def slot_shard(places, slot, same_core):
    return jnp.bitwise_xor(places[1], 2 * slot + (0 if same_core else 1))


def mixer_forward_kernel(
    seqs,
    keys,
    count,
    scalars,
    places,
    tokens,
    mine,
    theirs,
    first_out,
    raw_out,
    gate_out,
    gates_out,
    inverse_out,
    update_out,
    heads_out,
    mixed_out,
    weights,
    mix_row,
    ffn_row,
    gate_rows,
    taps,
    head_gain,
    gate_wide,
):
    size = tokens.shape[0] // seqs
    chips, block = mine.shape[0], mine.shape[1]
    chunk = block - ROWS16
    values = heads_out.shape[1]
    conv_width = 2 * keys + values
    gate_wide[...] = jnp.zeros(gate_wide.shape, WIDE)
    total = None
    for same_core, slots in ((True, mine), (False, theirs)):
        for slot in range(chips):
            shard = slot_shard(places, slot, same_core)
            line = pl.ds(pl.multiple_of(shard * chunk, chunk), chunk)
            weights[line, :] = slots[slot, :chunk, : conv_width + values]
            small = slots[slot, chunk:].astype(WIDE)
            mix_row[:, line] = small[0:1, :chunk]
            ffn_row[:, line] = small[0:1, chunk : 2 * chunk]
            pair = small[0:1, 2 * chunk : 3 * chunk], small[0:1, 3 * chunk : 4 * chunk]
            for row in range(4):
                gate_wide[row : row + 1, line] = pair[row % 2]
            total = small if total is None else total + small
    gate_rows[...] = gate_wide[...].astype(LOW)
    taps[...] = total[1 : count + 1, :conv_width]
    head_gain[...] = total[count + 1 : count + 2, :values]
    wide = tokens[...].astype(WIDE)
    first = (
        wide * lax.rsqrt(jnp.mean(wide * wide, -1, keepdims=True) + EPS) * mix_row[...]
    ).astype(LOW)
    first_out[...] = first
    raw_out[...] = local_dot(first, weights[:, :conv_width])
    gate_out[...] = local_dot(first, weights[:, conv_width:])
    gates_out[...] = right_dot(first, gate_rows[...])
    rows, cols = iotas(size)
    parts = []
    for seq in range(seqs):
        span = slice(seq * size, (seq + 1) * size)
        run, sig = conv_silu(raw_out[span], taps[...])
        query, key, value = unit_features(run * sig, keys)[:3]
        beta, _, _, upto = decay_matrix(gates_out[span], scalars[0], scalars[1])
        system = jnp.where(rows > cols, beta * dot_nt(key, key) * upto, 0.0)
        scores = dot_nt(query, key) * upto
        parts.append((system, scores, beta * value))
    inverses = unit_lower_inverse([p[0] for p in parts])
    for seq in range(seqs):
        span = slice(seq * size, (seq + 1) * size)
        inverse_out[span] = inverses[seq]
        update = dot_nn(inverses[seq], parts[seq][2])
        heads = dot_nn(parts[seq][1], update)
        update_out[span] = update
        heads_out[span] = heads
        gate = gate_out[span]
        normed = heads * lax.rsqrt(jnp.mean(heads * heads, -1, keepdims=True) + EPS)
        mixed_out[span] = (normed * head_gain[...] * (gate * sigmoid(gate))).astype(LOW)


def member(part, steps):
    return jnp.bitwise_xor(part, steps)


def feed_forward_kernel(
    team,
    scalars,
    *refs,
):
    outs_count = team
    far = refs[: outs_count + 3]
    refs = refs[outs_count + 3 :]
    mixed_slots, gain = refs[:team], refs[team]
    far_outs, gain_grad_out = refs[team + 1 : team + 7], refs[team + 7]
    (
        mixed,
        out_full,
        result,
        second_grad_low,
        grads,
        hidden,
        up_weights,
        down_weights,
        *near,
        sems,
        out_sems,
    ) = refs[team + 8 :]
    mixed_out, hidden_out, second_grad_out, result_out, out_rows_out, grads_out = far_outs
    fetch = [
        pltpu.make_async_copy(source, target, sems.at[index])
        for index, (source, target) in enumerate(zip(far, near))
    ]
    for copy in fetch:
        copy.start()
    sent = []

    def send(source, target):
        copy = pltpu.make_async_copy(source, target, out_sems.at[len(sent)])
        copy.start()
        sent.append(copy)

    out_slots = near[:outs_count]
    tokens, packs, cotangents = near[outs_count:]
    part = scalars[0]
    size = tokens.shape[0] // team
    values = mixed_slots[0].shape[1]
    outs = out_slots[0].shape[2]
    for steps in range(team):
        place = pl.multiple_of(member(part, steps) * values, values)
        for slot in range(team):
            there = slot ^ steps
            mixed[slot * size : (slot + 1) * size, pl.ds(place, values)] = mixed_slots[steps][
                there * size : (there + 1) * size
            ]
    send(mixed, mixed_out)
    chips, chunk = out_slots[0].shape[0] // 2, out_slots[0].shape[1]
    for copy in fetch[: outs_count + 1]:
        copy.wait()
    for index in range(outs_count):
        place = pl.multiple_of(member(part, index) * outs, outs)
        for slot in range(2 * chips):
            shard = slot_shard(scalars, slot % chips, slot < chips)
            line = pl.ds(pl.multiple_of(shard * chunk, chunk), chunk)
            out_full[line, pl.ds(place, outs)] = out_slots[index][slot]
    row = pl.multiple_of(part * values, values)
    send(out_full.at[pl.ds(row, values)], out_rows_out)
    hidden[...] = tokens[...].astype(WIDE) + local_dot(mixed[...], out_full[...])
    send(hidden.at[:size], hidden_out)
    wide = hidden[...]
    normed = wide * lax.rsqrt(jnp.mean(wide * wide, -1, keepdims=True) + EPS)
    second = (normed * gain[...]).astype(LOW)
    fetch[outs_count + 1].wait()
    feed_forward_unpack(packs.shape[0], packs, up_weights, down_weights)
    fetch[outs_count + 2].wait()
    part_width = down_weights.shape[0]
    both = local_dot(second, up_weights[...])
    gate, up = both[:, :part_width], both[:, part_width:]
    gate_sig = sigmoid(gate)
    gate_act = gate * gate_sig
    active = (gate_act * up).astype(LOW)
    result[...] = local_dot(active, down_weights[...]).astype(LOW)
    send(result, result_out)
    active_grad = right_dot(cotangents[...], down_weights[...])
    gate_back = (active_grad * up * gate_sig * (1.0 + gate * (1.0 - gate_sig))).astype(LOW)
    up_back = (active_grad * gate_act).astype(LOW)
    back = jnp.concatenate([gate_back, up_back], 1)
    second_grad = right_dot(back, up_weights[...])
    second_grad_low[...] = second_grad.astype(LOW)
    send(second_grad_low, second_grad_out)
    wide = hidden[...]
    normed = wide * lax.rsqrt(jnp.mean(wide * wide, -1, keepdims=True) + EPS)
    gain_grad_out[...] = jnp.sum(second_grad * normed, 0, keepdims=True)
    shards = grads.shape[0]
    chunk = out_full.shape[0] // shards
    each = part_width // shards
    ups = back.shape[1] // LANES
    down_grad = left_dot(active, cotangents[...])
    for shard in range(shards):
        for index in range(down_grad.shape[1] // (2 * LANES)):
            start = ups * chunk + 2 * index * each
            grads[shard, start : start + 2 * each] = on_end(
                down_grad[shard * each : (shard + 1) * each], index
            ).astype(LOW)
    half = shards // 2
    for first_shard in (0, half):
        line = slice(first_shard * chunk, (first_shard + half) * chunk)
        up_grad = left_dot(second[:, line], back)
        for shard in range(half):
            for index in range(ups):
                grads[first_shard + shard, index * chunk : (index + 1) * chunk] = up_grad[
                    shard * chunk : (shard + 1) * chunk, index * LANES : (index + 1) * LANES
                ].astype(LOW)
        place = pl.ds(first_shard, half)
        send(grads.at[place], grads_out.at[place])
    for copy in sent:
        copy.wait()


def on_end(rows, index):
    start = 2 * index * LANES
    return jnp.concatenate(
        [rows[:, start : start + LANES], rows[:, start + LANES : start + 2 * LANES]], 0
    )


def feed_forward_pack_kernel(team, shards, places, gate_far, up_far, down_far, pack, gate, up, down, sems):
    fetch = [
        pltpu.make_async_copy(far, near, sems.at[index])
        for index, (far, near) in enumerate(((gate_far, gate), (up_far, up), (down_far, down)))
    ]
    for copy in fetch:
        copy.start()
    chunk = gate.shape[0]
    each = down.shape[0] // team
    ups = 2 * shards * each // LANES
    for copy in fetch:
        copy.wait()

    for choice in range(team):

        @pl.when(places[0] == choice)
        def _():
            starts = [(s * team + choice) * each for s in range(shards)]
            wide = jnp.concatenate(
                [matrix[:, i : i + each].astype(WIDE) for matrix in (gate, up) for i in starts],
                1,
            )
            for index in range(ups):
                pack[index * chunk : (index + 1) * chunk] = wide[
                    :, index * LANES : (index + 1) * LANES
                ].astype(LOW)
            rows = down[...].astype(WIDE)[choice * each : (choice + 1) * each]
            for index in range(rows.shape[1] // (2 * LANES)):
                start = ups * chunk + 2 * index * each
                pack[start : start + 2 * each] = on_end(rows, index).astype(LOW)


def feed_forward_unpack(shards, packs, up_out, down_out):
    chunk = up_out.shape[0] // shards
    each = down_out.shape[0] // shards
    ups = up_out.shape[1] // LANES
    for shard in range(shards):
        for index in range(ups):
            up_out[shard * chunk : (shard + 1) * chunk, index * LANES : (index + 1) * LANES] = (
                packs[shard, index * chunk : (index + 1) * chunk]
            )
    for pair in range(shards // 2):
        for index in range(down_out.shape[1] // (2 * LANES)):
            start = ups * chunk + 2 * index * each
            even, odd = (
                packs[shard, start : start + 2 * each].astype(WIDE)
                for shard in (2 * pair, 2 * pair + 1)
            )
            for side in range(2):
                lane = (2 * index + side) * LANES
                line = slice(side * each, (side + 1) * each)
                down_out[2 * pair * each : 2 * (pair + 1) * each, lane : lane + LANES] = (
                    jnp.concatenate([even[line], odd[line]], 0).astype(LOW)
                )


def feed_forward_finish_kernel(team, shards, places, *refs):
    *slots, gate_out, up_out, down_out, ordered = refs
    chunk = gate_out.shape[0]
    each = down_out.shape[0] // team
    half = shards * each
    ups = 2 * half // LANES
    size = slots[0].shape[0]
    for index, slot in enumerate(slots):
        start = index // team * size
        ordered[member(places[0], index % team), start : start + size] = slot[...].astype(LOW)
    wide = [
        jnp.concatenate(
            [ordered[h, i * chunk : (i + 1) * chunk].astype(WIDE) for i in range(ups)], 1
        )
        for h in range(team)
    ]
    for base, out in ((0, gate_out), (half, up_out)):
        out[...] = jnp.concatenate(
            [
                wide[h][:, base + s * each : base + (s + 1) * each]
                for s in range(shards)
                for h in range(team)
            ],
            1,
        )
    for h in range(team):
        for index in range(down_out.shape[1] // (2 * LANES)):
            start = ups * chunk + 2 * index * each
            both = ordered[h, start : start + 2 * each].astype(WIDE)
            for side in range(2):
                lane = (2 * index + side) * LANES
                down_out[h * each : (h + 1) * each, lane : lane + LANES] = both[
                    side * each : (side + 1) * each
                ]


def mixer_backward_kernel(
    seqs,
    keys,
    shards,
    scalars,
    places,
    *refs,
):
    branch_slots = refs[:seqs]
    (
        out_rows,
        gate_raw,
        heads,
        head_gain,
        first,
        mixed,
        raw,
        gates,
        inverse,
        update,
        taps,
        weights,
        gate_rows,
        tokens,
        ffn_gain_grad,
        pack,
        first_grad_out,
        raw_grad_out,
        gates_grad_out,
        branch_grad,
        heads_grad,
    ) = refs[seqs:]
    values = heads.shape[1]
    outs = out_rows.shape[1] // seqs
    for slot in range(seqs):
        rows_each = branch_slots[slot].shape[0]
        branch_grad[slot * rows_each : (slot + 1) * rows_each] = branch_slots[slot][...]
    mixed_grad = right_dot(branch_grad[...], out_rows[...])
    out = heads[...]
    gate = gate_raw[...]
    gain = head_gain[...]
    scale = lax.rsqrt(jnp.mean(out * out, -1, keepdims=True) + EPS)
    normed = out * scale
    gate_sig = sigmoid(gate)
    gate_act = gate * gate_sig
    gate_grad = (
        mixed_grad * normed * gain * gate_sig * (1.0 + gate * (1.0 - gate_sig))
    ).astype(LOW)
    head_gain_grad = jnp.sum(mixed_grad * normed * gate_act, 0, keepdims=True)
    normed_grad = mixed_grad * gain * gate_act
    heads_grad[...] = scale * (
        normed_grad - normed * jnp.mean(normed_grad * normed, -1, keepdims=True)
    )
    place = pl.multiple_of(places[0] * outs, outs)
    gate_wgrad = left_dot(first[...], gate_grad)
    out_wgrad = left_dot(mixed[...], branch_grad[:, pl.ds(place, outs)])
    size = raw.shape[0] // seqs
    conv_width = taps.shape[1]
    count = taps.shape[0]
    part, shard = places[0], places[1]
    rows, cols = iotas(size)
    taps_grad = [jnp.zeros((1, conv_width), WIDE) for _ in range(count)]
    log_total = jnp.zeros((1, 1), WIDE)
    bias_total = jnp.zeros((1, 1), WIDE)
    for seq in range(seqs):
        span = slice(seq * size, (seq + 1) * size)
        out_grad = heads_grad[span]
        raw_in = raw[span]
        run, sig = conv_silu(raw_in, taps[...])
        query, key, value, query_act, query_r, key_act, key_r = unit_features(run * sig, keys)
        beta, decay_in, log_decay, upto = decay_matrix(gates[span], scalars[0], scalars[1])
        key_key = dot_nt(key, key) * upto
        scores = dot_nt(query, key) * upto
        solved = update[span]
        scores_grad = jnp.where(rows >= cols, dot_nt(out_grad, solved), 0.0)
        solved_grad = dot_tn(scores, out_grad)
        target_grad = dot_tn(inverse[span], solved_grad)
        system_grad = jnp.where(rows > cols, -dot_nt(target_grad, solved), 0.0)
        value_grad = beta * target_grad
        system_part = system_grad * key_key
        beta_grad = jnp.sum(target_grad * value, 1, keepdims=True) + jnp.sum(
            system_part, 1, keepdims=True
        )
        key_key_grad = system_grad * (beta * upto)
        scores_part = scores_grad * upto
        spread_grad = system_part * beta + scores_grad * scores
        query_grad = dot_nn(scores_part, key)
        key_grad = (
            dot_tn(scores_part, query) + dot_nn(key_key_grad, key) + dot_tn(key_key_grad, key)
        )
        total_row = jnp.sum(
            jnp.where(rows == cols, jnp.sum(spread_grad, 1, keepdims=True), 0.0),
            0,
            keepdims=True,
        ) - jnp.sum(spread_grad, 0, keepdims=True)
        decay_grad = jnp.sum(jnp.where(cols >= rows, total_row, 0.0), 1, keepdims=True)
        decay_raw_grad = -scalars[0] * decay_grad * sigmoid(decay_in)
        beta_raw_grad = beta_grad * beta * (1.0 - beta)
        log_total = log_total + jnp.sum(decay_grad * log_decay, 0, keepdims=True)
        bias_total = bias_total + jnp.sum(decay_raw_grad, 0, keepdims=True)
        beta_high = beta_raw_grad.astype(LOW).astype(WIDE)
        decay_high = decay_raw_grad.astype(LOW).astype(WIDE)
        lane = lax.broadcasted_iota(jnp.int32, (size, ROWS16), 1)
        gates_grad_out[span] = jnp.where(
            lane == 0,
            beta_high,
            jnp.where(
                lane == 1,
                decay_high,
                jnp.where(
                    lane == 2,
                    beta_raw_grad - beta_high,
                    jnp.where(lane == 3, decay_raw_grad - decay_high, 0.0),
                ),
            ),
        ).astype(LOW)
        query_grad = query_grad * (1.0 / math.sqrt(keys))
        query_unit = query_act * query_r
        query_act_grad = query_r * (
            query_grad - query_unit * jnp.sum(query_unit * query_grad, -1, keepdims=True)
        )
        key_act_grad = key_r * (key_grad - key * jnp.sum(key * key_grad, -1, keepdims=True))
        act_grad = jnp.concatenate([query_act_grad, key_act_grad, value_grad], 1)
        run_grad = act_grad * sig * (1.0 + run * (1.0 - sig))
        raw_grad = run_grad * taps[count - 1 : count]
        taps_grad[count - 1] = taps_grad[count - 1] + jnp.sum(
            run_grad * raw_in, 0, keepdims=True
        )
        for steps in range(1, count):
            tap = count - 1 - steps
            moved = earlier(run_grad, steps)
            raw_grad = raw_grad + moved * taps[tap : tap + 1]
            taps_grad[tap] = taps_grad[tap] + jnp.sum(moved * raw_in, 0, keepdims=True)
        raw_grad_out[span] = raw_grad.astype(LOW)
    width = tokens.shape[1]
    chunk = width // shards
    raw_low = raw_grad_out[...]
    head_wgrad = left_dot(first[...], raw_low)
    gates_rows = left_dot(gates_grad_out[...], first[...])
    first_grad = (
        right_dot(raw_low, weights[:, :conv_width])
        + right_dot(gate_grad, weights[:, conv_width:])
        + local_dot(gates_grad_out[...], gate_rows[...])
    )
    first_grad_out[...] = first_grad.astype(LOW)
    wide = tokens[...].astype(WIDE)
    normed = wide * lax.rsqrt(jnp.mean(wide * wide, -1, keepdims=True) + EPS)
    gain_grad = jnp.sum(first_grad * normed, 0, keepdims=True)
    beta_row = gates_rows[0:1] + gates_rows[2:3]
    decay_row = gates_rows[1:2] + gates_rows[3:4]
    head_shards = shards // seqs
    key_each = keys // head_shards
    value_each = (conv_width - 2 * keys) // head_shards
    head_each = head_gain_grad.shape[1] // shards
    all_taps = jnp.concatenate(taps_grad, 0)
    lane = lax.broadcasted_iota(jnp.int32, (1, conv_width), 1)
    decay_terms = jnp.zeros((1, conv_width), WIDE)
    for which, total in enumerate((log_total, bias_total)):
        for piece in range(3):
            high = total.astype(LOW).astype(WIDE)
            place = head_each + (which * 3 + piece) * shards + shard
            decay_terms = jnp.where(lane == place, high, decay_terms)
            total = total - high
    blocks = []
    for s in range(shards):
        line = slice(s * chunk, (s + 1) * chunk)
        i = s % head_shards
        gains = jnp.concatenate(
            [beta_row[:, line], decay_row[:, line], gain_grad[:, line], ffn_gain_grad[:, line]], 1
        )
        tap_rows = jnp.concatenate(
            [
                all_taps[:, i * key_each : (i + 1) * key_each],
                all_taps[:, keys + i * key_each : keys + (i + 1) * key_each],
                all_taps[:, 2 * keys + i * value_each : 2 * keys + (i + 1) * value_each],
            ],
            1,
        )
        tap_rows = jnp.where(part == s // head_shards, tap_rows, 0.0)
        tap_rows = jnp.concatenate(
            [tap_rows, jnp.zeros((count, conv_width - tap_rows.shape[1]), WIDE)], 1
        )
        head_row = jnp.concatenate(
            [
                head_gain_grad[:, s * head_each : (s + 1) * head_each],
                jnp.zeros((1, conv_width - head_each), WIDE),
            ],
            1,
        )
        small = jnp.concatenate(
            [
                gains,
                tap_rows,
                head_row + decay_terms,
                jnp.zeros((ROWS16 - count - 2, conv_width), WIDE),
            ],
            0,
        )
        empty = jnp.zeros((ROWS16, values + outs), WIDE)
        blocks.append(
            (
                head_wgrad[line],
                gate_wgrad[line],
                out_wgrad[line],
                jnp.concatenate([small, empty], 1),
            )
        )
    top, all_lanes = slice(0, chunk), slice(0, conv_width + values + outs)
    spots = (
        (top, slice(0, conv_width)),
        (top, slice(conv_width, conv_width + values)),
        (top, slice(conv_width + values, conv_width + values + outs)),
        (slice(chunk, chunk + ROWS16), all_lanes),
    )
    for s in range(shards):
        for block, (line, lanes) in zip(blocks[s], spots):
            pack[s, line, lanes] = block.astype(LOW)


def finish_kernel(
    team,
    keys,
    shards,
    count,
    scalars,
    *refs,
):
    slots = refs[:team]
    (
        query_out,
        key_out,
        value_out,
        gate_out,
        proj_out,
        beta_out,
        decay_out,
        mix_out,
        ffn_out,
        query_conv_out,
        key_conv_out,
        value_conv_out,
        head_out,
        log_out,
        bias_out,
        pair,
    ) = refs[team:]
    part = scalars[0]
    chunk = query_out.shape[0]
    values = value_out.shape[1] // team
    conv_width = 2 * keys + values
    key_each = query_conv_out.shape[1]
    conv_each = 2 * key_each + value_conv_out.shape[1]
    head_each = head_out.shape[1]
    total = None
    lane = lax.broadcasted_iota(jnp.int32, (1, LANES), 1)
    log_row = jnp.zeros((1, LANES), WIDE)
    bias_row = jnp.zeros((1, LANES), WIDE)
    pair[...] = jnp.zeros(pair.shape, WIDE)
    for steps in range(team):
        head = member(part, steps)
        key_place = pl.ds(pl.multiple_of(head * keys, keys), keys)
        value_place = pl.ds(pl.multiple_of(head * values, values), values)
        block = slots[steps]
        query_out[:, key_place] = block[:chunk, :keys].astype(WIDE)
        key_out[:, key_place] = block[:chunk, keys : 2 * keys].astype(WIDE)
        value_out[:, value_place] = block[:chunk, 2 * keys : conv_width].astype(WIDE)
        gate_out[:, value_place] = block[:chunk, conv_width : conv_width + values].astype(WIDE)
        proj_out[:, value_place] = block[:chunk, conv_width + values :].astype(WIDE)
        small = block[chunk:, :conv_width].astype(WIDE)
        total = small if total is None else total + small
        pair[pl.ds(head, 1), :] = small[0:1, :chunk]
        pair[pl.ds(head + team, 1), :] = small[0:1, chunk : 2 * chunk]
        terms = small[count + 1 : count + 2]
        wide_lane = lax.broadcasted_iota(jnp.int32, (1, conv_width), 1)
        ends = [head_each + 3 * shards * k for k in range(3)]
        log_sum = jnp.sum(
            jnp.where((wide_lane >= ends[0]) & (wide_lane < ends[1]), terms, 0.0),
            1,
            keepdims=True,
        )
        bias_sum = jnp.sum(
            jnp.where((wide_lane >= ends[1]) & (wide_lane < ends[2]), terms, 0.0),
            1,
            keepdims=True,
        )
        log_row = jnp.where(lane == head, log_sum, log_row)
        bias_row = jnp.where(lane == head, bias_sum, bias_row)
    beta_out[...] = pair[:team]
    decay_out[...] = pair[team : 2 * team]
    mix_out[...] = total[0:1, 2 * chunk : 3 * chunk]
    ffn_out[...] = total[0:1, 3 * chunk : 4 * chunk]
    query_conv_out[...] = total[1 : count + 1, :key_each]
    key_conv_out[...] = total[1 : count + 1, key_each : 2 * key_each]
    value_conv_out[...] = total[1 : count + 1, 2 * key_each : conv_each]
    head_out[...] = total[count + 1 : count + 2, :head_each]
    log_out[...] = log_row[:, :team]
    bias_out[...] = bias_row[:, :team]


def array(shape, dtype):
    return jax.ShapeDtypeStruct(shape, dtype)


def run_kernel(kernel, name, scalars, operands, outs, flops, scratch=(), far=0, far_outs=0):
    spec = pl.BlockSpec(memory_space=pltpu.VMEM)
    moved = sum(math.prod(v.shape) * v.dtype.itemsize for v in (*operands, *outs))
    return pl.pallas_call(
        kernel,
        out_shape=tuple(outs),
        in_specs=[pl.BlockSpec(memory_space=pltpu.SMEM)] * len(scalars)
        + [pl.BlockSpec(memory_space=pl.ANY)] * far
        + [spec] * (len(operands) - far),
        out_specs=[pl.BlockSpec(memory_space=pl.ANY)] * far_outs
        + [spec] * (len(outs) - far_outs),
        scratch_shapes=list(scratch),
        compiler_params=pltpu.CompilerParams(vmem_limit_bytes=(60 if far else 48) * 1024 * 1024),
        cost_estimate=pl.CostEstimate(flops=flops, bytes_accessed=moved, transcendentals=0),
        name=name,
    )(*scalars, *operands)


def team_pairs(devices, steps):
    return [(j, j ^ steps) for j in range(devices)]


def team_gather(block, devices, team):
    return [block] + [
        lax.ppermute(block, "rep", team_pairs(devices, steps)) for steps in range(1, team)
    ]


def swap(block, name, size, mask):
    return lax.ppermute(block, name, [(j, j ^ mask) for j in range(size)])


def line_gather(block, shards):
    return [block] + [
        swap(block, "shard", shards, 2 * steps) for steps in range(1, shards // 2)
    ]


def doubled(block, devices, near, far):
    size = block.shape[0]
    pair = swap(block, "rep", devices, near)
    quad = swap(both_ends(block, pair), "rep", devices, far)
    held = {0: block, near: pair, far: quad[:size], near | far: quad[size:]}
    return [held[e] for e in range(4)]


def team_halves(block, devices):
    half = block.shape[0] // 2
    return doubled(block[:half], devices, 1, 2) + doubled(block[half:], devices, 2, 1)


def both_ends(block, moved):
    return jnp.concatenate([block, moved], 0)


def team_send(slots, devices, team):
    return [slots[0]] + [
        lax.ppermute(slots[steps], "rep", team_pairs(devices, steps)) for steps in range(1, team)
    ]


def wide_sum(blocks):
    total = blocks[0].astype(WIDE)
    for block in blocks[1:]:
        total = total + block.astype(WIDE)
    return total


def norm_scale(v):
    return lax.rsqrt(jnp.mean(v * v, -1, keepdims=True) + EPS)


def replica_slots(block, part, devices, team):
    if devices == team:
        return team_gather(block, devices, team)
    blocks = lax.all_gather(block, "rep").astype(WIDE)
    blocks = jnp.sum(blocks.reshape((devices // team, team) + block.shape), 0)
    return [
        lax.dynamic_index_in_dim(blocks, part ^ e, 0, keepdims=False)
        for e in range(team)
    ]


def after(values, first):
    return lax.optimization_barrier((values, first))[0]


def body(
    inputs,
    cotangent,
    mix_gain,
    query_proj,
    key_proj,
    value_proj,
    beta_proj,
    decay_proj,
    gate_proj,
    query_conv,
    key_conv,
    value_conv,
    decay_log,
    decay_bias,
    head_gain,
    out_proj,
    ffn_gain,
    ffn_gate,
    ffn_up,
    ffn_down,
):
    devices = lax.axis_size("rep")
    shards = lax.axis_size("shard")
    team = beta_proj.shape[1]
    part = lax.axis_index("rep") % team
    shard = lax.axis_index("shard")
    places = jnp.stack([part, shard]).astype(jnp.int32)
    tokens_each, width = inputs.shape
    count = team * tokens_each
    chunk = mix_gain.shape[0]
    keys = query_proj.shape[1] // team
    values = value_proj.shape[1] // team
    outs = out_proj.shape[1] // team
    conv_width = 2 * keys + values
    hidden_each = ffn_down.shape[0] // team
    hidden_part = hidden_each * shards
    taps_count = query_conv.shape[0]
    key_each, value_each = query_conv.shape[1], value_conv.shape[1]
    head_each = head_gain.shape[0]

    ffn_rows = 2 * hidden_part * chunk // LANES + hidden_each * (width // LANES)

    mixer_pack = run_kernel(
        functools.partial(pack_kernel, team),
        "pack",
        (places,),
        (
            query_proj,
            key_proj,
            value_proj,
            gate_proj,
            out_proj,
            beta_proj.T,
            decay_proj.T,
            mix_gain[None],
            ffn_gain[None],
            query_conv,
            key_conv,
            value_conv,
            head_gain[None],
        ),
        (
            array((chunk + ROWS16, conv_width + values + outs), LOW),
        ),
        10**8,
        (pltpu.SemaphoreType.DMA((5,)),),
        5,
    )[0]
    pack_slots = line_gather(mixer_pack, shards)
    member_index = lax.axis_index("rep")
    gathered = lax.all_gather(inputs, "rep", axis=0)
    tokens = jnp.concatenate(
        [
            lax.dynamic_index_in_dim(gathered, member_index ^ e, 0, keepdims=False)
            for e in range(team)
        ],
        0,
    )
    cotangent_pair = swap(cotangent, "rep", devices, 2)
    pack_slots = after(pack_slots, cotangent_pair)
    cotangent_pair = both_ends(cotangent, cotangent_pair)
    ffn_pack = run_kernel(
        functools.partial(feed_forward_pack_kernel, team, shards),
        "feed_forward_pack",
        (places,),
        (after(ffn_gate, mixer_pack), ffn_up, ffn_down),
        (array((ffn_rows, LANES), LOW),),
        10**8,
        (
            pltpu.VMEM(ffn_gate.shape, LOW),
            pltpu.VMEM(ffn_up.shape, LOW),
            pltpu.VMEM(ffn_down.shape, LOW),
            pltpu.SemaphoreType.DMA((3,)),
        ),
        3,
    )[0]
    ffn_packs = lax.all_gather(after(ffn_pack, pack_slots), "shard", axis=0)
    pack_mine = jnp.stack(pack_slots)
    pack_theirs = swap(pack_mine, "shard", shards, 1)
    cotangent_quad = swap(after(cotangent_pair, pack_slots), "rep", devices, 1)
    tokens = after(tokens, cotangent_quad)
    cotangents = jnp.concatenate(
        [
            cotangent,
            cotangent_quad[:tokens_each],
            cotangent_pair[tokens_each:],
            cotangent_quad[tokens_each:],
        ],
        0,
    )
    scalars = jnp.stack(
        [
            jnp.exp(lax.dynamic_index_in_dim(decay_log, part, 0, keepdims=False)),
            lax.dynamic_index_in_dim(decay_bias, part, 0, keepdims=False),
        ]
    )

    (
        first,
        raw,
        gate_raw,
        gates,
        inverse,
        update,
        heads,
        mixed_part,
        head_weights,
        mix_row,
        ffn_row,
        gate_rows,
        taps,
        head_row,
    ) = run_kernel(
        functools.partial(mixer_forward_kernel, team, keys, taps_count),
        "mixer_forward",
        (scalars, places),
        (tokens, pack_mine, pack_theirs),
        (
            array((count, width), LOW),
            array((count, conv_width), WIDE),
            array((count, values), WIDE),
            array((count, ROWS16), WIDE),
            array((count, tokens_each), WIDE),
            array((count, values), WIDE),
            array((count, values), WIDE),
            array((count, values), LOW),
            array((width, conv_width + values), LOW),
            array((1, width), WIDE),
            array((1, width), WIDE),
            array((ROWS16, width), LOW),
            array((taps_count, conv_width), WIDE),
            array((1, values), WIDE),
        ),
        8 * 10**9,
        (pltpu.VMEM((ROWS16, width), WIDE),),
    )
    proj_all = both_ends(
        pack_mine[:, :chunk, conv_width + values :],
        pack_theirs[:, :chunk, conv_width + values :],
    )
    proj_slots = team_gather(proj_all, devices, team)
    mixed_part = after(mixed_part, proj_slots)
    mixed_slots = team_gather(mixed_part, devices, team)

    (
        mixed,
        hidden_own,
        second_part,
        result_part,
        out_rows,
        ffn_grads,
        ffn_gain_part,
    ) = run_kernel(
        functools.partial(feed_forward_kernel, team),
        "feed_forward",
        (places,),
        (*proj_slots, tokens, ffn_packs, cotangents, *mixed_slots, ffn_row),
        (
            array((count, width), LOW),
            array((tokens_each, width), WIDE),
            array((count, width), LOW),
            array((count, width), LOW),
            array((values, width), LOW),
            array((shards, ffn_rows, LANES), LOW),
            array((1, width), WIDE),
        ),
        16 * 10**9,
        (
            pltpu.VMEM((count, width), LOW),
            pltpu.VMEM((width, width), LOW),
            pltpu.VMEM((count, width), LOW),
            pltpu.VMEM((count, width), LOW),
            pltpu.VMEM((shards, ffn_rows, LANES), LOW),
            pltpu.VMEM((count, width), WIDE),
            pltpu.VMEM((width, 2 * hidden_part), LOW),
            pltpu.VMEM((hidden_part, width), LOW),
            *(pltpu.VMEM(slot.shape, LOW) for slot in proj_slots),
            pltpu.VMEM(tokens.shape, LOW),
            pltpu.VMEM(ffn_packs.shape, LOW),
            pltpu.VMEM(cotangents.shape, LOW),
            pltpu.SemaphoreType.DMA((team + 3,)),
            pltpu.SemaphoreType.DMA((7,)),
        ),
        team + 3,
        6,
    )

    def slots_of(v):
        return [v[e * tokens_each : (e + 1) * tokens_each] for e in range(team)]

    second_slots = team_send(slots_of(second_part), devices, team)
    ffn_shard = lax.psum_scatter(ffn_grads, "shard", scatter_dimension=0)
    second_grad = wide_sum(second_slots)
    scale_own = norm_scale(hidden_own)
    weighted = second_grad * ffn_row
    hidden_grad = cotangent.astype(WIDE) + scale_own * (
        weighted
        - hidden_own
        * (scale_own * scale_own * jnp.mean(hidden_own * weighted, -1, keepdims=True))
    )
    branch_slots = team_gather(hidden_grad.astype(LOW), devices, team)


    result_part = after(result_part, branch_slots)
    result_slots = team_send(slots_of(result_part), devices, team)

    head_grads, first_part = run_kernel(
        functools.partial(mixer_backward_kernel, team, keys, shards),
        "mixer_backward",
        (scalars, places),
        (
            *branch_slots,
            out_rows,
            gate_raw,
            heads,
            head_row,
            first,
            mixed,
            raw,
            gates,
            inverse,
            update,
            taps,
            head_weights,
            gate_rows,
            tokens,
            ffn_gain_part,
        ),
        (
            array((shards, chunk + ROWS16, conv_width + values + outs), LOW),
            array((count, width), LOW),
        ),
        10 * 10**9,
        (
            pltpu.VMEM((count, conv_width), LOW),
            pltpu.VMEM((count, ROWS16), LOW),
            pltpu.VMEM((count, width), LOW),
            pltpu.VMEM((count, values), WIDE),
        ),
    )
    head_grads = after(head_grads, result_slots)
    head_shard = lax.psum_scatter(head_grads, "shard", scatter_dimension=0)
    first_slots = team_send(slots_of(first_part), devices, team)
    if devices == team == 4:
        ffn_totals = team_halves(ffn_shard, devices)
    else:
        ffn_totals = replica_slots(ffn_shard, part, devices, team)
    first_grad = wide_sum(after(first_slots, ffn_totals))
    seq_in = inputs.astype(WIDE)
    seq_scale = norm_scale(seq_in)
    weighted = first_grad * mix_row
    inputs_grad = hidden_grad + seq_scale * (
        weighted
        - seq_in * (seq_scale * seq_scale * jnp.mean(seq_in * weighted, -1, keepdims=True))
    )
    result = hidden_own + wide_sum(result_slots)

    head_totals = replica_slots(after(head_shard, ffn_totals), part, devices, team)
    gate_grads, up_grads, down_grads = run_kernel(
        functools.partial(feed_forward_finish_kernel, team, shards),
        "feed_forward_finish",
        (places,),
        ffn_totals,
        (
            array(ffn_gate.shape, WIDE),
            array(ffn_up.shape, WIDE),
            array(ffn_down.shape, WIDE),
        ),
        10**8,
        (pltpu.VMEM((team, ffn_rows, LANES), LOW),),
    )
    (
        query_total,
        key_total,
        value_total,
        gate_total,
        out_total,
        beta_total,
        decay_total,
        mix_total,
        ffn_total,
        query_conv_total,
        key_conv_total,
        value_conv_total,
        head_total,
        log_total,
        bias_total,
    ) = run_kernel(
        functools.partial(finish_kernel, team, keys, shards, taps_count),
        "finish",
        (places,),
        head_totals,
        (
            array((chunk, team * keys), WIDE),
            array((chunk, team * keys), WIDE),
            array((chunk, team * values), WIDE),
            array((chunk, team * values), WIDE),
            array((chunk, team * outs), WIDE),
            array((team, chunk), WIDE),
            array((team, chunk), WIDE),
            array((1, chunk), WIDE),
            array((1, chunk), WIDE),
            array((taps_count, key_each), WIDE),
            array((taps_count, key_each), WIDE),
            array((taps_count, value_each), WIDE),
            array((1, head_each), WIDE),
            array((1, team), WIDE),
            array((1, team), WIDE),
        ),
        10**8,
        (pltpu.VMEM((max(8, 2 * team), chunk), WIDE),),
    )
    return (
        result.astype(LOW),
        inputs_grad,
        mix_total[0],
        query_total,
        key_total,
        value_total,
        beta_total.T,
        decay_total.T,
        gate_total,
        query_conv_total,
        key_conv_total,
        value_conv_total,
        log_total[0],
        bias_total[0],
        head_total[0],
        out_total,
        ffn_total[0],
        gate_grads,
        up_grads,
        down_grads,
    )


def solution(mesh):
    rows = P("shard", None)
    return jax.shard_map(
        body,
        mesh=mesh,
        in_specs=(
            P(("rep", "shard"), None),
            P(("rep", "shard"), None),
            P("shard"),
            rows,
            rows,
            rows,
            rows,
            rows,
            rows,
            P(None, "shard"),
            P(None, "shard"),
            P(None, "shard"),
            P(),
            P(),
            P("shard"),
            rows,
            P("shard"),
            rows,
            rows,
            rows,
        ),
        out_specs=(
            P(("rep", "shard"), None),
            P(("rep", "shard"), None),
            P("shard"),
            rows,
            rows,
            rows,
            rows,
            rows,
            rows,
            P(None, "shard"),
            P(None, "shard"),
            P(None, "shard"),
            P(),
            P(),
            P("shard"),
            rows,
            P("shard"),
            rows,
            rows,
            rows,
        ),
        check_vma=False,
    )
```

```python
import functools
import math

import jax
import jax.numpy as jnp
from jax import lax
from jax.experimental import pallas as pl
from jax.experimental.pallas import tpu as pltpu
from jax.sharding import PartitionSpec as P

EPS = 1e-06
HIGH = lax.Precision.HIGHEST
LOW = jnp.bfloat16
WIDE = jnp.float32
LANES = 128
ROWS16 = 16


def local_dot(left, right):
    return jnp.dot(left, right, preferred_element_type=WIDE)


def left_dot(left, right):
    return lax.dot_general(left, right, (((0,), (0,)), ((), ())), preferred_element_type=WIDE)


def right_dot(left, right):
    return lax.dot_general(left, right, (((1,), (1,)), ((), ())), preferred_element_type=WIDE)


def dot_nn(left, right):
    return jnp.dot(left, right, preferred_element_type=WIDE, precision=HIGH)


def dot_nt(left, right):
    return lax.dot_general(
        left, right, (((1,), (1,)), ((), ())), preferred_element_type=WIDE, precision=HIGH
    )


def dot_tn(left, right):
    return lax.dot_general(
        left, right, (((0,), (0,)), ((), ())), preferred_element_type=WIDE, precision=HIGH
    )


def sigmoid(v):
    return 1.0 / (1.0 + jnp.exp(-v))


def iotas(size):
    return (
        lax.broadcasted_iota(jnp.int32, (size, size), 0),
        lax.broadcasted_iota(jnp.int32, (size, size), 1),
    )


def later(v, steps):
    rows = lax.broadcasted_iota(jnp.int32, v.shape, 0)
    return jnp.where(rows >= steps, pltpu.roll(v, steps, 0), 0.0)


def earlier(v, steps):
    rows = lax.broadcasted_iota(jnp.int32, v.shape, 0)
    return jnp.where(rows < v.shape[0] - steps, pltpu.roll(v, v.shape[0] - steps, 0), 0.0)


def conv_silu(raw, taps):
    count = taps.shape[0]
    run = raw * taps[count - 1 : count]
    for steps in range(1, count):
        run = run + later(raw, steps) * taps[count - 1 - steps : count - steps]
    sig = sigmoid(run)
    return run, sig


def unit_features(act, keys):
    query_act, key_act, value = act[:, :keys], act[:, keys : 2 * keys], act[:, 2 * keys :]
    query_r = lax.rsqrt(jnp.sum(query_act * query_act, -1, keepdims=True) + EPS)
    key_r = lax.rsqrt(jnp.sum(key_act * key_act, -1, keepdims=True) + EPS)
    query = query_act * query_r * (1.0 / math.sqrt(keys))
    return query, key_act * key_r, value, query_act, query_r, key_act, key_r


def softplus(v):
    return jnp.maximum(v, 0.0) + jnp.log1p(jnp.exp(-jnp.abs(v)))


def decay_matrix(gates, decay, bias):
    size = gates.shape[0]
    rows, cols = iotas(size)
    beta = sigmoid(gates[:, 0:1])
    decay_in = gates[:, 1:2] + bias
    log_decay = -decay * softplus(decay_in)
    decay_row = jnp.sum(jnp.where(rows == cols, log_decay, 0.0), 0, keepdims=True)
    total_col = jnp.sum(jnp.where(cols <= rows, decay_row, 0.0), 1, keepdims=True)
    total_row = jnp.sum(jnp.where(rows <= cols, log_decay, 0.0), 0, keepdims=True)
    spread = jnp.where(rows >= cols, total_col - total_row, 0.0)
    upto = jnp.where(rows >= cols, jnp.exp(spread), 0.0)
    return beta, decay_in, log_decay, upto


def unit_lower_inverse(systems):
    size = systems[0].shape[0]
    rows, cols = iotas(size)
    block = 8
    near = [jnp.where(rows // block == cols // block, a, 0.0) for a in systems]
    eye = jnp.where(rows == cols, 1.0, 0.0)
    power = [dot_nn(a, a) for a in near]
    inverse = [eye - a for a in near]
    inverse = [x + dot_nn(x, p) for x, p in zip(inverse, power)]
    power = [dot_nn(p, p) for p in power]
    inverse = [x + dot_nn(x, p) for x, p in zip(inverse, power)]
    while block < size:
        cross = (rows // (2 * block) == cols // (2 * block)) & (rows // block != cols // block)
        middle = [dot_nn(jnp.where(cross, a, 0.0), x) for a, x in zip(systems, inverse)]
        inverse = [x - dot_nn(x, m) for x, m in zip(inverse, middle)]
        block *= 2
    return inverse


def pack_kernel(
    team,
    places,
    query,
    key,
    value,
    gate,
    proj,
    beta,
    decay,
    mix_gain,
    ffn_gain,
    query_conv,
    key_conv,
    value_conv,
    head_gain,
    pack_out,
    sems,
):
    part, shard = places[0], places[1]
    chunk = query.shape[0]
    keys, values = query.shape[1] // team, value.shape[1] // team
    outs = proj.shape[1] // team
    width = pack_out.shape[1]
    count = query_conv.shape[0]
    head_each = head_gain.shape[1]
    copies = []
    start = 0
    for index, (matrix, size) in enumerate(
        ((query, keys), (key, keys), (value, values), (gate, values), (proj, outs))
    ):
        source = matrix.at[:, pl.ds(pl.multiple_of(part * size, size), size)]
        target = pack_out.at[:chunk, start : start + size]
        start += size
        copies.append(pltpu.make_async_copy(source, target, sems.at[index]))
    for copy in copies:
        copy.start()

    def head_row(matrix):
        line = lax.broadcasted_iota(jnp.int32, matrix.shape, 0)
        return jnp.sum(jnp.where(line == part, matrix[...].astype(WIDE), 0.0), 0, keepdims=True)

    gains = [mix_gain[...].astype(WIDE), ffn_gain[...].astype(WIDE)]
    gains += [head_row(beta), head_row(decay)]
    gains.append(jnp.zeros((1, width - 4 * chunk), WIDE))
    pieces = []
    for taps, size in ((query_conv, keys), (key_conv, keys), (value_conv, values)):
        wide = taps[...].astype(WIDE)
        pieces.append(jnp.concatenate([wide] * (size // wide.shape[1]), 1))
    pieces = jnp.concatenate(pieces, 1)
    lane = lax.broadcasted_iota(jnp.int32, pieces.shape, 1)
    inside = jnp.where(lane < 2 * keys, lane % keys // query_conv.shape[1], 0)
    inside = jnp.where(lane < 2 * keys, inside, (lane - 2 * keys) // value_conv.shape[1])
    owners = keys // query_conv.shape[1]
    pieces = jnp.where(inside + part * owners == shard, pieces, 0.0)
    taps_rows = jnp.concatenate(
        [pieces, jnp.zeros((count, width - pieces.shape[1]), WIDE)], 1
    )
    head = jnp.concatenate([head_gain[...].astype(WIDE)] * (values // head_each), 1)
    lane = lax.broadcasted_iota(jnp.int32, head.shape, 1)
    head = jnp.where(lane // head_each == shard, head, 0.0)
    head = jnp.concatenate([head, jnp.zeros((1, width - values), WIDE)], 1)
    small = jnp.concatenate(
        [
            jnp.concatenate(gains, 1),
            taps_rows,
            head,
            jnp.zeros((ROWS16 - count - 2, width), WIDE),
        ],
        0,
    )
    pack_out[chunk:] = small.astype(LOW)
    for copy in copies:
        copy.wait()


def slot_shard(places, slot, same_core):
    return jnp.bitwise_xor(places[1], 2 * slot + (0 if same_core else 1))


def mixer_forward_kernel(
    seqs,
    keys,
    count,
    scalars,
    places,
    tokens,
    mine,
    theirs,
    first_out,
    raw_out,
    gate_out,
    gates_out,
    inverse_out,
    update_out,
    heads_out,
    mixed_out,
    weights,
    mix_row,
    ffn_row,
    gate_rows,
    taps,
    head_gain,
    gate_wide,
):
    size = tokens.shape[0] // seqs
    chips, block = mine.shape[0], mine.shape[1]
    chunk = block - ROWS16
    values = heads_out.shape[1]
    conv_width = 2 * keys + values
    gate_wide[...] = jnp.zeros(gate_wide.shape, WIDE)
    total = None
    for same_core, slots in ((True, mine), (False, theirs)):
        for slot in range(chips):
            shard = slot_shard(places, slot, same_core)
            line = pl.ds(pl.multiple_of(shard * chunk, chunk), chunk)
            weights[line, :] = slots[slot, :chunk, : conv_width + values]
            small = slots[slot, chunk:].astype(WIDE)
            mix_row[:, line] = small[0:1, :chunk]
            ffn_row[:, line] = small[0:1, chunk : 2 * chunk]
            pair = small[0:1, 2 * chunk : 3 * chunk], small[0:1, 3 * chunk : 4 * chunk]
            for row in range(4):
                gate_wide[row : row + 1, line] = pair[row % 2]
            total = small if total is None else total + small
    gate_rows[...] = gate_wide[...].astype(LOW)
    taps[...] = total[1 : count + 1, :conv_width]
    head_gain[...] = total[count + 1 : count + 2, :values]
    wide = tokens[...].astype(WIDE)
    first = (
        wide * lax.rsqrt(jnp.mean(wide * wide, -1, keepdims=True) + EPS) * mix_row[...]
    ).astype(LOW)
    first_out[...] = first
    raw_out[...] = local_dot(first, weights[:, :conv_width])
    gate_out[...] = local_dot(first, weights[:, conv_width:])
    gates_out[...] = right_dot(first, gate_rows[...])
    rows, cols = iotas(size)
    parts = []
    for seq in range(seqs):
        span = slice(seq * size, (seq + 1) * size)
        run, sig = conv_silu(raw_out[span], taps[...])
        query, key, value = unit_features(run * sig, keys)[:3]
        beta, _, _, upto = decay_matrix(gates_out[span], scalars[0], scalars[1])
        system = jnp.where(rows > cols, beta * dot_nt(key, key) * upto, 0.0)
        scores = dot_nt(query, key) * upto
        parts.append((system, scores, beta * value))
    inverses = unit_lower_inverse([p[0] for p in parts])
    for seq in range(seqs):
        span = slice(seq * size, (seq + 1) * size)
        inverse_out[span] = inverses[seq]
        update = dot_nn(inverses[seq], parts[seq][2])
        heads = dot_nn(parts[seq][1], update)
        update_out[span] = update
        heads_out[span] = heads
        gate = gate_out[span]
        normed = heads * lax.rsqrt(jnp.mean(heads * heads, -1, keepdims=True) + EPS)
        mixed_out[span] = (normed * head_gain[...] * (gate * sigmoid(gate))).astype(LOW)


def member(part, steps):
    return jnp.bitwise_xor(part, steps)


def feed_forward_kernel(
    team,
    scalars,
    *refs,
):
    outs_count = team
    far = refs[: outs_count + 3]
    refs = refs[outs_count + 3 :]
    mixed_slots, gain = refs[:team], refs[team]
    far_outs, gain_grad_out = refs[team + 1 : team + 7], refs[team + 7]
    (
        mixed,
        out_full,
        result,
        second_grad_low,
        grads,
        hidden,
        up_weights,
        down_weights,
        *near,
        sems,
        out_sems,
    ) = refs[team + 8 :]
    mixed_out, hidden_out, second_grad_out, result_out, out_rows_out, grads_out = far_outs
    fetch = [
        pltpu.make_async_copy(source, target, sems.at[index])
        for index, (source, target) in enumerate(zip(far, near))
    ]
    early = outs_count + 1
    for copy in fetch:
        copy.start()
    sent = []

    def send(source, target):
        copy = pltpu.make_async_copy(source, target, out_sems.at[len(sent)])
        copy.start()
        sent.append(copy)

    out_slots = near[:outs_count]
    tokens, packs, cotangents = near[outs_count:]
    part = scalars[0]
    size = tokens.shape[0] // team
    values = mixed_slots[0].shape[1]
    outs = out_slots[0].shape[2]
    for steps in range(team):
        place = pl.multiple_of(member(part, steps) * values, values)
        for slot in range(team):
            there = slot ^ steps
            mixed[slot * size : (slot + 1) * size, pl.ds(place, values)] = mixed_slots[steps][
                there * size : (there + 1) * size
            ]
    send(mixed, mixed_out)
    chips, chunk = out_slots[0].shape[0] // 2, out_slots[0].shape[1]
    for copy in fetch[:early]:
        copy.wait()
    for index in range(outs_count):
        place = pl.multiple_of(member(part, index) * outs, outs)
        for slot in range(2 * chips):
            shard = slot_shard(scalars, slot % chips, slot < chips)
            line = pl.ds(pl.multiple_of(shard * chunk, chunk), chunk)
            out_full[line, pl.ds(place, outs)] = out_slots[index][slot]
    row = pl.multiple_of(part * values, values)
    send(out_full.at[pl.ds(row, values)], out_rows_out)
    hidden[...] = tokens[...].astype(WIDE) + local_dot(mixed[...], out_full[...])
    send(hidden.at[:size], hidden_out)
    wide = hidden[...]
    normed = wide * lax.rsqrt(jnp.mean(wide * wide, -1, keepdims=True) + EPS)
    second = (normed * gain[...]).astype(LOW)
    fetch[early].wait()
    feed_forward_unpack(packs.shape[0], packs, up_weights, down_weights)
    fetch[early + 1].wait()
    part_width = down_weights.shape[0]
    both = local_dot(second, up_weights[...])
    gate, up = both[:, :part_width], both[:, part_width:]
    gate_sig = sigmoid(gate)
    gate_act = gate * gate_sig
    active = (gate_act * up).astype(LOW)
    result[...] = local_dot(active, down_weights[...]).astype(LOW)
    send(result, result_out)
    shards = grads.shape[0]
    chunk = out_full.shape[0] // shards
    each = part_width // shards
    ups = 2 * part_width // LANES
    down_grad = left_dot(active, cotangents[...])
    for shard in range(shards):
        for index in range(down_grad.shape[1] // (2 * LANES)):
            start = ups * chunk + 2 * index * each
            grads[shard, start : start + 2 * each] = on_end(
                down_grad[shard * each : (shard + 1) * each], index
            ).astype(LOW)
    lower = pl.ds(ups * chunk, grads.shape[1] - ups * chunk)
    send(grads.at[:, lower], grads_out.at[:, lower])
    active_grad = right_dot(cotangents[...], down_weights[...])
    gate_back = (active_grad * up * gate_sig * (1.0 + gate * (1.0 - gate_sig))).astype(LOW)
    up_back = (active_grad * gate_act).astype(LOW)
    back = jnp.concatenate([gate_back, up_back], 1)
    half = shards // 2
    for first_shard in (0, half):
        line = slice(first_shard * chunk, (first_shard + half) * chunk)
        up_grad = left_dot(second[:, line], back)
        for shard in range(half):
            for index in range(ups):
                grads[first_shard + shard, index * chunk : (index + 1) * chunk] = up_grad[
                    shard * chunk : (shard + 1) * chunk, index * LANES : (index + 1) * LANES
                ].astype(LOW)
        spot = pl.ds(first_shard, half), pl.ds(0, ups * chunk)
        send(grads.at[spot], grads_out.at[spot])
    second_grad = right_dot(back, up_weights[...])
    second_grad_low[...] = second_grad.astype(LOW)
    send(second_grad_low, second_grad_out)
    wide = hidden[...]
    normed = wide * lax.rsqrt(jnp.mean(wide * wide, -1, keepdims=True) + EPS)
    gain_grad_out[...] = jnp.sum(second_grad * normed, 0, keepdims=True)
    for copy in sent:
        copy.wait()


def on_end(rows, index):
    start = 2 * index * LANES
    return jnp.concatenate(
        [rows[:, start : start + LANES], rows[:, start + LANES : start + 2 * LANES]], 0
    )


def feed_forward_pack_kernel(team, shards, places, gate_far, up_far, down_far, pack, gate, up, down, sems):
    fetch = [
        pltpu.make_async_copy(far, near, sems.at[index])
        for index, (far, near) in enumerate(((gate_far, gate), (up_far, up), (down_far, down)))
    ]
    for copy in fetch:
        copy.start()
    chunk = gate.shape[0]
    each = down.shape[0] // team
    ups = 2 * shards * each // LANES
    for copy in fetch:
        copy.wait()

    for choice in range(team):

        @pl.when(places[0] == choice)
        def _():
            starts = [(s * team + choice) * each for s in range(shards)]
            wide = jnp.concatenate(
                [matrix[:, i : i + each].astype(WIDE) for matrix in (gate, up) for i in starts],
                1,
            )
            for index in range(ups):
                pack[index * chunk : (index + 1) * chunk] = wide[
                    :, index * LANES : (index + 1) * LANES
                ].astype(LOW)
            rows = down[...].astype(WIDE)[choice * each : (choice + 1) * each]
            for index in range(rows.shape[1] // (2 * LANES)):
                start = ups * chunk + 2 * index * each
                pack[start : start + 2 * each] = on_end(rows, index).astype(LOW)


def feed_forward_unpack(shards, packs, up_out, down_out):
    chunk = up_out.shape[0] // shards
    each = down_out.shape[0] // shards
    ups = up_out.shape[1] // LANES
    for shard in range(shards):
        for index in range(ups):
            up_out[shard * chunk : (shard + 1) * chunk, index * LANES : (index + 1) * LANES] = (
                packs[shard, index * chunk : (index + 1) * chunk]
            )
    for pair in range(shards // 2):
        for index in range(down_out.shape[1] // (2 * LANES)):
            start = ups * chunk + 2 * index * each
            even, odd = (
                packs[shard, start : start + 2 * each].astype(WIDE)
                for shard in (2 * pair, 2 * pair + 1)
            )
            for side in range(2):
                lane = (2 * index + side) * LANES
                line = slice(side * each, (side + 1) * each)
                down_out[2 * pair * each : 2 * (pair + 1) * each, lane : lane + LANES] = (
                    jnp.concatenate([even[line], odd[line]], 0).astype(LOW)
                )


def feed_forward_finish_kernel(team, shards, places, *refs):
    *slots, gate_out, up_out, down_out, ordered = refs
    chunk = gate_out.shape[0]
    each = down_out.shape[0] // team
    half = shards * each
    ups = 2 * half // LANES
    size = slots[0].shape[0]
    for index, slot in enumerate(slots):
        start = index // team * size
        ordered[member(places[0], index % team), start : start + size] = slot[...].astype(LOW)
    wide = [
        jnp.concatenate(
            [ordered[h, i * chunk : (i + 1) * chunk].astype(WIDE) for i in range(ups)], 1
        )
        for h in range(team)
    ]
    for base, out in ((0, gate_out), (half, up_out)):
        out[...] = jnp.concatenate(
            [
                wide[h][:, base + s * each : base + (s + 1) * each]
                for s in range(shards)
                for h in range(team)
            ],
            1,
        )
    for h in range(team):
        for index in range(down_out.shape[1] // (2 * LANES)):
            start = ups * chunk + 2 * index * each
            both = ordered[h, start : start + 2 * each].astype(WIDE)
            for side in range(2):
                lane = (2 * index + side) * LANES
                down_out[h * each : (h + 1) * each, lane : lane + LANES] = both[
                    side * each : (side + 1) * each
                ]


def mixer_backward_kernel(
    seqs,
    keys,
    shards,
    scalars,
    places,
    *refs,
):
    branch_slots = refs[:seqs]
    (
        out_rows,
        gate_raw,
        heads,
        head_gain,
        first,
        mixed,
        raw,
        gates,
        inverse,
        update,
        taps,
        weights,
        gate_rows,
        tokens,
        ffn_gain_grad,
        pack,
        first_grad_out,
        raw_grad_out,
        gates_grad_out,
        branch_grad,
        heads_grad,
    ) = refs[seqs:]
    values = heads.shape[1]
    outs = out_rows.shape[1] // seqs
    for slot in range(seqs):
        rows_each = branch_slots[slot].shape[0]
        branch_grad[slot * rows_each : (slot + 1) * rows_each] = branch_slots[slot][...]
    mixed_grad = right_dot(branch_grad[...], out_rows[...])
    out = heads[...]
    gate = gate_raw[...]
    gain = head_gain[...]
    scale = lax.rsqrt(jnp.mean(out * out, -1, keepdims=True) + EPS)
    normed = out * scale
    gate_sig = sigmoid(gate)
    gate_act = gate * gate_sig
    gate_grad = (
        mixed_grad * normed * gain * gate_sig * (1.0 + gate * (1.0 - gate_sig))
    ).astype(LOW)
    head_gain_grad = jnp.sum(mixed_grad * normed * gate_act, 0, keepdims=True)
    normed_grad = mixed_grad * gain * gate_act
    heads_grad[...] = scale * (
        normed_grad - normed * jnp.mean(normed_grad * normed, -1, keepdims=True)
    )
    place = pl.multiple_of(places[0] * outs, outs)
    gate_wgrad = left_dot(first[...], gate_grad)
    out_wgrad = left_dot(mixed[...], branch_grad[:, pl.ds(place, outs)])
    size = raw.shape[0] // seqs
    conv_width = taps.shape[1]
    count = taps.shape[0]
    part, shard = places[0], places[1]
    rows, cols = iotas(size)
    taps_grad = [jnp.zeros((1, conv_width), WIDE) for _ in range(count)]
    log_total = jnp.zeros((1, 1), WIDE)
    bias_total = jnp.zeros((1, 1), WIDE)
    for seq in range(seqs):
        span = slice(seq * size, (seq + 1) * size)
        out_grad = heads_grad[span]
        raw_in = raw[span]
        run, sig = conv_silu(raw_in, taps[...])
        query, key, value, query_act, query_r, key_act, key_r = unit_features(run * sig, keys)
        beta, decay_in, log_decay, upto = decay_matrix(gates[span], scalars[0], scalars[1])
        key_key = dot_nt(key, key) * upto
        scores = dot_nt(query, key) * upto
        solved = update[span]
        scores_grad = jnp.where(rows >= cols, dot_nt(out_grad, solved), 0.0)
        solved_grad = dot_tn(scores, out_grad)
        target_grad = dot_tn(inverse[span], solved_grad)
        system_grad = jnp.where(rows > cols, -dot_nt(target_grad, solved), 0.0)
        value_grad = beta * target_grad
        system_part = system_grad * key_key
        beta_grad = jnp.sum(target_grad * value, 1, keepdims=True) + jnp.sum(
            system_part, 1, keepdims=True
        )
        key_key_grad = system_grad * (beta * upto)
        scores_part = scores_grad * upto
        spread_grad = system_part * beta + scores_grad * scores
        query_grad = dot_nn(scores_part, key)
        key_grad = (
            dot_tn(scores_part, query) + dot_nn(key_key_grad, key) + dot_tn(key_key_grad, key)
        )
        total_row = jnp.sum(
            jnp.where(rows == cols, jnp.sum(spread_grad, 1, keepdims=True), 0.0),
            0,
            keepdims=True,
        ) - jnp.sum(spread_grad, 0, keepdims=True)
        decay_grad = jnp.sum(jnp.where(cols >= rows, total_row, 0.0), 1, keepdims=True)
        decay_raw_grad = -scalars[0] * decay_grad * sigmoid(decay_in)
        beta_raw_grad = beta_grad * beta * (1.0 - beta)
        log_total = log_total + jnp.sum(decay_grad * log_decay, 0, keepdims=True)
        bias_total = bias_total + jnp.sum(decay_raw_grad, 0, keepdims=True)
        beta_high = beta_raw_grad.astype(LOW).astype(WIDE)
        decay_high = decay_raw_grad.astype(LOW).astype(WIDE)
        lane = lax.broadcasted_iota(jnp.int32, (size, ROWS16), 1)
        gates_grad_out[span] = jnp.where(
            lane == 0,
            beta_high,
            jnp.where(
                lane == 1,
                decay_high,
                jnp.where(
                    lane == 2,
                    beta_raw_grad - beta_high,
                    jnp.where(lane == 3, decay_raw_grad - decay_high, 0.0),
                ),
            ),
        ).astype(LOW)
        query_grad = query_grad * (1.0 / math.sqrt(keys))
        query_unit = query_act * query_r
        query_act_grad = query_r * (
            query_grad - query_unit * jnp.sum(query_unit * query_grad, -1, keepdims=True)
        )
        key_act_grad = key_r * (key_grad - key * jnp.sum(key * key_grad, -1, keepdims=True))
        act_grad = jnp.concatenate([query_act_grad, key_act_grad, value_grad], 1)
        run_grad = act_grad * sig * (1.0 + run * (1.0 - sig))
        raw_grad = run_grad * taps[count - 1 : count]
        taps_grad[count - 1] = taps_grad[count - 1] + jnp.sum(
            run_grad * raw_in, 0, keepdims=True
        )
        for steps in range(1, count):
            tap = count - 1 - steps
            moved = earlier(run_grad, steps)
            raw_grad = raw_grad + moved * taps[tap : tap + 1]
            taps_grad[tap] = taps_grad[tap] + jnp.sum(moved * raw_in, 0, keepdims=True)
        raw_grad_out[span] = raw_grad.astype(LOW)
    width = tokens.shape[1]
    chunk = width // shards
    raw_low = raw_grad_out[...]
    head_wgrad = left_dot(first[...], raw_low)
    gates_rows = left_dot(gates_grad_out[...], first[...])
    first_grad = (
        right_dot(raw_low, weights[:, :conv_width])
        + right_dot(gate_grad, weights[:, conv_width:])
        + local_dot(gates_grad_out[...], gate_rows[...])
    )
    first_grad_out[...] = first_grad.astype(LOW)
    wide = tokens[...].astype(WIDE)
    normed = wide * lax.rsqrt(jnp.mean(wide * wide, -1, keepdims=True) + EPS)
    gain_grad = jnp.sum(first_grad * normed, 0, keepdims=True)
    beta_row = gates_rows[0:1] + gates_rows[2:3]
    decay_row = gates_rows[1:2] + gates_rows[3:4]
    head_shards = shards // seqs
    key_each = keys // head_shards
    value_each = (conv_width - 2 * keys) // head_shards
    head_each = head_gain_grad.shape[1] // shards
    all_taps = jnp.concatenate(taps_grad, 0)
    lane = lax.broadcasted_iota(jnp.int32, (1, conv_width), 1)
    decay_terms = jnp.zeros((1, conv_width), WIDE)
    for which, total in enumerate((log_total, bias_total)):
        for piece in range(3):
            high = total.astype(LOW).astype(WIDE)
            place = head_each + (which * 3 + piece) * shards + shard
            decay_terms = jnp.where(lane == place, high, decay_terms)
            total = total - high
    blocks = []
    for s in range(shards):
        line = slice(s * chunk, (s + 1) * chunk)
        i = s % head_shards
        gains = jnp.concatenate(
            [beta_row[:, line], decay_row[:, line], gain_grad[:, line], ffn_gain_grad[:, line]], 1
        )
        tap_rows = jnp.concatenate(
            [
                all_taps[:, i * key_each : (i + 1) * key_each],
                all_taps[:, keys + i * key_each : keys + (i + 1) * key_each],
                all_taps[:, 2 * keys + i * value_each : 2 * keys + (i + 1) * value_each],
            ],
            1,
        )
        tap_rows = jnp.where(part == s // head_shards, tap_rows, 0.0)
        tap_rows = jnp.concatenate(
            [tap_rows, jnp.zeros((count, conv_width - tap_rows.shape[1]), WIDE)], 1
        )
        head_row = jnp.concatenate(
            [
                head_gain_grad[:, s * head_each : (s + 1) * head_each],
                jnp.zeros((1, conv_width - head_each), WIDE),
            ],
            1,
        )
        small = jnp.concatenate(
            [
                gains,
                tap_rows,
                head_row + decay_terms,
                jnp.zeros((ROWS16 - count - 2, conv_width), WIDE),
            ],
            0,
        )
        empty = jnp.zeros((ROWS16, values + outs), WIDE)
        blocks.append(
            (
                head_wgrad[line],
                gate_wgrad[line],
                out_wgrad[line],
                jnp.concatenate([small, empty], 1),
            )
        )
    top, all_lanes = slice(0, chunk), slice(0, conv_width + values + outs)
    spots = (
        (top, slice(0, conv_width)),
        (top, slice(conv_width, conv_width + values)),
        (top, slice(conv_width + values, conv_width + values + outs)),
        (slice(chunk, chunk + ROWS16), all_lanes),
    )
    for s in range(shards):
        for block, (line, lanes) in zip(blocks[s], spots):
            pack[s, line, lanes] = block.astype(LOW)


def finish_kernel(
    team,
    keys,
    shards,
    count,
    scalars,
    *refs,
):
    slots = refs[:team]
    (
        query_out,
        key_out,
        value_out,
        gate_out,
        proj_out,
        beta_out,
        decay_out,
        mix_out,
        ffn_out,
        query_conv_out,
        key_conv_out,
        value_conv_out,
        head_out,
        log_out,
        bias_out,
        pair,
    ) = refs[team:]
    part = scalars[0]
    chunk = query_out.shape[0]
    values = value_out.shape[1] // team
    conv_width = 2 * keys + values
    key_each = query_conv_out.shape[1]
    conv_each = 2 * key_each + value_conv_out.shape[1]
    head_each = head_out.shape[1]
    total = None
    lane = lax.broadcasted_iota(jnp.int32, (1, LANES), 1)
    log_row = jnp.zeros((1, LANES), WIDE)
    bias_row = jnp.zeros((1, LANES), WIDE)
    pair[...] = jnp.zeros(pair.shape, WIDE)
    for steps in range(team):
        head = member(part, steps)
        key_place = pl.ds(pl.multiple_of(head * keys, keys), keys)
        value_place = pl.ds(pl.multiple_of(head * values, values), values)
        block = slots[steps]
        query_out[:, key_place] = block[:chunk, :keys].astype(WIDE)
        key_out[:, key_place] = block[:chunk, keys : 2 * keys].astype(WIDE)
        value_out[:, value_place] = block[:chunk, 2 * keys : conv_width].astype(WIDE)
        gate_out[:, value_place] = block[:chunk, conv_width : conv_width + values].astype(WIDE)
        proj_out[:, value_place] = block[:chunk, conv_width + values :].astype(WIDE)
        small = block[chunk:, :conv_width].astype(WIDE)
        total = small if total is None else total + small
        pair[pl.ds(head, 1), :] = small[0:1, :chunk]
        pair[pl.ds(head + team, 1), :] = small[0:1, chunk : 2 * chunk]
        terms = small[count + 1 : count + 2]
        wide_lane = lax.broadcasted_iota(jnp.int32, (1, conv_width), 1)
        ends = [head_each + 3 * shards * k for k in range(3)]
        log_sum = jnp.sum(
            jnp.where((wide_lane >= ends[0]) & (wide_lane < ends[1]), terms, 0.0),
            1,
            keepdims=True,
        )
        bias_sum = jnp.sum(
            jnp.where((wide_lane >= ends[1]) & (wide_lane < ends[2]), terms, 0.0),
            1,
            keepdims=True,
        )
        log_row = jnp.where(lane == head, log_sum, log_row)
        bias_row = jnp.where(lane == head, bias_sum, bias_row)
    beta_out[...] = pair[:team]
    decay_out[...] = pair[team : 2 * team]
    mix_out[...] = total[0:1, 2 * chunk : 3 * chunk]
    ffn_out[...] = total[0:1, 3 * chunk : 4 * chunk]
    query_conv_out[...] = total[1 : count + 1, :key_each]
    key_conv_out[...] = total[1 : count + 1, key_each : 2 * key_each]
    value_conv_out[...] = total[1 : count + 1, 2 * key_each : conv_each]
    head_out[...] = total[count + 1 : count + 2, :head_each]
    log_out[...] = log_row[:, :team]
    bias_out[...] = bias_row[:, :team]


def array(shape, dtype):
    return jax.ShapeDtypeStruct(shape, dtype)


def run_kernel(kernel, name, scalars, operands, outs, flops, scratch=(), far=0, far_outs=0):
    spec = pl.BlockSpec(memory_space=pltpu.VMEM)
    moved = sum(math.prod(v.shape) * v.dtype.itemsize for v in (*operands, *outs))
    return pl.pallas_call(
        kernel,
        out_shape=tuple(outs),
        in_specs=[pl.BlockSpec(memory_space=pltpu.SMEM)] * len(scalars)
        + [pl.BlockSpec(memory_space=pl.ANY)] * far
        + [spec] * (len(operands) - far),
        out_specs=[pl.BlockSpec(memory_space=pl.ANY)] * far_outs
        + [spec] * (len(outs) - far_outs),
        scratch_shapes=list(scratch),
        compiler_params=pltpu.CompilerParams(vmem_limit_bytes=(60 if far else 48) * 1024 * 1024),
        cost_estimate=pl.CostEstimate(flops=flops, bytes_accessed=moved, transcendentals=0),
        name=name,
    )(*scalars, *operands)


def team_pairs(devices, steps):
    return [(j, j ^ steps) for j in range(devices)]


def team_gather(block, devices, team):
    return [block] + [
        lax.ppermute(block, "rep", team_pairs(devices, steps)) for steps in range(1, team)
    ]


def swap(block, name, size, mask):
    return lax.ppermute(block, name, [(j, j ^ mask) for j in range(size)])


def line_gather(block, shards):
    return [block] + [
        swap(block, "shard", shards, 2 * steps) for steps in range(1, shards // 2)
    ]


def doubled(block, devices, near, far):
    size = block.shape[0]
    pair = swap(block, "rep", devices, near)
    quad = swap(both_ends(block, pair), "rep", devices, far)
    held = {0: block, near: pair, far: quad[:size], near | far: quad[size:]}
    return [held[e] for e in range(4)]


def team_halves(block, devices):
    half = block.shape[0] // 2
    return doubled(block[:half], devices, 1, 2) + doubled(block[half:], devices, 2, 1)


def both_ends(block, moved):
    return jnp.concatenate([block, moved], 0)


def team_send(slots, devices, team):
    return [slots[0]] + [
        lax.ppermute(slots[steps], "rep", team_pairs(devices, steps)) for steps in range(1, team)
    ]


def wide_sum(blocks):
    total = blocks[0].astype(WIDE)
    for block in blocks[1:]:
        total = total + block.astype(WIDE)
    return total


def norm_scale(v):
    return lax.rsqrt(jnp.mean(v * v, -1, keepdims=True) + EPS)


def replica_slots(block, part, devices, team):
    if devices == team:
        return team_gather(block, devices, team)
    blocks = lax.all_gather(block, "rep").astype(WIDE)
    blocks = jnp.sum(blocks.reshape((devices // team, team) + block.shape), 0)
    return [
        lax.dynamic_index_in_dim(blocks, part ^ e, 0, keepdims=False)
        for e in range(team)
    ]


def after(values, first):
    return lax.optimization_barrier((values, first))[0]


def body(
    inputs,
    cotangent,
    mix_gain,
    query_proj,
    key_proj,
    value_proj,
    beta_proj,
    decay_proj,
    gate_proj,
    query_conv,
    key_conv,
    value_conv,
    decay_log,
    decay_bias,
    head_gain,
    out_proj,
    ffn_gain,
    ffn_gate,
    ffn_up,
    ffn_down,
):
    devices = lax.axis_size("rep")
    shards = lax.axis_size("shard")
    team = beta_proj.shape[1]
    part = lax.axis_index("rep") % team
    shard = lax.axis_index("shard")
    places = jnp.stack([part, shard]).astype(jnp.int32)
    tokens_each, width = inputs.shape
    count = team * tokens_each
    chunk = mix_gain.shape[0]
    keys = query_proj.shape[1] // team
    values = value_proj.shape[1] // team
    outs = out_proj.shape[1] // team
    conv_width = 2 * keys + values
    hidden_each = ffn_down.shape[0] // team
    hidden_part = hidden_each * shards
    taps_count = query_conv.shape[0]
    key_each, value_each = query_conv.shape[1], value_conv.shape[1]
    head_each = head_gain.shape[0]

    ffn_rows = 2 * hidden_part * chunk // LANES + hidden_each * (width // LANES)

    mixer_pack = run_kernel(
        functools.partial(pack_kernel, team),
        "pack",
        (places,),
        (
            query_proj,
            key_proj,
            value_proj,
            gate_proj,
            out_proj,
            beta_proj.T,
            decay_proj.T,
            mix_gain[None],
            ffn_gain[None],
            query_conv,
            key_conv,
            value_conv,
            head_gain[None],
        ),
        (
            array((chunk + ROWS16, conv_width + values + outs), LOW),
        ),
        10**8,
        (pltpu.SemaphoreType.DMA((5,)),),
        5,
    )[0]
    pack_slots = line_gather(mixer_pack, shards)
    member_index = lax.axis_index("rep")
    gathered = lax.all_gather(inputs, "rep", axis=0)
    tokens = jnp.concatenate(
        [
            lax.dynamic_index_in_dim(gathered, member_index ^ e, 0, keepdims=False)
            for e in range(team)
        ],
        0,
    )
    cotangent_pair = swap(cotangent, "rep", devices, 2)
    pack_slots = after(pack_slots, cotangent_pair)
    cotangent_pair = both_ends(cotangent, cotangent_pair)
    ffn_pack = run_kernel(
        functools.partial(feed_forward_pack_kernel, team, shards),
        "feed_forward_pack",
        (places,),
        (after(ffn_gate, mixer_pack), ffn_up, ffn_down),
        (array((ffn_rows, LANES), LOW),),
        10**8,
        (
            pltpu.VMEM(ffn_gate.shape, LOW),
            pltpu.VMEM(ffn_up.shape, LOW),
            pltpu.VMEM(ffn_down.shape, LOW),
            pltpu.SemaphoreType.DMA((3,)),
        ),
        3,
    )[0]
    ffn_packs = lax.all_gather(after(ffn_pack, pack_slots), "shard", axis=0)
    pack_mine = jnp.stack(pack_slots)
    pack_theirs = swap(pack_mine, "shard", shards, 1)
    cotangent_quad = swap(after(cotangent_pair, pack_slots), "rep", devices, 1)
    tokens = after(tokens, cotangent_quad)
    cotangents = jnp.concatenate(
        [
            cotangent,
            cotangent_quad[:tokens_each],
            cotangent_pair[tokens_each:],
            cotangent_quad[tokens_each:],
        ],
        0,
    )
    scalars = jnp.stack(
        [
            jnp.exp(lax.dynamic_index_in_dim(decay_log, part, 0, keepdims=False)),
            lax.dynamic_index_in_dim(decay_bias, part, 0, keepdims=False),
        ]
    )

    (
        first,
        raw,
        gate_raw,
        gates,
        inverse,
        update,
        heads,
        mixed_part,
        head_weights,
        mix_row,
        ffn_row,
        gate_rows,
        taps,
        head_row,
    ) = run_kernel(
        functools.partial(mixer_forward_kernel, team, keys, taps_count),
        "mixer_forward",
        (scalars, places),
        (tokens, pack_mine, pack_theirs),
        (
            array((count, width), LOW),
            array((count, conv_width), WIDE),
            array((count, values), WIDE),
            array((count, ROWS16), WIDE),
            array((count, tokens_each), WIDE),
            array((count, values), WIDE),
            array((count, values), WIDE),
            array((count, values), LOW),
            array((width, conv_width + values), LOW),
            array((1, width), WIDE),
            array((1, width), WIDE),
            array((ROWS16, width), LOW),
            array((taps_count, conv_width), WIDE),
            array((1, values), WIDE),
        ),
        8 * 10**9,
        (pltpu.VMEM((ROWS16, width), WIDE),),
    )
    proj_all = both_ends(
        pack_mine[:, :chunk, conv_width + values :],
        pack_theirs[:, :chunk, conv_width + values :],
    )
    proj_slots = team_gather(proj_all, devices, team)
    mixed_part = after(mixed_part, proj_slots)
    mixed_slots = team_gather(mixed_part, devices, team)

    (
        mixed,
        hidden_own,
        second_part,
        result_part,
        out_rows,
        ffn_grads,
        ffn_gain_part,
    ) = run_kernel(
        functools.partial(feed_forward_kernel, team),
        "feed_forward",
        (places,),
        (*proj_slots, tokens, ffn_packs, cotangents, *mixed_slots, ffn_row),
        (
            array((count, width), LOW),
            array((tokens_each, width), WIDE),
            array((count, width), LOW),
            array((count, width), LOW),
            array((values, width), LOW),
            array((shards, ffn_rows, LANES), LOW),
            array((1, width), WIDE),
        ),
        16 * 10**9,
        (
            pltpu.VMEM((count, width), LOW),
            pltpu.VMEM((width, width), LOW),
            pltpu.VMEM((count, width), LOW),
            pltpu.VMEM((count, width), LOW),
            pltpu.VMEM((shards, ffn_rows, LANES), LOW),
            pltpu.VMEM((count, width), WIDE),
            pltpu.VMEM((width, 2 * hidden_part), LOW),
            pltpu.VMEM((hidden_part, width), LOW),
            *(pltpu.VMEM(slot.shape, LOW) for slot in proj_slots),
            pltpu.VMEM(tokens.shape, LOW),
            pltpu.VMEM(ffn_packs.shape, LOW),
            pltpu.VMEM(cotangents.shape, LOW),
            pltpu.SemaphoreType.DMA((team + 3,)),
            pltpu.SemaphoreType.DMA((8,)),
        ),
        team + 3,
        6,
    )

    def slots_of(v):
        return [v[e * tokens_each : (e + 1) * tokens_each] for e in range(team)]

    second_slots = team_send(slots_of(second_part), devices, team)
    ffn_shard = lax.psum_scatter(ffn_grads, "shard", scatter_dimension=0)
    second_grad = wide_sum(second_slots)
    scale_own = norm_scale(hidden_own)
    weighted = second_grad * ffn_row
    hidden_grad = cotangent.astype(WIDE) + scale_own * (
        weighted
        - hidden_own
        * (scale_own * scale_own * jnp.mean(hidden_own * weighted, -1, keepdims=True))
    )
    branch_slots = team_gather(hidden_grad.astype(LOW), devices, team)


    result_part = after(result_part, branch_slots)
    result_slots = team_send(slots_of(result_part), devices, team)

    head_grads, first_part = run_kernel(
        functools.partial(mixer_backward_kernel, team, keys, shards),
        "mixer_backward",
        (scalars, places),
        (
            *branch_slots,
            out_rows,
            gate_raw,
            heads,
            head_row,
            first,
            mixed,
            raw,
            gates,
            inverse,
            update,
            taps,
            head_weights,
            gate_rows,
            tokens,
            ffn_gain_part,
        ),
        (
            array((shards, chunk + ROWS16, conv_width + values + outs), LOW),
            array((count, width), LOW),
        ),
        10 * 10**9,
        (
            pltpu.VMEM((count, conv_width), LOW),
            pltpu.VMEM((count, ROWS16), LOW),
            pltpu.VMEM((count, width), LOW),
            pltpu.VMEM((count, values), WIDE),
        ),
    )
    head_grads = after(head_grads, result_slots)
    head_shard = lax.psum_scatter(head_grads, "shard", scatter_dimension=0)
    first_slots = team_send(slots_of(first_part), devices, team)
    if devices == team == 4:
        ffn_totals = team_halves(ffn_shard, devices)
    else:
        ffn_totals = replica_slots(ffn_shard, part, devices, team)
    first_grad = wide_sum(after(first_slots, ffn_totals))
    seq_in = inputs.astype(WIDE)
    seq_scale = norm_scale(seq_in)
    weighted = first_grad * mix_row
    inputs_grad = hidden_grad + seq_scale * (
        weighted
        - seq_in * (seq_scale * seq_scale * jnp.mean(seq_in * weighted, -1, keepdims=True))
    )
    result = hidden_own + wide_sum(result_slots)

    head_totals = replica_slots(after(head_shard, ffn_totals), part, devices, team)
    gate_grads, up_grads, down_grads = run_kernel(
        functools.partial(feed_forward_finish_kernel, team, shards),
        "feed_forward_finish",
        (places,),
        ffn_totals,
        (
            array(ffn_gate.shape, WIDE),
            array(ffn_up.shape, WIDE),
            array(ffn_down.shape, WIDE),
        ),
        10**8,
        (pltpu.VMEM((team, ffn_rows, LANES), LOW),),
    )
    (
        query_total,
        key_total,
        value_total,
        gate_total,
        out_total,
        beta_total,
        decay_total,
        mix_total,
        ffn_total,
        query_conv_total,
        key_conv_total,
        value_conv_total,
        head_total,
        log_total,
        bias_total,
    ) = run_kernel(
        functools.partial(finish_kernel, team, keys, shards, taps_count),
        "finish",
        (places,),
        head_totals,
        (
            array((chunk, team * keys), WIDE),
            array((chunk, team * keys), WIDE),
            array((chunk, team * values), WIDE),
            array((chunk, team * values), WIDE),
            array((chunk, team * outs), WIDE),
            array((team, chunk), WIDE),
            array((team, chunk), WIDE),
            array((1, chunk), WIDE),
            array((1, chunk), WIDE),
            array((taps_count, key_each), WIDE),
            array((taps_count, key_each), WIDE),
            array((taps_count, value_each), WIDE),
            array((1, head_each), WIDE),
            array((1, team), WIDE),
            array((1, team), WIDE),
        ),
        10**8,
        (pltpu.VMEM((max(8, 2 * team), chunk), WIDE),),
    )
    return (
        result.astype(LOW),
        inputs_grad,
        mix_total[0],
        query_total,
        key_total,
        value_total,
        beta_total.T,
        decay_total.T,
        gate_total,
        query_conv_total,
        key_conv_total,
        value_conv_total,
        log_total[0],
        bias_total[0],
        head_total[0],
        out_total,
        ffn_total[0],
        gate_grads,
        up_grads,
        down_grads,
    )


def solution(mesh):
    rows = P("shard", None)
    return jax.shard_map(
        body,
        mesh=mesh,
        in_specs=(
            P(("rep", "shard"), None),
            P(("rep", "shard"), None),
            P("shard"),
            rows,
            rows,
            rows,
            rows,
            rows,
            rows,
            P(None, "shard"),
            P(None, "shard"),
            P(None, "shard"),
            P(),
            P(),
            P("shard"),
            rows,
            P("shard"),
            rows,
            rows,
            rows,
        ),
        out_specs=(
            P(("rep", "shard"), None),
            P(("rep", "shard"), None),
            P("shard"),
            rows,
            rows,
            rows,
            rows,
            rows,
            rows,
            P(None, "shard"),
            P(None, "shard"),
            P(None, "shard"),
            P(),
            P(),
            P("shard"),
            rows,
            P("shard"),
            rows,
            rows,
            rows,
        ),
        check_vma=False,
    )
```
